256 devices in a mesh: ctx: 32 (over x, z_hi, core), ch: 8 (over z_lo, y).
Axes of the slice: x: 4, y: 4, z: 8 (z_hi: 4, z_lo: 2; z = z_hi * 2 + z_lo), core: 2. Of those that a mesh axis runs over, the one named last changes fastest.
Arguments:
- query_input: bfloat16 [16384, 4096], P(('ctx', 'ch')), may hold values from -6 to 6
- key_input: bfloat16 [16384, 4096], P(('ctx', 'ch')), may hold values from -6 to 6
- value_input: bfloat16 [16384, 4096], P(('ctx', 'ch')), may hold values from -6 to 6
- filters: bfloat16 [16384, 4096], P('ctx', 'ch'), may hold values from -0.046875 to 0.046875
- direct_gain: float32 [4096], P('ch'), may hold values from -4 to 4
Outputs:
- mixed_output: bfloat16 [16384, 4096], P(('ctx', 'ch'))
The draws below stay inside these ranges and needn't reach their ends.
All inputs are finite; a program needn't handle non-finite values.
Results may differ from the reference program's by a relative error of at most 0.012.
Values may be sent and summed in bfloat16 or wider, within the bound.
A program may use at most 64 MiB of HBM per device.

```python
import math
import jax
import jax.numpy as jnp
from jax import lax

CH = 4096
SEQ = 16384


def steps_of(stream_key, dims, shards, smallest, high):
    def one(position, shards_of):
        heights = jax.random.uniform(jax.random.fold_in(jax.random.fold_in(stream_key, 6), position), (shards_of,), jnp.float32, smallest / len(shards), high / len(shards))
        return jnp.repeat(jnp.exp(heights), dims[position] // shards_of).reshape((-1,) + (1,) * (len(dims) - position - 1))

    level = one(*shards[0])
    for cut in shards[1:]:
        level = level * one(*cut)
    return level


def noise(rng, dims, scale, reach, split=(), held_as=jnp.bfloat16):
    result = jax.random.normal(rng, dims, jnp.float32) * scale
    if len(split) > 0:
        result = steps_of(rng, dims, split, -0.22, 0.18) * result
    return jnp.clip(result, min=-reach, max=reach).astype(held_as)


def setup_inputs(seed: int = 0) -> dict:
    keys = jax.random.split(jax.random.key(seed), 6)
    return {
        "query_input": noise(keys[0], (SEQ, CH), 1.0, 6.0, ((0, 256),)),
        "key_input": noise(keys[1], (SEQ, CH), 1.0, 6.0, ((0, 256),)),
        "value_input": noise(keys[2], (SEQ, CH), 1.0, 6.0, ((0, 256),)),
        "filters": noise(keys[3], (SEQ, CH), SEQ ** -0.5, 0.046875, ((0, 32), (1, 8))),
        "direct_gain": noise(keys[4], (CH,), 1.0, 4.0, ((0, 8),), jnp.float32),
    }


def convolve(signal, kernel):
    length = signal.shape[0]
    padded = 2 * length
    product = jnp.fft.rfft(signal, n=padded, axis=0) * jnp.fft.rfft(kernel, n=padded, axis=0)
    return jnp.fft.irfft(product, n=padded, axis=0)[:length]


def convolve_pair(blocks_pair):
    return convolve(blocks_pair[0], blocks_pair[1])


def reference(query_input, key_input, value_input, filters, direct_gain):
    gated = (key_input.astype(jnp.float32) * value_input.astype(jnp.float32)).astype(jnp.bfloat16)
    signal = gated.astype(jnp.float32)
    kernel = filters.astype(jnp.float32)
    block_width = math.gcd(CH, 256)
    block_count = CH // block_width
    signal_blocks = signal.reshape(SEQ, block_count, block_width).transpose(1, 0, 2)
    kernel_blocks = kernel.reshape(SEQ, block_count, block_width).transpose(1, 0, 2)
    convolved_blocks = lax.map(convolve_pair, (signal_blocks, kernel_blocks))
    convolved = convolved_blocks.transpose(1, 0, 2).reshape(SEQ, CH)
    mixed_output = query_input.astype(jnp.float32) * (convolved + direct_gain[None, :] * signal)
    return mixed_output.astype(jnp.bfloat16)
```

```python
import functools

import jax
import jax.numpy as jnp
import ml_dtypes
import numpy as np
from jax import lax
from jax.experimental import pallas as pl
from jax.experimental.pallas import tpu as pltpu
from jax.sharding import PartitionSpec as P

MESH = pl.DeviceIdType.MESH
SIDE = 128
GROUP = 4


def halves(table):
    high = table.astype(ml_dtypes.bfloat16)
    low = (table - high.astype(np.float64)).astype(ml_dtypes.bfloat16)
    return high, low


def tables(per_slab, slabs):
    length = SIDE * SIDE
    side = np.arange(SIDE)
    offset = side + 0.25
    coarse = 2 * np.pi * np.outer(offset, side) / SIDE
    turn = 2 * np.pi * np.outer(offset, side) / length
    fine = 2 * np.pi * np.outer(side, side) / SIDE

    def order(pieces):
        count = SIDE // pieces
        return (np.arange(count)[None, :] * pieces + np.arange(pieces)[:, None]).reshape(-1)

    def forward(pieces):
        angle = coarse[:, order(pieces)]
        high, low = halves(np.concatenate([np.cos(angle), -np.sin(angle)], axis=0))
        return np.concatenate([high, low], axis=1)

    angle = coarse[:, order(per_slab)].T
    back = np.concatenate([np.cos(angle), -np.sin(angle)], axis=1) / length
    cos, sin = np.cos(fine), np.sin(fine)
    into = np.block([[cos, -sin], [sin, cos]])
    outof = np.block([[cos, sin], [-sin, cos]])
    return (
        forward(per_slab),
        forward(2 * per_slab),
        np.concatenate([np.cos(turn), np.sin(turn)], axis=1).astype(np.float32),
        np.stack(halves(into)),
        np.stack(halves(outof)),
        np.stack(halves(back)),
    )


def kernel(
    sizes,
    key_ref,
    value_ref,
    filter_ref,
    gain_ref,
    signal_coarse,
    filter_coarse,
    turn,
    into,
    outof,
    back,
    out_ref,
    gated,
    slab,
    slab_turned,
    signal_in,
    filter_turned,
    filter_in,
    signal_wide,
    filter_wide,
    spectrum,
    wide,
    sent,
    returned,
    rows,
    row_send,
    row_recv,
    filter_send,
    filter_recv,
    signal_send,
    signal_recv,
    back_send,
    back_recv,
    out_send,
    out_recv,
):
    n_ctx, n_lo, n_y = sizes
    count = key_ref.shape[0]
    width = filter_ref.shape[1]
    own = width // n_ctx
    piece = n_y * count
    ctx = lax.axis_index("ctx")
    ch = lax.axis_index("ch")
    lo = ch // n_y
    y = lax.rem(ch, n_y)
    peers = n_ctx * n_lo
    me = ctx * n_lo + lo

    def peer(step):
        other = lax.rem(me + step, peers)
        return other // n_lo, lax.rem(other, n_lo), other

    def of_peer(there, low):
        return pl.ds(pl.multiple_of(low * width + there * own, own), own)

    def at(slot):
        return pl.ds(pl.multiple_of(slot * own, own), own)

    barrier = pltpu.get_barrier_semaphore()

    @pl.loop(1, peers)
    def _(step):
        there, low, _ = peer(step)
        pl.semaphore_signal(barrier, inc=1, device_id=(there, low * n_y + y), device_id_type=MESH)

    @pl.loop(1, n_y)
    def _(step):
        other = lax.rem(y + step, n_y)
        pl.semaphore_signal(barrier, inc=1, device_id=(ctx, lo * n_y + other), device_id_type=MESH)

    gated[...] = (key_ref[...].astype(jnp.float32) * value_ref[...].astype(jnp.float32)).astype(
        jnp.bfloat16
    )
    filter_turned[...] = filter_ref[...].T

    pl.semaphore_wait(barrier, peers + n_y - 2)

    def columns(low, other):
        return pl.ds(pl.multiple_of((low * n_y + other) * width, width), width)

    slab_rows = pl.ds(pl.multiple_of(y * count, count), count)

    @pl.loop(1, n_y)
    def _(step):
        other = lax.rem(y + step, n_y)
        for low in range(n_lo):
            pltpu.make_async_remote_copy(
                src_ref=gated.at[:, columns(low, other)],
                dst_ref=slab.at[slab_rows, pl.ds(low * width, width)],
                send_sem=row_send,
                recv_sem=row_recv,
                device_id=(ctx, lo * n_y + other),
                device_id_type=MESH,
            ).start()

    for low in range(n_lo):
        pltpu.make_async_copy(
            gated.at[:, columns(low, y)],
            slab.at[slab_rows, pl.ds(low * width, width)],
            row_recv,
        ).start()

    @pl.loop(1, n_ctx)
    def _(step):
        there = lax.rem(ctx + step, n_ctx)
        pltpu.make_async_remote_copy(
            src_ref=filter_turned.at[at(there), :],
            dst_ref=filter_in.at[at(ctx), :],
            send_sem=filter_send,
            recv_sem=filter_recv,
            device_id=(there, ch),
            device_id_type=MESH,
        ).start()

    pltpu.make_async_copy(filter_turned.at[at(ctx), :], filter_in.at[at(ctx), :], filter_recv).start()

    pltpu.make_async_copy(slab, slab, row_recv).wait()
    slab_turned[...] = slab[...].T

    @pl.loop(1, peers)
    def _(step):
        there, low, _ = peer(step)
        pltpu.make_async_remote_copy(
            src_ref=slab_turned.at[of_peer(there, low), :],
            dst_ref=signal_in.at[at(me), :],
            send_sem=signal_send,
            recv_sem=signal_recv,
            device_id=(there, low * n_y + y),
            device_id_type=MESH,
        ).start()

    pltpu.make_async_copy(slab_turned.at[of_peer(ctx, lo), :], signal_in.at[at(me), :], signal_recv).start()

    def load(source, channel):
        pieces, height, _ = source.shape
        return jnp.concatenate(
            [source[h, pl.ds(channel, height // own, stride=own), :] for h in range(pieces)], axis=0
        ).astype(jnp.bfloat16)

    def dot(left, right):
        return jnp.dot(left, right, preferred_element_type=jnp.float32)

    def transform(source, table, first):
        columns_of = jnp.concatenate([load(source, first + u) for u in range(GROUP)], axis=1)
        part = dot(table[...], jnp.concatenate([columns_of, columns_of], axis=0))
        cos, sin = turn[:, :SIDE], turn[:, SIDE:]
        turned = []
        for u in range(GROUP):
            real = part[:SIDE, u * SIDE : (u + 1) * SIDE]
            imag = part[SIDE:, u * SIDE : (u + 1) * SIDE]
            turned.append(
                jnp.concatenate([real * cos + imag * sin, imag * cos - real * sin], axis=1)
            )
        turned = jnp.concatenate(turned, axis=0).astype(jnp.bfloat16)
        return dot(turned, into[0]) + dot(turned, into[1])

    def widen(source, target):
        pieces = target.shape[0]
        for h in range(pieces):
            target[h] = source[:, h * SIDE : (h + 1) * SIDE].astype(jnp.float32)

    pltpu.make_async_copy(filter_in, filter_in, filter_recv).wait()
    widen(filter_in, filter_wide)

    @pl.loop(0, own // GROUP)
    def _(group):
        spectrum[group] = transform(filter_wide, filter_coarse, group * GROUP)

    pltpu.make_async_copy(signal_in, signal_in, signal_recv).wait()
    widen(signal_in, signal_wide)

    @pl.loop(0, own // GROUP)
    def _(group):
        first = group * GROUP
        wave = transform(signal_wide, signal_coarse, first)
        held = spectrum[group]
        wave_real, wave_imag = wave[:, :SIDE], wave[:, SIDE:]
        held_real, held_imag = held[:, :SIDE], held[:, SIDE:]
        product = jnp.concatenate(
            [wave_real * held_real - wave_imag * held_imag, wave_real * held_imag + wave_imag * held_real],
            axis=1,
        ).astype(jnp.bfloat16)
        part = dot(product, outof[0]) + dot(product, outof[1])
        cos, sin = turn[:, :SIDE], turn[:, SIDE:]
        turned = []
        for u in range(GROUP):
            real = part[u * SIDE : (u + 1) * SIDE, :SIDE]
            imag = part[u * SIDE : (u + 1) * SIDE, SIDE:]
            turned.append(
                jnp.concatenate([real * cos - imag * sin, imag * cos + real * sin], axis=0)
            )
        turned = jnp.concatenate(turned, axis=1).astype(jnp.bfloat16)
        result = dot(back[0], turned) + dot(back[1], turned)
        pieces, height, _ = wide.shape
        each = height // own
        for u in range(GROUP):
            for h in range(pieces):
                wide[h, pl.ds(first + u, each, stride=own), :] = result[
                    h * each : (h + 1) * each, u * SIDE : (u + 1) * SIDE
                ]

    line = lax.broadcasted_iota(jnp.int32, (own, SIDE), 0)
    gain = jnp.zeros((own, SIDE), jnp.float32)
    for c in range(own):
        gain = jnp.where(line == c, gain_ref[ctx * own + c], gain)

    pieces = wide.shape[0]
    gain = jnp.concatenate([gain] * 4, axis=0)

    @pl.loop(0, peers // 4)
    def _(slot):
        here = pl.ds(pl.multiple_of(slot * own * 4, own * 4), own * 4)
        for h in range(pieces):
            sent[here, h * SIDE : (h + 1) * SIDE] = (
                wide[h, here, :] + gain * signal_wide[h, here, :]
            ).astype(jnp.bfloat16)

    @pl.loop(1, peers)
    def _(step):
        there, low, other = peer(step)
        pltpu.make_async_remote_copy(
            src_ref=sent.at[at(other), :],
            dst_ref=returned.at[of_peer(ctx, lo), :],
            send_sem=back_send,
            recv_sem=back_recv,
            device_id=(there, low * n_y + y),
            device_id_type=MESH,
        ).start()

    pltpu.make_async_copy(sent.at[at(me), :], returned.at[of_peer(ctx, lo), :], back_recv).start()
    pltpu.make_async_copy(returned, returned, back_recv).wait()
    rows[...] = returned[...].T

    @pl.loop(1, n_y)
    def _(step):
        other = lax.rem(y + step, n_y)
        for low in range(n_lo):
            pltpu.make_async_remote_copy(
                src_ref=rows.at[pl.ds(pl.multiple_of(other * count, count), count), pl.ds(low * width, width)],
                dst_ref=out_ref.at[:, columns(low, y)],
                send_sem=out_send,
                recv_sem=out_recv,
                device_id=(ctx, lo * n_y + other),
                device_id_type=MESH,
            ).start()

    for low in range(n_lo):
        pltpu.make_async_copy(
            rows.at[slab_rows, pl.ds(low * width, width)], out_ref.at[:, columns(low, y)], out_recv
        ).start()

    pltpu.make_async_copy(out_ref, out_ref, out_recv).wait()

    def settle(ref, amount, semaphore):
        part = ref.at[pl.ds(0, amount), :]
        pltpu.make_async_copy(part, part, semaphore).wait()

    settle(slab, (n_y - 1) * count, row_send)
    settle(filter_turned, (n_ctx - 1) * own, filter_send)
    settle(slab_turned, (peers - 1) * own, signal_send)
    settle(sent, (peers - 1) * own, back_send)
    settle(rows, (n_y - 1) * count, out_send)


def shards(query_input, key_input, value_input, filters, direct_gain):
    n_ctx, n_ch = lax.axis_size("ctx"), lax.axis_size("ch")
    n_lo = 2
    n_y = n_ch // n_lo
    count, channels = key_input.shape
    block, width = filters.shape
    own = width // n_ctx
    piece = count * n_y
    per_slab = piece // SIDE
    peers = n_ctx * n_lo
    groups = own // GROUP
    constants = [jnp.asarray(t) for t in tables(per_slab, peers)]
    vmem = pl.BlockSpec(memory_space=pltpu.VMEM)
    half, single = jnp.bfloat16, jnp.float32
    dma = pltpu.SemaphoreType.DMA(())
    mixed = pl.pallas_call(
        functools.partial(kernel, (n_ctx, n_lo, n_y)),
        out_shape=jax.ShapeDtypeStruct((count, channels), half),
        in_specs=[vmem] * 3 + [pl.BlockSpec(memory_space=pltpu.SMEM)] + [vmem] * len(constants),
        out_specs=vmem,
        scratch_shapes=[
            pltpu.VMEM((count, channels), half),
            pltpu.VMEM((piece, n_lo * width), half),
            pltpu.VMEM((n_lo * width, piece), half),
            pltpu.VMEM((peers * own, piece), half),
            pltpu.VMEM((width, block), half),
            pltpu.VMEM((n_ctx * own, block), half),
            pltpu.VMEM((per_slab, peers * own, SIDE), single),
            pltpu.VMEM((2 * per_slab, n_ctx * own, SIDE), single),
            pltpu.VMEM((groups, GROUP * SIDE, 2 * SIDE), single),
            pltpu.VMEM((per_slab, peers * own, SIDE), single),
            pltpu.VMEM((peers * own, piece), half),
            pltpu.VMEM((n_lo * width, piece), half),
            pltpu.VMEM((piece, n_lo * width), half),
        ]
        + [dma] * 10,
        compiler_params=pltpu.CompilerParams(
            collective_id=0, has_side_effects=True, vmem_limit_bytes=40 * 1024 * 1024
        ),
    )(key_input, value_input, filters, direct_gain, *constants)
    return (query_input.astype(jnp.float32) * mixed.astype(jnp.float32)).astype(jnp.bfloat16)


def solution(mesh):
    return jax.shard_map(
        shards,
        mesh=mesh,
        in_specs=(
            P(("ctx", "ch"), None),
            P(("ctx", "ch"), None),
            P(("ctx", "ch"), None),
            P("ctx", "ch"),
            P("ch"),
        ),
        out_specs=P(("ctx", "ch"), None),
        check_vma=False,
    )
```

```python
import functools

import jax
import jax.numpy as jnp
import numpy as np
from jax import lax
from jax.experimental import pallas as pl
from jax.experimental.pallas import tpu as pltpu
from jax.sharding import PartitionSpec as P

MESH = pl.DeviceIdType.MESH
SIDE = 128
OCTET = 8
GROUP = 4
X, Z_HI, CORE = 4, 4, 2
Z_LO, Y = 2, 4
OWNERS = X * Z_HI
PEERS = OWNERS * Z_LO
CHUNKS = 2


def tables():
    length = SIDE * SIDE
    side = np.arange(SIDE)
    offset = side + 0.25
    coarse = 2 * np.pi * np.outer(offset, side) / SIDE
    turn = 2 * np.pi * np.outer(offset, side) / length
    fine = 2 * np.pi * np.outer(side, side) / SIDE
    arrival = side.reshape(OWNERS, CORE, Z_LO, 2).transpose(0, 2, 1, 3).reshape(-1)

    def forward(angle):
        return np.concatenate([np.cos(angle), -np.sin(angle)], axis=0)

    angle = coarse[:, arrival].T
    back = np.concatenate([np.cos(angle), -np.sin(angle)], axis=1) / length
    cos, sin = np.cos(fine), np.sin(fine)
    into = np.block([[cos, -sin], [sin, cos]])
    outof = np.block([[cos, sin], [-sin, cos]])
    stacked = [
        np.concatenate([forward(coarse[:, arrival]), forward(coarse)], axis=1),
        into,
        outof,
        back,
        np.concatenate([np.cos(turn), np.sin(turn)], axis=1),
    ]
    return np.concatenate(stacked, axis=0).astype(np.float32)


def halves(table):
    high = table.astype(jnp.bfloat16)
    return high, (table - high.astype(jnp.float32)).astype(jnp.bfloat16)


def dot(left, right):
    return jnp.dot(left, right, preferred_element_type=jnp.float32)


def kernel(
    key_hbm,
    value_hbm,
    filter_hbm,
    gain_ref,
    tables_hbm,
    out_ref,
    key_ref,
    value_ref,
    filter_ref,
    stacked,
    signal_coarse,
    filter_coarse,
    into,
    outof,
    back,
    gated,
    slab,
    signal_turned,
    signal_in,
    filter_turned,
    filter_mid,
    filter_in,
    signal_wide,
    filter_wide,
    spectrum,
    wide,
    sent,
    returned,
    rows,
    load_sems,
    row_send,
    row_recv,
    filter_send,
    filter_recv,
    swap_send,
    swap_recv,
    signal_send,
    signal_recv,
    back_send,
    back_recv,
    out_send,
    out_recv,
):
    count = gated.shape[0]
    ctx = lax.axis_index("ctx")
    ch = lax.axis_index("ch")
    x, z_hi, core = ctx // (Z_HI * CORE), lax.rem(ctx // CORE, Z_HI), lax.rem(ctx, CORE)
    z_lo, y = ch // Y, lax.rem(ch, Y)
    owner = x * Z_HI + z_hi
    me = owner * Z_LO + z_lo
    half = lambda low, other_y, other_core: (low * Y + other_y) * CORE + other_core

    loads = [
        pltpu.make_async_copy(source, target, load_sems.at[n])
        for n, (source, target) in enumerate(
            [
                (filter_hbm, filter_ref),
                (key_hbm, key_ref),
                (value_hbm, value_ref),
                (tables_hbm, stacked),
            ]
        )
    ]
    for load_copy in loads:
        load_copy.start()

    def across(step):
        other = lax.rem(me + step + core * (PEERS - 2 * step), PEERS)
        owner_there, low = other // Z_LO, lax.rem(other, Z_LO)
        return other, owner_there, low, (owner_there * CORE + core, low * Y + y)

    def owners(step):
        other = lax.rem(owner + step + core * (OWNERS - 2 * step), OWNERS)
        return other, (other * CORE + core, ch)

    def aside(step):
        other = lax.rem(y * CORE + core + step, Y * CORE)
        other_y, other_core = other // CORE, lax.rem(other, CORE)
        return other_y, other_core, (owner * CORE + other_core, z_lo * Y + other_y)

    barrier = pltpu.get_barrier_semaphore()

    with jax.named_scope("greet"):

        @pl.loop(1, PEERS)
        def _(step):
            pl.semaphore_signal(barrier, inc=1, device_id=across(step)[-1], device_id_type=MESH)

        @pl.loop(1, Y * CORE)
        def _(step):
            pl.semaphore_signal(barrier, inc=1, device_id=aside(step)[-1], device_id_type=MESH)

    def turned_pair(source, pair, column):
        parts = []
        for tile in (2 * pair, 2 * pair + 1):
            block = source[tile * SIDE : (tile + 1) * SIDE, column * SIDE : (column + 1) * SIDE]
            parts.append(block.astype(jnp.float32).T.reshape(OWNERS, OCTET, SIDE))
        return jnp.concatenate(parts, axis=1).astype(jnp.bfloat16)

    with jax.named_scope("turn_filter"):
        loads[0].wait()
        for column in range(CORE * CHUNKS):
            for pair in range(2):
                filter_turned[:, column, pair * 16 : (pair + 1) * 16, :] = turned_pair(
                    filter_ref, pair, column
                )

    with jax.named_scope("gate"):
        loads[1].wait()
        loads[2].wait()
        gated[...] = (
            key_ref[...].astype(jnp.float32) * value_ref[...].astype(jnp.float32)
        ).astype(jnp.bfloat16)

    with jax.named_scope("await_greet"):
        pl.semaphore_wait(barrier, PEERS + Y * CORE - 2)

    with jax.named_scope("send_filter"):

        @pl.loop(1, OWNERS)
        def _(step):
            other, device = owners(step)
            pltpu.make_async_remote_copy(
                src_ref=filter_turned.at[other],
                dst_ref=filter_mid.at[:, owner],
                send_sem=filter_send,
                recv_sem=filter_recv,
                device_id=device,
                device_id_type=MESH,
            ).start()

        pltpu.make_async_copy(filter_turned.at[owner], filter_mid.at[:, owner], filter_recv).start()

    def columns(low, other_y, other_core, first, size):
        start = half(low, other_y, other_core) * CHUNKS * SIDE + first
        return pl.ds(pl.multiple_of(start, SIDE), size)

    def line_of(other_y, other_core):
        return pl.ds(pl.multiple_of((other_core * Y + other_y) * count, count), count)

    with jax.named_scope("send_rows"):
        span = CHUNKS * SIDE

        @pl.loop(1, Y * CORE)
        def _(step):
            other_y, other_core, device = aside(step)
            for low in range(Z_LO):
                pltpu.make_async_remote_copy(
                    src_ref=gated.at[:, columns(low, other_y, other_core, 0, span)],
                    dst_ref=slab.at[line_of(y, core), pl.ds(low * span, span)],
                    send_sem=row_send,
                    recv_sem=row_recv,
                    device_id=device,
                    device_id_type=MESH,
                ).start()

        for low in range(Z_LO):
            pltpu.make_async_copy(
                gated.at[:, columns(low, y, core, 0, span)],
                slab.at[line_of(y, core), pl.ds(low * span, span)],
                row_recv,
            ).start()

    with jax.named_scope("split_tables"):
        loads[3].wait()
        for target, start in ((signal_coarse, 0), (filter_coarse, SIDE)):
            high, low = halves(stacked[:256, start : start + SIDE])
            target[:, :SIDE], target[:, SIDE:] = high, low
        for target, start in ((into, 256), (outof, 512), (back, 768)):
            target[0], target[1] = halves(stacked[start : start + target.shape[1]])

    with jax.named_scope("await_rows"):
        pltpu.make_async_copy(slab, slab, row_recv).wait()

    with jax.named_scope("send_signal"):
        for chunk in range(CHUNKS):
            for low in range(Z_LO):
                for pair in range(2):
                    signal_turned[
                        chunk, low * OWNERS : (low + 1) * OWNERS, pair * 16 : (pair + 1) * 16, :
                    ] = turned_pair(slab, pair, low * CHUNKS + chunk)

            @pl.loop(1, PEERS)
            def _(step):
                _, owner_there, low, device = across(step)
                pltpu.make_async_remote_copy(
                    src_ref=signal_turned.at[chunk, low * OWNERS + owner_there],
                    dst_ref=signal_in.at[chunk, me],
                    send_sem=signal_send,
                    recv_sem=signal_recv.at[chunk],
                    device_id=device,
                    device_id_type=MESH,
                ).start()

            pltpu.make_async_copy(
                signal_turned.at[chunk, z_lo * OWNERS + owner],
                signal_in.at[chunk, me],
                signal_recv.at[chunk],
            ).start()

    turn = stacked.at[896:1024]

    def transform(source, table, first):
        parts = [
            source[pl.ds(first + u, SIDE, stride=OCTET), :].astype(jnp.bfloat16) for u in range(GROUP)
        ]
        parts = jnp.concatenate(parts, axis=1)
        part = dot(table[...], jnp.concatenate([parts, parts], axis=0))
        cos, sin = turn[:, :SIDE], turn[:, SIDE:]
        turned = []
        for u in range(GROUP):
            real = part[:SIDE, u * SIDE : (u + 1) * SIDE]
            imag = part[SIDE:, u * SIDE : (u + 1) * SIDE]
            turned.append(
                jnp.concatenate([real * cos + imag * sin, imag * cos - real * sin], axis=1)
            )
        turned = jnp.concatenate(turned, axis=0).astype(jnp.bfloat16)
        return dot(turned, into[0]) + dot(turned, into[1])

    def widen(source, target):
        target[...] = source[...].astype(jnp.float32).reshape(target.shape)

    with jax.named_scope("await_filter"):
        pltpu.make_async_copy(filter_mid, filter_mid, filter_recv).wait()
        swap = pltpu.make_async_remote_copy(
            src_ref=filter_mid.at[pl.ds((1 - core) * CHUNKS, CHUNKS)],
            dst_ref=filter_in.at[:, :, core],
            send_sem=swap_send,
            recv_sem=swap_recv.at[0],
            device_id=(owner * CORE + 1 - core, ch),
            device_id_type=MESH,
        )
        swap.start()
        keep = pltpu.make_async_copy(
            filter_mid.at[pl.ds(core * CHUNKS, CHUNKS)], filter_in.at[:, :, core], swap_recv.at[1]
        )
        keep.start()
        keep.wait()
        swap.wait()

    with jax.named_scope("transform_filter"):
        for chunk in range(CHUNKS):
            widen(filter_in.at[chunk], filter_wide)

            @pl.loop(0, OCTET // GROUP)
            def _(group):
                spectrum[chunk, group] = transform(filter_wide, filter_coarse, group * GROUP)

    line = lax.broadcasted_iota(jnp.int32, (OCTET, SIDE), 0)

    for chunk in range(CHUNKS):
        with jax.named_scope(f"await_signal{chunk}"):
            pltpu.make_async_copy(
                signal_in.at[chunk], signal_in.at[chunk], signal_recv.at[chunk]
            ).wait()

        with jax.named_scope(f"convolve{chunk}"):
            widen(signal_in.at[chunk], signal_wide)

            @pl.loop(0, OCTET // GROUP)
            def _(group):
                first = group * GROUP
                wave = transform(signal_wide, signal_coarse, first)
                held = spectrum[chunk, group]
                wave_real, wave_imag = wave[:, :SIDE], wave[:, SIDE:]
                held_real, held_imag = held[:, :SIDE], held[:, SIDE:]
                product = jnp.concatenate(
                    [
                        wave_real * held_real - wave_imag * held_imag,
                        wave_real * held_imag + wave_imag * held_real,
                    ],
                    axis=1,
                ).astype(jnp.bfloat16)
                part = dot(product, outof[0]) + dot(product, outof[1])
                cos, sin = turn[:, :SIDE], turn[:, SIDE:]
                turned = []
                for u in range(GROUP):
                    real = part[u * SIDE : (u + 1) * SIDE, :SIDE]
                    imag = part[u * SIDE : (u + 1) * SIDE, SIDE:]
                    turned.append(
                        jnp.concatenate([real * cos - imag * sin, imag * cos + real * sin], axis=0)
                    )
                turned = jnp.concatenate(turned, axis=1).astype(jnp.bfloat16)
                result = dot(back[0], turned) + dot(back[1], turned)
                for u in range(GROUP):
                    wide[pl.ds(first + u, SIDE, stride=OCTET), :] = result[:, u * SIDE : (u + 1) * SIDE]

            gain = jnp.zeros((OCTET, SIDE), jnp.float32)
            for u in range(OCTET):
                place = (core * CHUNKS + chunk) * SIDE + owner * OCTET + u
                gain = jnp.where(line == u, gain_ref[place], gain)
            mixed = wide[...].reshape(SIDE, OCTET, SIDE) + gain[None] * signal_wide[...].reshape(
                SIDE, OCTET, SIDE
            )
            sent[chunk] = mixed.astype(jnp.bfloat16).reshape(sent.shape[1:])

        with jax.named_scope(f"send_back{chunk}"):

            @pl.loop(1, PEERS)
            def _(step):
                other, _, _, device = across(step)
                pltpu.make_async_remote_copy(
                    src_ref=sent.at[chunk, other],
                    dst_ref=returned.at[chunk, z_lo * OWNERS + owner],
                    send_sem=back_send,
                    recv_sem=back_recv.at[chunk],
                    device_id=device,
                    device_id_type=MESH,
                ).start()

            pltpu.make_async_copy(
                sent.at[chunk, me], returned.at[chunk, z_lo * OWNERS + owner], back_recv.at[chunk]
            ).start()

    for chunk in range(CHUNKS):
        with jax.named_scope(f"await_back{chunk}"):
            pltpu.make_async_copy(returned.at[chunk], returned.at[chunk], back_recv.at[chunk]).wait()

        with jax.named_scope(f"send_out{chunk}"):
            for low in range(Z_LO):
                block = returned[chunk, low * OWNERS : (low + 1) * OWNERS].astype(jnp.float32)
                for tile in range(4):
                    part = block[:, tile * OCTET : (tile + 1) * OCTET, :].reshape(SIDE, SIDE)
                    rows[
                        chunk, tile * SIDE : (tile + 1) * SIDE, low * SIDE : (low + 1) * SIDE
                    ] = part.T.astype(jnp.bfloat16)

            @pl.loop(1, Y * CORE)
            def _(step):
                other_y, other_core, device = aside(step)
                for low in range(Z_LO):
                    pltpu.make_async_remote_copy(
                        src_ref=rows.at[chunk, line_of(other_y, other_core), pl.ds(low * SIDE, SIDE)],
                        dst_ref=out_ref.at[:, columns(low, y, core, chunk * SIDE, SIDE)],
                        send_sem=out_send,
                        recv_sem=out_recv,
                        device_id=device,
                        device_id_type=MESH,
                    ).start()

            for low in range(Z_LO):
                pltpu.make_async_copy(
                    rows.at[chunk, line_of(y, core), pl.ds(low * SIDE, SIDE)],
                    out_ref.at[:, columns(low, y, core, chunk * SIDE, SIDE)],
                    out_recv,
                ).start()

    with jax.named_scope("await_out"):
        pltpu.make_async_copy(out_ref, out_ref, out_recv).wait()

    def settle(part, semaphore):
        pltpu.make_async_copy(part, part, semaphore).wait()

    with jax.named_scope("settle"):
        others = (Y * CORE - 1) * count
        settle(slab.at[pl.ds(0, others)], row_send)
        settle(filter_turned.at[pl.ds(0, OWNERS - 1)], filter_send)
        for chunk in range(CHUNKS):
            settle(signal_turned.at[chunk, pl.ds(0, PEERS - 1)], signal_send)
            settle(sent.at[chunk, pl.ds(0, PEERS - 1)], back_send)
        settle(slab.at[pl.ds(0, others)], out_send)


def shards(query_input, key_input, value_input, filters, direct_gain):
    count, channels = key_input.shape
    table = jnp.asarray(tables())
    stays = pl.BlockSpec(memory_space=pltpu.HBM)
    half, single = jnp.bfloat16, jnp.float32
    span = Y * CORE * count
    octets = (SIDE * OCTET, SIDE)
    dma = pltpu.SemaphoreType.DMA
    mixed = pl.pallas_call(
        kernel,
        out_shape=jax.ShapeDtypeStruct((count, channels), half),
        in_specs=[stays] * 3 + [pl.BlockSpec(memory_space=pltpu.SMEM), stays],
        out_specs=pl.BlockSpec(memory_space=pltpu.VMEM),
        scratch_shapes=[
            pltpu.VMEM((count, channels), half),
            pltpu.VMEM((count, channels), half),
            pltpu.VMEM(filters.shape, half),
            pltpu.VMEM(table.shape, single),
            pltpu.VMEM((2 * SIDE, 2 * SIDE), half),
            pltpu.VMEM((2 * SIDE, 2 * SIDE), half),
            pltpu.VMEM((2, 2 * SIDE, 2 * SIDE), half),
            pltpu.VMEM((2, 2 * SIDE, 2 * SIDE), half),
            pltpu.VMEM((2, SIDE, 2 * SIDE), half),
            pltpu.VMEM((count, channels), half),
            pltpu.VMEM((span, span), half),
            pltpu.VMEM((CHUNKS, PEERS, 4 * OCTET, SIDE), half),
            pltpu.VMEM((CHUNKS, PEERS, 4 * OCTET, SIDE), half),
            pltpu.VMEM((OWNERS, CORE * CHUNKS, 4 * OCTET, SIDE), half),
            pltpu.VMEM((CORE * CHUNKS, OWNERS, 4 * OCTET, SIDE), half),
            pltpu.VMEM((CHUNKS, OWNERS, CORE, 4 * OCTET, SIDE), half),
            pltpu.VMEM(octets, single),
            pltpu.VMEM(octets, single),
            pltpu.VMEM((CHUNKS, OCTET // GROUP, GROUP * SIDE, 2 * SIDE), single),
            pltpu.VMEM(octets, single),
            pltpu.VMEM((CHUNKS, PEERS, 4 * OCTET, SIDE), half),
            pltpu.VMEM((CHUNKS, PEERS, 4 * OCTET, SIDE), half),
            pltpu.VMEM((CHUNKS, span, Z_LO * SIDE), half),
            dma((4,)),
            dma(()),
            dma(()),
            dma(()),
            dma(()),
            dma(()),
            dma((2,)),
            dma(()),
            dma((CHUNKS,)),
            dma(()),
            dma((CHUNKS,)),
            dma(()),
            dma(()),
        ],
        compiler_params=pltpu.CompilerParams(
            collective_id=0, has_side_effects=True, vmem_limit_bytes=60 * 1024 * 1024
        ),
    )(key_input, value_input, filters, direct_gain, table)
    return (query_input.astype(jnp.float32) * mixed.astype(jnp.float32)).astype(jnp.bfloat16)


def solution(mesh):
    return jax.shard_map(
        shards,
        mesh=mesh,
        in_specs=(
            P(("ctx", "ch"), None),
            P(("ctx", "ch"), None),
            P(("ctx", "ch"), None),
            P("ctx", "ch"),
            P("ch"),
        ),
        out_specs=P(("ctx", "ch"), None),
        check_vma=False,
    )
```

```python
import functools

import jax
import jax.numpy as jnp
import numpy as np
from jax import lax
from jax.experimental import pallas as pl
from jax.experimental.pallas import tpu as pltpu
from jax.sharding import PartitionSpec as P

MESH = pl.DeviceIdType.MESH
SIDE = 128
OCTET = 8
GROUP = 4
X, Z_HI, CORE = 4, 4, 2
Z_LO, Y = 2, 4
OWNERS = X * Z_HI
PEERS = OWNERS * Z_LO
CHUNKS = 2


def tables():
    length = SIDE * SIDE
    side = np.arange(SIDE)
    offset = side + 0.25
    coarse = 2 * np.pi * np.outer(offset, side) / SIDE
    turn = 2 * np.pi * np.outer(offset, side) / length
    fine = 2 * np.pi * np.outer(side, side) / SIDE
    arrival = side.reshape(OWNERS, CORE, Z_LO, 2).transpose(1, 3, 0, 2).reshape(-1)

    def forward(angle):
        return np.concatenate([np.cos(angle), -np.sin(angle)], axis=0)

    angle = coarse[:, arrival].T
    back = np.concatenate([np.cos(angle), -np.sin(angle)], axis=1) / length
    cos, sin = np.cos(fine), np.sin(fine)
    into = np.block([[cos, -sin], [sin, cos]])
    outof = np.block([[cos, sin], [-sin, cos]])
    stacked = [
        np.concatenate([forward(coarse[:, arrival]), forward(coarse)], axis=1),
        into,
        outof,
        back,
        np.concatenate([np.cos(turn), np.sin(turn)], axis=1),
    ]
    return np.concatenate(stacked, axis=0).astype(np.float32)


def halves(table):
    high = table.astype(jnp.bfloat16)
    return high, (table - high.astype(jnp.float32)).astype(jnp.bfloat16)


def dot(left, right):
    return jnp.dot(left, right, preferred_element_type=jnp.float32)


def kernel(
    key_hbm,
    value_hbm,
    filter_hbm,
    gain_ref,
    tables_hbm,
    out_ref,
    key_ref,
    value_ref,
    filter_ref,
    stacked,
    signal_coarse,
    filter_coarse,
    into,
    outof,
    back,
    gated,
    slab,
    signal_turned,
    signal_in,
    filter_turned,
    filter_mid,
    filter_in,
    signal_wide,
    filter_wide,
    spectrum,
    wide,
    mixed,
    aside_send,
    aside_in,
    sent,
    returned,
    load_sems,
    row_send,
    row_recv,
    filter_send,
    filter_recv,
    swap_send,
    swap_recv,
    signal_send,
    signal_recv,
    back_send,
    back_recv,
    mixed_send,
    mixed_recv,
):
    count = gated.shape[0]
    ctx = lax.axis_index("ctx")
    ch = lax.axis_index("ch")
    x, z_hi, core = ctx // (Z_HI * CORE), lax.rem(ctx // CORE, Z_HI), lax.rem(ctx, CORE)
    z_lo, y = ch // Y, lax.rem(ch, Y)
    owner = x * Z_HI + z_hi
    me = owner * Z_LO + z_lo
    half = lambda low, other_y, other_core: (low * Y + other_y) * CORE + other_core

    loads = [
        pltpu.make_async_copy(source, target, load_sems.at[n])
        for n, (source, target) in enumerate(
            [
                (filter_hbm, filter_ref),
                (key_hbm, key_ref),
                (value_hbm, value_ref),
                (tables_hbm, stacked),
            ]
        )
    ]
    for load_copy in loads:
        load_copy.start()

    def across(step):
        other = lax.rem(me + step + core * (PEERS - 2 * step), PEERS)
        owner_there, low = other // Z_LO, lax.rem(other, Z_LO)
        return other, owner_there, low, (owner_there * CORE + core, low * Y + y)

    def owners(step):
        other = lax.rem(owner + step + core * (OWNERS - 2 * step), OWNERS)
        return other, (other * CORE + core, ch)

    def aside(step):
        other = lax.rem(y * CORE + core + step, Y * CORE)
        other_y, other_core = other // CORE, lax.rem(other, CORE)
        return other_y, other_core, (owner * CORE + other_core, z_lo * Y + other_y)

    barrier = pltpu.get_barrier_semaphore()

    with jax.named_scope("greet"):

        @pl.loop(1, PEERS)
        def _(step):
            pl.semaphore_signal(barrier, inc=1, device_id=across(step)[-1], device_id_type=MESH)

        @pl.loop(1, Y * CORE)
        def _(step):
            pl.semaphore_signal(barrier, inc=1, device_id=aside(step)[-1], device_id_type=MESH)

    line = lax.broadcasted_iota(jnp.int32, (SIDE, SIDE), 0)
    lane = lax.broadcasted_iota(jnp.int32, (SIDE, SIDE), 1)
    place = 64 * ((line >> 1) & 1) + 4 * (line >> 3) + 2 * ((line >> 2) & 1) + (line & 1)
    pick = jnp.where(lane == place, 1.0, 0.0).astype(jnp.bfloat16)

    def turned(source, column):
        block = lax.dot_general(
            pick,
            source[:, column * SIDE : (column + 1) * SIDE],
            (((1,), (1,)), ((), ())),
            preferred_element_type=jnp.float32,
        )
        tiles = [block[:, t * SIDE : (t + 1) * SIDE].reshape(OWNERS, OCTET, SIDE) for t in range(4)]
        return jnp.concatenate(tiles, axis=1).astype(jnp.bfloat16)

    with jax.named_scope("turn_filter"):
        loads[0].wait()
        for column in range(CORE * CHUNKS):
            filter_turned[:, column] = turned(filter_ref, column)

    with jax.named_scope("gate"):
        loads[1].wait()
        loads[2].wait()
        gated[...] = (
            key_ref[...].astype(jnp.float32) * value_ref[...].astype(jnp.float32)
        ).astype(jnp.bfloat16)

    with jax.named_scope("await_greet"):
        pl.semaphore_wait(barrier, PEERS + Y * CORE - 2)

    with jax.named_scope("send_filter"):

        @pl.loop(1, OWNERS)
        def _(step):
            other, device = owners(step)
            pltpu.make_async_remote_copy(
                src_ref=filter_turned.at[other],
                dst_ref=filter_mid.at[:, owner],
                send_sem=filter_send,
                recv_sem=filter_recv,
                device_id=device,
                device_id_type=MESH,
            ).start()

        pltpu.make_async_copy(filter_turned.at[owner], filter_mid.at[:, owner], filter_recv).start()

    def columns(low, other_y, other_core, first, size):
        start = half(low, other_y, other_core) * CHUNKS * SIDE + first
        return pl.ds(pl.multiple_of(start, SIDE), size)

    def line_of(other_y, other_core):
        return pl.ds(pl.multiple_of((other_core * Y + other_y) * count, count), count)

    with jax.named_scope("send_rows"):
        span = CHUNKS * SIDE

        @pl.loop(1, Y * CORE)
        def _(step):
            other_y, other_core, device = aside(step)
            for low in range(Z_LO):
                pltpu.make_async_remote_copy(
                    src_ref=gated.at[:, columns(low, other_y, other_core, 0, span)],
                    dst_ref=slab.at[line_of(y, core), pl.ds(low * span, span)],
                    send_sem=row_send,
                    recv_sem=row_recv,
                    device_id=device,
                    device_id_type=MESH,
                ).start()

        for low in range(Z_LO):
            pltpu.make_async_copy(
                gated.at[:, columns(low, y, core, 0, span)],
                slab.at[line_of(y, core), pl.ds(low * span, span)],
                row_recv,
            ).start()

    with jax.named_scope("split_tables"):
        loads[3].wait()
        for target, start in ((signal_coarse, 0), (filter_coarse, SIDE)):
            high, low = halves(stacked[:256, start : start + SIDE])
            target[:, :SIDE], target[:, SIDE:] = high, low
        for target, start in ((into, 256), (outof, 512), (back, 768)):
            target[0], target[1] = halves(stacked[start : start + target.shape[1]])

    with jax.named_scope("await_rows"):
        pltpu.make_async_copy(slab, slab, row_recv).wait()

    with jax.named_scope("send_signal"):
        for chunk in range(CHUNKS):
            for low in range(Z_LO):
                signal_turned[chunk, low * OWNERS : (low + 1) * OWNERS] = turned(
                    slab, low * CHUNKS + chunk
                )

            @pl.loop(1, PEERS)
            def _(step):
                _, owner_there, low, device = across(step)
                pltpu.make_async_remote_copy(
                    src_ref=signal_turned.at[chunk, low * OWNERS + owner_there],
                    dst_ref=signal_in.at[chunk, me],
                    send_sem=signal_send,
                    recv_sem=signal_recv.at[chunk],
                    device_id=device,
                    device_id_type=MESH,
                ).start()

            pltpu.make_async_copy(
                signal_turned.at[chunk, z_lo * OWNERS + owner],
                signal_in.at[chunk, me],
                signal_recv.at[chunk],
            ).start()

    turn = stacked.at[896:1024]

    def transform(parts, table):
        parts = jnp.concatenate(parts, axis=1).astype(jnp.bfloat16)
        part = dot(table[...], jnp.concatenate([parts, parts], axis=0))
        cos, sin = turn[:, :SIDE], turn[:, SIDE:]
        turned = []
        for u in range(GROUP):
            real = part[:SIDE, u * SIDE : (u + 1) * SIDE]
            imag = part[SIDE:, u * SIDE : (u + 1) * SIDE]
            turned.append(
                jnp.concatenate([real * cos + imag * sin, imag * cos - real * sin], axis=1)
            )
        turned = jnp.concatenate(turned, axis=0).astype(jnp.bfloat16)
        return dot(turned, into[0]) + dot(turned, into[1])

    def widen(source, target):
        target[...] = source[...].astype(jnp.float32).reshape(target.shape)

    with jax.named_scope("await_filter"):
        pltpu.make_async_copy(filter_mid, filter_mid, filter_recv).wait()
        swap = pltpu.make_async_remote_copy(
            src_ref=filter_mid.at[pl.ds((1 - core) * CHUNKS, CHUNKS)],
            dst_ref=filter_in.at[:, :, core],
            send_sem=swap_send,
            recv_sem=swap_recv.at[0],
            device_id=(owner * CORE + 1 - core, ch),
            device_id_type=MESH,
        )
        swap.start()
        keep = pltpu.make_async_copy(
            filter_mid.at[pl.ds(core * CHUNKS, CHUNKS)], filter_in.at[:, :, core], swap_recv.at[1]
        )
        keep.start()
        keep.wait()
        swap.wait()

    with jax.named_scope("transform_filter"):
        for chunk in range(CHUNKS):
            widen(filter_in.at[chunk], filter_wide)

            for group in range(OCTET // GROUP):
                parts = [
                    filter_wide[pl.ds(group * GROUP + u, SIDE, stride=OCTET), :] for u in range(GROUP)
                ]
                spectrum[chunk, group] = transform(parts, filter_coarse)

    left = lax.broadcasted_iota(jnp.int32, (PEERS, SIDE), 1) < SIDE // 2
    left_half = lax.broadcasted_iota(jnp.int32, (SIDE // 2, SIDE), 1) < SIDE // 2

    def convolve(chunk, group):
        parts = [
            jnp.concatenate(
                [
                    signal_wide[pl.ds(tile * OCTET + group * GROUP + u, PEERS, stride=4 * OCTET), :]
                    for tile in range(4)
                ],
                axis=0,
            )
            for u in range(GROUP)
        ]
        wave = transform(parts, signal_coarse)
        held = spectrum[chunk, group]
        wave_real, wave_imag = wave[:, :SIDE], wave[:, SIDE:]
        held_real, held_imag = held[:, :SIDE], held[:, SIDE:]
        product = jnp.concatenate(
            [
                wave_real * held_real - wave_imag * held_imag,
                wave_real * held_imag + wave_imag * held_real,
            ],
            axis=1,
        ).astype(jnp.bfloat16)
        part = dot(product, outof[0]) + dot(product, outof[1])
        cos, sin = turn[:, :SIDE], turn[:, SIDE:]
        spun = []
        for u in range(GROUP):
            real = part[u * SIDE : (u + 1) * SIDE, :SIDE]
            imag = part[u * SIDE : (u + 1) * SIDE, SIDE:]
            spun.append(jnp.concatenate([real * cos - imag * sin, imag * cos + real * sin], axis=0))
        spun = jnp.concatenate(spun, axis=1).astype(jnp.bfloat16)
        result = dot(back[0], spun) + dot(back[1], spun)
        block = (core * CHUNKS + chunk) * SIDE + owner * 4 + group * 2
        for w in range(2):
            pair = []
            for v in range(2):
                u = 2 * v + w
                gain = gain_ref[block + 64 * v + w]
                pair.append(result[:, u * SIDE : (u + 1) * SIDE] + gain * parts[u])
            for tile in range(4):
                first, second = (p[tile * PEERS : (tile + 1) * PEERS] for p in pair)
                mixed[2 * tile, pl.ds(w, PEERS, stride=2), :] = jnp.where(
                    left, first, pltpu.roll(second, SIDE // 2, 1)
                )
                mixed[2 * tile + 1, pl.ds(w, PEERS, stride=2), :] = jnp.where(
                    left, pltpu.roll(first, SIDE // 2, 1), second
                )
        aside_send[chunk, group] = mixed[...].astype(jnp.bfloat16)

    for chunk in range(CHUNKS):
        with jax.named_scope(f"await_signal{chunk}"):
            pltpu.make_async_copy(
                signal_in.at[chunk], signal_in.at[chunk], signal_recv.at[chunk]
            ).wait()

        with jax.named_scope(f"convolve{chunk}"):
            widen(signal_in.at[chunk], signal_wide)
            for group in range(OCTET // GROUP):
                convolve(chunk, group)

                @pl.loop(1, Y * CORE)
                def _(step):
                    other_y, other_core, device = aside(step)
                    pltpu.make_async_remote_copy(
                        src_ref=aside_send.at[chunk, group, other_core * Y + other_y],
                        dst_ref=aside_in.at[chunk, group, y * CORE + core],
                        send_sem=mixed_send,
                        recv_sem=mixed_recv.at[chunk],
                        device_id=device,
                        device_id_type=MESH,
                    ).start()

                pltpu.make_async_copy(
                    aside_send.at[chunk, group, core * Y + y],
                    aside_in.at[chunk, group, y * CORE + core],
                    mixed_recv.at[chunk],
                ).start()

        with jax.named_scope(f"send_back{chunk}"):
            pltpu.make_async_copy(aside_in.at[chunk], aside_in.at[chunk], mixed_recv.at[chunk]).wait()
            widen(aside_in.at[chunk], wide)
            for peer in range(PEERS):
                lines = [
                    wide[pl.ds(group * 512 + peer * 2 + w, OCTET, stride=64), :]
                    for group in range(2)
                    for w in range(2)
                ]
                sent[chunk, peer] = jnp.concatenate(lines, axis=0).astype(jnp.bfloat16)

            @pl.loop(1, PEERS)
            def _(step):
                other, _, _, device = across(step)
                pltpu.make_async_remote_copy(
                    src_ref=sent.at[chunk, other],
                    dst_ref=returned.at[chunk, z_lo * OWNERS + owner],
                    send_sem=back_send,
                    recv_sem=back_recv.at[chunk],
                    device_id=device,
                    device_id_type=MESH,
                ).start()

            pltpu.make_async_copy(
                sent.at[chunk, me], returned.at[chunk, z_lo * OWNERS + owner], back_recv.at[chunk]
            ).start()

    for chunk in range(CHUNKS):
        with jax.named_scope(f"await_back{chunk}"):
            pltpu.make_async_copy(returned.at[chunk], returned.at[chunk], back_recv.at[chunk]).wait()

        with jax.named_scope(f"finish{chunk}"):
            widen(returned.at[chunk], wide)
            for low in range(Z_LO):
                for other_y in range(Y):
                    lines = [
                        wide[pl.ds(low * 512 + other_y * CORE + c, SIDE // 2, stride=OCTET), :]
                        for c in range(CORE)
                    ]
                    block = jnp.concatenate(lines, axis=0).T
                    upper, lower = block[: SIDE // 2], block[SIDE // 2 :]
                    for c, whole in enumerate(
                        (
                            jnp.where(left_half, upper, pltpu.roll(lower, SIDE // 2, 1)),
                            jnp.where(left_half, pltpu.roll(upper, SIDE // 2, 1), lower),
                        )
                    ):
                        start = (half(low, other_y, c) * CHUNKS + chunk) * SIDE
                        out_ref[:, start : start + SIDE] = whole.astype(jnp.bfloat16)

    def settle(part, semaphore):
        pltpu.make_async_copy(part, part, semaphore).wait()

    with jax.named_scope("settle"):
        others = (Y * CORE - 1) * count
        settle(slab.at[pl.ds(0, others)], row_send)
        settle(filter_turned.at[pl.ds(0, OWNERS - 1)], filter_send)
        for chunk in range(CHUNKS):
            settle(signal_turned.at[chunk, pl.ds(0, PEERS - 1)], signal_send)
            settle(sent.at[chunk, pl.ds(0, PEERS - 1)], back_send)
        for part in range(4):
            settle(aside_in.at[part // 2, part % 2, pl.ds(0, Y * CORE - 1)], mixed_send)


def shards(query_input, key_input, value_input, filters, direct_gain):
    count, channels = key_input.shape
    table = jnp.asarray(tables())
    stays = pl.BlockSpec(memory_space=pltpu.HBM)
    half, single = jnp.bfloat16, jnp.float32
    span = Y * CORE * count
    octets = (SIDE * OCTET, SIDE)
    dma = pltpu.SemaphoreType.DMA
    mixed = pl.pallas_call(
        kernel,
        out_shape=jax.ShapeDtypeStruct((count, channels), half),
        in_specs=[stays] * 3 + [pl.BlockSpec(memory_space=pltpu.SMEM), stays],
        out_specs=pl.BlockSpec(memory_space=pltpu.VMEM),
        scratch_shapes=[
            pltpu.VMEM((count, channels), half),
            pltpu.VMEM((count, channels), half),
            pltpu.VMEM(filters.shape, half),
            pltpu.VMEM(table.shape, single),
            pltpu.VMEM((2 * SIDE, 2 * SIDE), half),
            pltpu.VMEM((2 * SIDE, 2 * SIDE), half),
            pltpu.VMEM((2, 2 * SIDE, 2 * SIDE), half),
            pltpu.VMEM((2, 2 * SIDE, 2 * SIDE), half),
            pltpu.VMEM((2, SIDE, 2 * SIDE), half),
            pltpu.VMEM((count, channels), half),
            pltpu.VMEM((span, span), half),
            pltpu.VMEM((CHUNKS, PEERS, 4 * OCTET, SIDE), half),
            pltpu.VMEM((CHUNKS, PEERS, 4 * OCTET, SIDE), half),
            pltpu.VMEM((OWNERS, CORE * CHUNKS, 4 * OCTET, SIDE), half),
            pltpu.VMEM((CORE * CHUNKS, OWNERS, 4 * OCTET, SIDE), half),
            pltpu.VMEM((CHUNKS, OWNERS, CORE, 4 * OCTET, SIDE), half),
            pltpu.VMEM(octets, single),
            pltpu.VMEM(octets, single),
            pltpu.VMEM((CHUNKS, OCTET // GROUP, GROUP * SIDE, 2 * SIDE), single),
            pltpu.VMEM(octets, single),
            pltpu.VMEM((Y * CORE, 2 * PEERS, SIDE), single),
            pltpu.VMEM((CHUNKS, 2, Y * CORE, 2 * PEERS, SIDE), half),
            pltpu.VMEM((CHUNKS, 2, Y * CORE, 2 * PEERS, SIDE), half),
            pltpu.VMEM((CHUNKS, PEERS, 4 * OCTET, SIDE), half),
            pltpu.VMEM((CHUNKS, PEERS, 4 * OCTET, SIDE), half),
            dma((4,)),
            dma(()),
            dma(()),
            dma(()),
            dma(()),
            dma(()),
            dma((2,)),
            dma(()),
            dma((CHUNKS,)),
            dma(()),
            dma((CHUNKS,)),
            dma(()),
            dma((CHUNKS,)),
        ],
        compiler_params=pltpu.CompilerParams(
            collective_id=0, has_side_effects=True, vmem_limit_bytes=60 * 1024 * 1024
        ),
    )(key_input, value_input, filters, direct_gain, table)
    return (query_input.astype(jnp.float32) * mixed.astype(jnp.float32)).astype(jnp.bfloat16)


def solution(mesh):
    return jax.shard_map(
        shards,
        mesh=mesh,
        in_specs=(
            P(("ctx", "ch"), None),
            P(("ctx", "ch"), None),
            P(("ctx", "ch"), None),
            P("ctx", "ch"),
            P("ch"),
        ),
        out_specs=P(("ctx", "ch"), None),
        check_vma=False,
    )
```

```python
import functools

import jax
import jax.numpy as jnp
import numpy as np
from jax import lax
from jax.experimental import pallas as pl
from jax.experimental.pallas import tpu as pltpu
from jax.sharding import PartitionSpec as P

MESH = pl.DeviceIdType.MESH
SIDE = 128
OCTET = 8
GROUP = 4
X, Z_HI, CORE = 4, 4, 2
Z_LO, Y = 2, 4
OWNERS = X * Z_HI
PEERS = OWNERS * Z_LO
CHUNKS = 2


def tables():
    length = SIDE * SIDE
    side = np.arange(SIDE)
    offset = side + 0.25
    coarse = 2 * np.pi * np.outer(offset, side) / SIDE
    turn = 2 * np.pi * np.outer(offset, side) / length
    fine = 2 * np.pi * np.outer(side, side) / SIDE
    arrival = side.reshape(OWNERS, CORE, Z_LO, 2).transpose(1, 3, 0, 2).reshape(-1)

    def forward(angle):
        return np.concatenate([np.cos(angle), -np.sin(angle)], axis=0)

    angle = coarse[:, arrival].T
    back = np.concatenate([np.cos(angle), -np.sin(angle)], axis=1) / length
    cos, sin = np.cos(fine), np.sin(fine)
    into = np.block([[cos, -sin], [sin, cos]])
    outof = np.block([[cos, sin], [-sin, cos]])
    stacked = [
        np.concatenate([forward(coarse[:, arrival]), forward(coarse)], axis=1),
        into,
        outof,
        back,
        np.concatenate([np.cos(turn), np.sin(turn)], axis=1),
    ]
    return np.concatenate(stacked, axis=0).astype(np.float32)


def halves(table):
    high = table.astype(jnp.bfloat16)
    return high, (table - high.astype(jnp.float32)).astype(jnp.bfloat16)


def dot(left, right):
    return jnp.dot(left, right, preferred_element_type=jnp.float32)


def kernel(
    key_hbm,
    value_hbm,
    filter_hbm,
    gain_ref,
    tables_hbm,
    out_ref,
    key_ref,
    value_ref,
    filter_ref,
    stacked,
    signal_coarse,
    filter_coarse,
    into,
    outof,
    back,
    gated,
    slab,
    signal_turned,
    signal_in,
    filter_turned,
    filter_mid,
    filter_in,
    signal_wide,
    filter_wide,
    spectrum,
    wide,
    mixed,
    aside_send,
    aside_in,
    small,
    sent,
    first_sent,
    last_sent,
    returned,
    first_returned,
    last_returned,
    rows,
    first_rows,
    landed,
    first_landed,
    load_sems,
    row_send,
    row_recv,
    filter_send,
    filter_recv,
    swap_send,
    swap_recv,
    signal_send,
    signal_recv,
    back_send,
    back_recv,
    mixed_send,
    mixed_recv,
    out_send,
    out_recv,
):
    count = gated.shape[0]
    ctx = lax.axis_index("ctx")
    ch = lax.axis_index("ch")
    x, z_hi, core = ctx // (Z_HI * CORE), lax.rem(ctx // CORE, Z_HI), lax.rem(ctx, CORE)
    z_lo, y = ch // Y, lax.rem(ch, Y)
    owner = x * Z_HI + z_hi
    me = owner * Z_LO + z_lo
    half = lambda low, other_y, other_core: (low * Y + other_y) * CORE + other_core

    loads = [
        pltpu.make_async_copy(source, target, load_sems.at[n])
        for n, (source, target) in enumerate(
            [
                (filter_hbm, filter_ref),
                (key_hbm, key_ref),
                (value_hbm, value_ref),
                (tables_hbm, stacked),
            ]
        )
    ]
    for load_copy in loads:
        load_copy.start()

    def across(step):
        other = lax.rem(me + step + core * (PEERS - 2 * step), PEERS)
        owner_there, low = other // Z_LO, lax.rem(other, Z_LO)
        return other, owner_there, low, (owner_there * CORE + core, low * Y + y)

    def owners(step):
        other = lax.rem(owner + step + core * (OWNERS - 2 * step), OWNERS)
        return other, (other * CORE + core, ch)

    def aside(step):
        other = lax.rem(y * CORE + core + step, Y * CORE)
        other_y, other_core = other // CORE, lax.rem(other, CORE)
        return other_y, other_core, (owner * CORE + other_core, z_lo * Y + other_y)

    barrier = pltpu.get_barrier_semaphore()

    with jax.named_scope("greet"):

        @pl.loop(1, PEERS)
        def _(step):
            pl.semaphore_signal(barrier, inc=1, device_id=across(step)[-1], device_id_type=MESH)

        @pl.loop(1, Y * CORE)
        def _(step):
            pl.semaphore_signal(barrier, inc=1, device_id=aside(step)[-1], device_id_type=MESH)

    line = lax.broadcasted_iota(jnp.int32, (SIDE, SIDE), 0)
    lane = lax.broadcasted_iota(jnp.int32, (SIDE, SIDE), 1)
    place = jnp.where(
        ((line >> 2) & 1) == 1,
        64 + 32 * ((line >> 1) & 1) + 2 * (line >> 3) + (line & 1),
        4 * (line >> 3) + (line & 3),
    )
    picks = [jnp.where(lane == p, 1.0, 0.0).astype(jnp.bfloat16) for p in (line, place)]

    def turned(source, column):
        block = lax.dot_general(
            picks[column % CHUNKS],
            source[:, column * SIDE : (column + 1) * SIDE],
            (((1,), (1,)), ((), ())),
            preferred_element_type=jnp.float32,
        )
        tiles = [block[:, t * SIDE : (t + 1) * SIDE].reshape(OWNERS, OCTET, SIDE) for t in range(4)]
        return jnp.concatenate(tiles, axis=1).astype(jnp.bfloat16)

    with jax.named_scope("turn_filter"):
        loads[0].wait()
        for column in range(CORE * CHUNKS):
            filter_turned[:, column] = turned(filter_ref, column)

    with jax.named_scope("gate"):
        loads[1].wait()
        loads[2].wait()
        gated[...] = (
            key_ref[...].astype(jnp.float32) * value_ref[...].astype(jnp.float32)
        ).astype(jnp.bfloat16)

    with jax.named_scope("await_greet"):
        pl.semaphore_wait(barrier, PEERS + Y * CORE - 2)

    with jax.named_scope("send_filter"):

        @pl.loop(1, OWNERS)
        def _(step):
            other, device = owners(step)
            pltpu.make_async_remote_copy(
                src_ref=filter_turned.at[other],
                dst_ref=filter_mid.at[:, owner],
                send_sem=filter_send,
                recv_sem=filter_recv,
                device_id=device,
                device_id_type=MESH,
            ).start()

        pltpu.make_async_copy(filter_turned.at[owner], filter_mid.at[:, owner], filter_recv).start()

    def columns(low, other_y, other_core, first, size):
        start = half(low, other_y, other_core) * CHUNKS * SIDE + first
        return pl.ds(pl.multiple_of(start, SIDE), size)

    def line_of(other_y, other_core):
        return pl.ds(pl.multiple_of((other_core * Y + other_y) * count, count), count)

    with jax.named_scope("send_rows"):
        span = CHUNKS * SIDE

        @pl.loop(1, Y * CORE)
        def _(step):
            other_y, other_core, device = aside(step)
            for low in range(Z_LO):
                pltpu.make_async_remote_copy(
                    src_ref=gated.at[:, columns(low, other_y, other_core, 0, span)],
                    dst_ref=slab.at[line_of(y, core), pl.ds(low * span, span)],
                    send_sem=row_send,
                    recv_sem=row_recv,
                    device_id=device,
                    device_id_type=MESH,
                ).start()

        for low in range(Z_LO):
            pltpu.make_async_copy(
                gated.at[:, columns(low, y, core, 0, span)],
                slab.at[line_of(y, core), pl.ds(low * span, span)],
                row_recv,
            ).start()

    with jax.named_scope("split_tables"):
        loads[3].wait()
        for target, start in ((signal_coarse, 0), (filter_coarse, SIDE)):
            high, low = halves(stacked[:256, start : start + SIDE])
            target[:, :SIDE], target[:, SIDE:] = high, low
        for target, start in ((into, 256), (outof, 512), (back, 768)):
            target[0], target[1] = halves(stacked[start : start + target.shape[1]])

    with jax.named_scope("await_rows"):
        pltpu.make_async_copy(slab, slab, row_recv).wait()

    with jax.named_scope("send_signal"):
        for chunk in range(CHUNKS):
            for low in range(Z_LO):
                signal_turned[chunk, low * OWNERS : (low + 1) * OWNERS] = turned(
                    slab, low * CHUNKS + chunk
                )

            @pl.loop(1, PEERS)
            def _(step):
                _, owner_there, low, device = across(step)
                pltpu.make_async_remote_copy(
                    src_ref=signal_turned.at[chunk, low * OWNERS + owner_there],
                    dst_ref=signal_in.at[chunk, me],
                    send_sem=signal_send,
                    recv_sem=signal_recv.at[chunk],
                    device_id=device,
                    device_id_type=MESH,
                ).start()

            pltpu.make_async_copy(
                signal_turned.at[chunk, z_lo * OWNERS + owner],
                signal_in.at[chunk, me],
                signal_recv.at[chunk],
            ).start()

    turn = stacked.at[896:1024]

    def transform(parts, table):
        parts = jnp.concatenate(parts, axis=1).astype(jnp.bfloat16)
        part = dot(table[...], jnp.concatenate([parts, parts], axis=0))
        cos, sin = turn[:, :SIDE], turn[:, SIDE:]
        turned = []
        for u in range(GROUP):
            real = part[:SIDE, u * SIDE : (u + 1) * SIDE]
            imag = part[SIDE:, u * SIDE : (u + 1) * SIDE]
            turned.append(
                jnp.concatenate([real * cos + imag * sin, imag * cos - real * sin], axis=1)
            )
        turned = jnp.concatenate(turned, axis=0).astype(jnp.bfloat16)
        return dot(turned, into[0]) + dot(turned, into[1])

    def widen(source, target):
        target[...] = source[...].astype(jnp.float32).reshape(target.shape)

    with jax.named_scope("await_filter"):
        pltpu.make_async_copy(filter_mid, filter_mid, filter_recv).wait()
        swap = pltpu.make_async_remote_copy(
            src_ref=filter_mid.at[pl.ds((1 - core) * CHUNKS, CHUNKS)],
            dst_ref=filter_in.at[:, :, core],
            send_sem=swap_send,
            recv_sem=swap_recv.at[0],
            device_id=(owner * CORE + 1 - core, ch),
            device_id_type=MESH,
        )
        swap.start()
        keep = pltpu.make_async_copy(
            filter_mid.at[pl.ds(core * CHUNKS, CHUNKS)], filter_in.at[:, :, core], swap_recv.at[1]
        )
        keep.start()
        keep.wait()
        swap.wait()

    with jax.named_scope("transform_filter"):
        for chunk in range(CHUNKS):
            widen(filter_in.at[chunk], filter_wide)

            for group in range(OCTET // GROUP):
                parts = [
                    filter_wide[pl.ds(group * GROUP + u, SIDE, stride=OCTET), :] for u in range(GROUP)
                ]
                spectrum[chunk, group] = transform(parts, filter_coarse)

    left = lax.broadcasted_iota(jnp.int32, (PEERS, SIDE), 1) < SIDE // 2

    def convolve(chunk, group):
        parts = [
            jnp.concatenate(
                [
                    signal_wide[pl.ds(tile * OCTET + group * GROUP + u, PEERS, stride=4 * OCTET), :]
                    for tile in range(4)
                ],
                axis=0,
            )
            for u in range(GROUP)
        ]
        wave = transform(parts, signal_coarse)
        held = spectrum[chunk, group]
        wave_real, wave_imag = wave[:, :SIDE], wave[:, SIDE:]
        held_real, held_imag = held[:, :SIDE], held[:, SIDE:]
        product = jnp.concatenate(
            [
                wave_real * held_real - wave_imag * held_imag,
                wave_real * held_imag + wave_imag * held_real,
            ],
            axis=1,
        ).astype(jnp.bfloat16)
        part = dot(product, outof[0]) + dot(product, outof[1])
        cos, sin = turn[:, :SIDE], turn[:, SIDE:]
        spun = []
        for u in range(GROUP):
            real = part[u * SIDE : (u + 1) * SIDE, :SIDE]
            imag = part[u * SIDE : (u + 1) * SIDE, SIDE:]
            spun.append(jnp.concatenate([real * cos - imag * sin, imag * cos + real * sin], axis=0))
        spun = jnp.concatenate(spun, axis=1).astype(jnp.bfloat16)
        result = dot(back[0], spun) + dot(back[1], spun)
        block = (core * CHUNKS + chunk) * SIDE
        if chunk == 0:
            places = [block + owner * OCTET + group * GROUP + u for u in range(GROUP)]
        elif group == 0:
            places = [block + owner * GROUP + u for u in range(GROUP)]
        else:
            places = [block + 64 + 32 * (u // 2) + 2 * owner + u % 2 for u in range(GROUP)]
        return [
            result[:, u * SIDE : (u + 1) * SIDE] + gain_ref[places[u]] * parts[u]
            for u in range(GROUP)
        ]

    def spread(sums):
        for w in range(2):
            for tile in range(4):
                first, second = (p[tile * PEERS : (tile + 1) * PEERS] for p in (sums[w], sums[2 + w]))
                mixed[2 * tile, pl.ds(w, PEERS, stride=2), :] = jnp.where(
                    left, first, pltpu.roll(second, SIDE // 2, 1)
                )
                mixed[2 * tile + 1, pl.ds(w, PEERS, stride=2), :] = jnp.where(
                    left, pltpu.roll(first, SIDE // 2, 1), second
                )

    def await_signal(chunk):
        pltpu.make_async_copy(signal_in.at[chunk], signal_in.at[chunk], signal_recv.at[chunk]).wait()
        widen(signal_in.at[chunk], signal_wide)

    def send_back(source, target, which):
        @pl.loop(1, PEERS)
        def _(step):
            other, _, _, device = across(step)
            pltpu.make_async_remote_copy(
                src_ref=source.at[other],
                dst_ref=target.at[z_lo * OWNERS + owner],
                send_sem=back_send,
                recv_sem=back_recv.at[which],
                device_id=device,
                device_id_type=MESH,
            ).start()

        pltpu.make_async_copy(
            source.at[me], target.at[z_lo * OWNERS + owner], back_recv.at[which]
        ).start()

    def send_aside(source, target, send_sem, recv_sem):
        @pl.loop(1, Y * CORE)
        def _(step):
            other_y, other_core, device = aside(step)
            pltpu.make_async_remote_copy(
                src_ref=source.at[other_core * Y + other_y],
                dst_ref=target.at[y * CORE + core],
                send_sem=send_sem,
                recv_sem=recv_sem,
                device_id=device,
                device_id_type=MESH,
            ).start()

        pltpu.make_async_copy(source.at[core * Y + y], target.at[y * CORE + core], recv_sem).start()

    def arrived(ref, semaphore):
        pltpu.make_async_copy(ref, ref, semaphore).wait()

    def gather(sums, target, each, first):
        for u in range(GROUP):
            for tile in range(4):
                target[pl.ds(tile * each + first + u, PEERS, stride=4 * each), :] = sums[u][
                    tile * PEERS : (tile + 1) * PEERS
                ]

    with jax.named_scope("convolve0"):
        await_signal(0)
        for group in range(OCTET // GROUP):
            gather(convolve(0, group), wide, OCTET, group * GROUP)
        sent[...] = wide[...].astype(jnp.bfloat16).reshape(sent.shape)
        send_back(sent, returned, 0)

    with jax.named_scope("convolve1"):
        await_signal(1)
        spread(convolve(1, 1))
        aside_send[...] = mixed[...].astype(jnp.bfloat16)
        send_aside(aside_send, aside_in, mixed_send, mixed_recv)
        gather(convolve(1, 0), small, GROUP, 0)
        first_sent[...] = small[...].astype(jnp.bfloat16).reshape(first_sent.shape)
        send_back(first_sent, first_returned, 1)

    with jax.named_scope("relay1"):
        arrived(aside_in, mixed_recv)
        widen(aside_in, small)
        for peer in range(PEERS):
            lines = [small[pl.ds(peer * 2 + w, OCTET, stride=64), :] for w in range(2)]
            last_sent[peer] = jnp.concatenate(lines, axis=0).astype(jnp.bfloat16)
        send_back(last_sent, last_returned, 2)

    with jax.named_scope("send_out0"):
        arrived(returned, back_recv.at[0])
        for low in range(Z_LO):
            block = returned[low * OWNERS : (low + 1) * OWNERS].astype(jnp.float32)
            for tile in range(4):
                part = block[:, tile * OCTET : (tile + 1) * OCTET, :].reshape(SIDE, SIDE)
                rows[2 * tile : 2 * tile + 2, :, low * SIDE : (low + 1) * SIDE] = part.T.astype(
                    jnp.bfloat16
                ).reshape(2, count, SIDE)
        send_aside(rows, landed, out_send, out_recv.at[0])

    with jax.named_scope("send_out1"):
        arrived(first_returned, back_recv.at[1])
        widen(first_returned, small)
        blocks = small[...].reshape(PEERS, 4, GROUP, SIDE)
        for tile in range(4):
            part = blocks[:, tile].reshape(SIDE, SIDE)
            first_rows[2 * tile : 2 * tile + 2] = part.T.astype(jnp.bfloat16).reshape(2, count, SIDE)
        send_aside(first_rows, first_landed, out_send, out_recv.at[1])

    def put(low, other, chunk, block):
        start = ((low * Y * CORE + other) * CHUNKS + chunk) * SIDE
        out_ref[:, start : start + SIDE] = block

    with jax.named_scope("finish0"):
        arrived(landed, out_recv.at[0])
        for low in range(Z_LO):
            for other in range(Y * CORE):
                put(low, other, 0, landed[other, :, low * SIDE : (low + 1) * SIDE])

    quarter = lax.broadcasted_iota(jnp.int32, (count, SIDE), 1) // 32
    with jax.named_scope("finish1"):
        arrived(last_returned, back_recv.at[2])
        widen(last_returned, small)
        lasts = {}
        for low in range(Z_LO):
            for four in range(2):
                lines = [
                    small[pl.ds(low * 256 + four * 4 + k, PEERS, stride=OCTET), :] for k in range(4)
                ]
                block = jnp.concatenate(lines, axis=0).T
                upper, lower = block[:count], block[count:]
                for k in range(4):
                    lasts[low, four * 4 + k] = jnp.where(
                        quarter == 2,
                        upper if k == 2 else pltpu.roll(upper, (64 - 32 * k) % SIDE, 1),
                        lower if k == 3 else pltpu.roll(lower, (96 - 32 * k) % SIDE, 1),
                    )
        arrived(first_landed, out_recv.at[1])
        for other in range(Y * CORE):
            first = first_landed[other].astype(jnp.float32)
            for low in range(Z_LO):
                whole = jnp.where(
                    quarter < 2,
                    pltpu.roll(first, SIDE // 2, 1) if low else first,
                    lasts[low, other],
                )
                put(low, other, 1, whole.astype(jnp.bfloat16))

    def settle(part, semaphore):
        pltpu.make_async_copy(part, part, semaphore).wait()

    with jax.named_scope("settle"):
        others = (Y * CORE - 1) * count
        settle(slab.at[pl.ds(0, others)], row_send)
        settle(filter_turned.at[pl.ds(0, OWNERS - 1)], filter_send)
        for chunk in range(CHUNKS):
            settle(signal_turned.at[chunk, pl.ds(0, PEERS - 1)], signal_send)
        for source in (sent, first_sent, last_sent):
            settle(source.at[pl.ds(0, PEERS - 1)], back_send)
        settle(aside_send.at[pl.ds(0, Y * CORE - 1)], mixed_send)
        for source in (rows, first_rows):
            settle(source.at[pl.ds(0, Y * CORE - 1)], out_send)


def shards(query_input, key_input, value_input, filters, direct_gain):
    count, channels = key_input.shape
    table = jnp.asarray(tables())
    stays = pl.BlockSpec(memory_space=pltpu.HBM)
    half, single = jnp.bfloat16, jnp.float32
    span = Y * CORE * count
    octets = (SIDE * OCTET, SIDE)
    dma = pltpu.SemaphoreType.DMA
    mixed = pl.pallas_call(
        kernel,
        out_shape=jax.ShapeDtypeStruct((count, channels), half),
        in_specs=[stays] * 3 + [pl.BlockSpec(memory_space=pltpu.SMEM), stays],
        out_specs=pl.BlockSpec(memory_space=pltpu.VMEM),
        scratch_shapes=[
            pltpu.VMEM((count, channels), half),
            pltpu.VMEM((count, channels), half),
            pltpu.VMEM(filters.shape, half),
            pltpu.VMEM(table.shape, single),
            pltpu.VMEM((2 * SIDE, 2 * SIDE), half),
            pltpu.VMEM((2 * SIDE, 2 * SIDE), half),
            pltpu.VMEM((2, 2 * SIDE, 2 * SIDE), half),
            pltpu.VMEM((2, 2 * SIDE, 2 * SIDE), half),
            pltpu.VMEM((2, SIDE, 2 * SIDE), half),
            pltpu.VMEM((count, channels), half),
            pltpu.VMEM((span, span), half),
            pltpu.VMEM((CHUNKS, PEERS, 4 * OCTET, SIDE), half),
            pltpu.VMEM((CHUNKS, PEERS, 4 * OCTET, SIDE), half),
            pltpu.VMEM((OWNERS, CORE * CHUNKS, 4 * OCTET, SIDE), half),
            pltpu.VMEM((CORE * CHUNKS, OWNERS, 4 * OCTET, SIDE), half),
            pltpu.VMEM((CHUNKS, OWNERS, CORE, 4 * OCTET, SIDE), half),
            pltpu.VMEM(octets, single),
            pltpu.VMEM(octets, single),
            pltpu.VMEM((CHUNKS, OCTET // GROUP, GROUP * SIDE, 2 * SIDE), single),
            pltpu.VMEM(octets, single),
            pltpu.VMEM((Y * CORE, 2 * PEERS, SIDE), single),
            pltpu.VMEM((Y * CORE, 2 * PEERS, SIDE), half),
            pltpu.VMEM((Y * CORE, 2 * PEERS, SIDE), half),
            pltpu.VMEM((SIDE * GROUP, SIDE), single),
            pltpu.VMEM((PEERS, 4 * OCTET, SIDE), half),
            pltpu.VMEM((PEERS, 4 * GROUP, SIDE), half),
            pltpu.VMEM((PEERS, 4 * GROUP, SIDE), half),
            pltpu.VMEM((PEERS, 4 * OCTET, SIDE), half),
            pltpu.VMEM((PEERS, 4 * GROUP, SIDE), half),
            pltpu.VMEM((PEERS, 4 * GROUP, SIDE), half),
            pltpu.VMEM((Y * CORE, count, Z_LO * SIDE), half),
            pltpu.VMEM((Y * CORE, count, SIDE), half),
            pltpu.VMEM((Y * CORE, count, Z_LO * SIDE), half),
            pltpu.VMEM((Y * CORE, count, SIDE), half),
            dma((4,)),
            dma(()),
            dma(()),
            dma(()),
            dma(()),
            dma(()),
            dma((2,)),
            dma(()),
            dma((CHUNKS,)),
            dma(()),
            dma((3,)),
            dma(()),
            dma(()),
            dma(()),
            dma((2,)),
        ],
        compiler_params=pltpu.CompilerParams(
            collective_id=0, has_side_effects=True, vmem_limit_bytes=56000000
        ),
    )(key_input, value_input, filters, direct_gain, table)
    return (query_input.astype(jnp.float32) * mixed.astype(jnp.float32)).astype(jnp.bfloat16)


def solution(mesh):
    return jax.shard_map(
        shards,
        mesh=mesh,
        in_specs=(
            P(("ctx", "ch"), None),
            P(("ctx", "ch"), None),
            P(("ctx", "ch"), None),
            P("ctx", "ch"),
            P("ch"),
        ),
        out_specs=P(("ctx", "ch"), None),
        check_vma=False,
    )
```

```python
import functools

import jax
import jax.numpy as jnp
import numpy as np
from jax import lax
from jax.experimental import pallas as pl
from jax.experimental.pallas import tpu as pltpu
from jax.sharding import PartitionSpec as P

MESH = pl.DeviceIdType.MESH
SIDE = 128
OCTET = 8
GROUP = 4
X, Z_HI, CORE = 4, 4, 2
Z_LO, Y = 2, 4
OWNERS = X * Z_HI
PEERS = OWNERS * Z_LO
CHUNKS = 2


def tables():
    length = SIDE * SIDE
    side = np.arange(SIDE)
    offset = side + 0.25
    coarse = 2 * np.pi * np.outer(offset, side) / SIDE
    turn = 2 * np.pi * np.outer(offset, side) / length
    fine = 2 * np.pi * np.outer(side, side) / SIDE
    arrival = side.reshape(OWNERS, CORE, Z_LO, 2).transpose(1, 3, 0, 2).reshape(-1)

    def forward(angle):
        return np.concatenate([np.cos(angle), -np.sin(angle)], axis=0)

    angle = coarse[:, arrival].T
    back = np.concatenate([np.cos(angle), -np.sin(angle)], axis=1) / length
    cos, sin = np.cos(fine), np.sin(fine)
    into = np.block([[cos, -sin], [sin, cos]])
    outof = np.block([[cos, sin], [-sin, cos]])
    stacked = [
        np.concatenate([forward(coarse[:, arrival]), forward(coarse)], axis=1),
        into,
        outof,
        back,
        np.concatenate([np.cos(turn), np.sin(turn)], axis=1),
    ]
    return np.concatenate(stacked, axis=0).astype(np.float32)


def halves(table):
    high = table.astype(jnp.bfloat16)
    return high, (table - high.astype(jnp.float32)).astype(jnp.bfloat16)


def dot(left, right):
    return jnp.dot(left, right, preferred_element_type=jnp.float32)


def kernel(
    key_hbm,
    value_hbm,
    filter_hbm,
    gain_ref,
    tables_hbm,
    out_ref,
    key_ref,
    value_ref,
    filter_ref,
    stacked,
    signal_coarse,
    filter_coarse,
    into,
    outof,
    back,
    gated,
    slab,
    signal_turned,
    signal_in,
    filter_turned,
    filter_mid,
    filter_in,
    signal_wide,
    filter_wide,
    spectrum,
    wide,
    mixed,
    aside_send,
    aside_in,
    small,
    sent,
    first_sent,
    last_sent,
    returned,
    first_returned,
    last_returned,
    rows,
    first_rows,
    landed,
    first_landed,
    load_sems,
    row_send,
    row_recv,
    filter_send,
    filter_recv,
    swap_send,
    swap_recv,
    signal_send,
    signal_recv,
    back_send,
    back_recv,
    mixed_send,
    mixed_recv,
    out_send,
    out_recv,
):
    count = gated.shape[0]
    ctx = lax.axis_index("ctx")
    ch = lax.axis_index("ch")
    x, z_hi, core = ctx // (Z_HI * CORE), lax.rem(ctx // CORE, Z_HI), lax.rem(ctx, CORE)
    z_lo, y = ch // Y, lax.rem(ch, Y)
    owner = x * Z_HI + z_hi
    me = owner * Z_LO + z_lo
    half = lambda low, other_y, other_core: (low * Y + other_y) * CORE + other_core

    loads = [
        pltpu.make_async_copy(source, target, load_sems.at[n])
        for n, (source, target) in enumerate(
            [
                (filter_hbm, filter_ref),
                (key_hbm, key_ref),
                (value_hbm, value_ref),
                (tables_hbm, stacked),
            ]
        )
    ]
    for load_copy in loads:
        load_copy.start()

    def across(step):
        other = lax.rem(me + step + core * (PEERS - 2 * step), PEERS)
        owner_there, low = other // Z_LO, lax.rem(other, Z_LO)
        return other, owner_there, low, (owner_there * CORE + core, low * Y + y)

    def owners(step):
        other = lax.rem(owner + step + core * (OWNERS - 2 * step), OWNERS)
        return other, (other * CORE + core, ch)

    def aside(step):
        other = lax.rem(y * CORE + core + step, Y * CORE)
        other_y, other_core = other // CORE, lax.rem(other, CORE)
        return other_y, other_core, (owner * CORE + other_core, z_lo * Y + other_y)

    barrier = pltpu.get_barrier_semaphore()

    with jax.named_scope("greet"):

        @pl.loop(1, PEERS)
        def _(step):
            pl.semaphore_signal(barrier, inc=1, device_id=across(step)[-1], device_id_type=MESH)

        @pl.loop(1, Y * CORE)
        def _(step):
            pl.semaphore_signal(barrier, inc=1, device_id=aside(step)[-1], device_id_type=MESH)

    line = lax.broadcasted_iota(jnp.int32, (SIDE, SIDE), 0)
    lane = lax.broadcasted_iota(jnp.int32, (SIDE, SIDE), 1)
    place = jnp.where(
        ((line >> 2) & 1) == 1,
        64 + 32 * ((line >> 1) & 1) + 2 * (line >> 3) + (line & 1),
        4 * (line >> 3) + (line & 3),
    )
    picks = [jnp.where(lane == p, 1.0, 0.0).astype(jnp.bfloat16) for p in (line, place)]

    def turned(source, column):
        block = lax.dot_general(
            picks[column % CHUNKS],
            source[:, column * SIDE : (column + 1) * SIDE],
            (((1,), (1,)), ((), ())),
            preferred_element_type=jnp.float32,
        )
        tiles = [block[:, t * SIDE : (t + 1) * SIDE].reshape(OWNERS, OCTET, SIDE) for t in range(4)]
        return jnp.concatenate(tiles, axis=1).astype(jnp.bfloat16)

    with jax.named_scope("turn_filter"):
        loads[0].wait()
        for column in range(CORE * CHUNKS):
            filter_turned[:, column] = turned(filter_ref, column)

    with jax.named_scope("gate"):
        loads[1].wait()
        loads[2].wait()
        gated[...] = (
            key_ref[...].astype(jnp.float32) * value_ref[...].astype(jnp.float32)
        ).astype(jnp.bfloat16)

    with jax.named_scope("await_greet"):
        pl.semaphore_wait(barrier, PEERS + Y * CORE - 2)

    with jax.named_scope("send_filter"):

        @pl.loop(1, OWNERS)
        def _(step):
            other, device = owners(step)
            pltpu.make_async_remote_copy(
                src_ref=filter_turned.at[other],
                dst_ref=filter_mid.at[:, owner],
                send_sem=filter_send,
                recv_sem=filter_recv,
                device_id=device,
                device_id_type=MESH,
            ).start()

        pltpu.make_async_copy(filter_turned.at[owner], filter_mid.at[:, owner], filter_recv).start()

    def columns(low, other_y, other_core, first, size):
        start = half(low, other_y, other_core) * CHUNKS * SIDE + first
        return pl.ds(pl.multiple_of(start, SIDE), size)

    def line_of(other_y, other_core):
        return pl.ds(pl.multiple_of((other_core * Y + other_y) * count, count), count)

    with jax.named_scope("send_rows"):
        span = CHUNKS * SIDE

        @pl.loop(1, Y * CORE)
        def _(step):
            other_y, other_core, device = aside(step)
            for low in range(Z_LO):
                pltpu.make_async_remote_copy(
                    src_ref=gated.at[:, columns(low, other_y, other_core, 0, span)],
                    dst_ref=slab.at[line_of(y, core), pl.ds(low * span, span)],
                    send_sem=row_send,
                    recv_sem=row_recv,
                    device_id=device,
                    device_id_type=MESH,
                ).start()

        for low in range(Z_LO):
            pltpu.make_async_copy(
                gated.at[:, columns(low, y, core, 0, span)],
                slab.at[line_of(y, core), pl.ds(low * span, span)],
                row_recv,
            ).start()

    with jax.named_scope("split_tables"):
        loads[3].wait()
        for target, start in ((signal_coarse, 0), (filter_coarse, SIDE)):
            high, low = halves(stacked[:256, start : start + SIDE])
            target[:, :SIDE], target[:, SIDE:] = high, low
        for target, start in ((into, 256), (back, 768)):
            target[0], target[1] = halves(stacked[start : start + target.shape[1]])
        outof[...] = stacked[512:768].astype(jnp.bfloat16)

    with jax.named_scope("await_rows"):
        pltpu.make_async_copy(slab, slab, row_recv).wait()

    with jax.named_scope("send_signal"):
        for chunk in range(CHUNKS):
            for low in range(Z_LO):
                signal_turned[chunk, low * OWNERS : (low + 1) * OWNERS] = turned(
                    slab, low * CHUNKS + chunk
                )

            @pl.loop(1, PEERS)
            def _(step):
                _, owner_there, low, device = across(step)
                pltpu.make_async_remote_copy(
                    src_ref=signal_turned.at[chunk, low * OWNERS + owner_there],
                    dst_ref=signal_in.at[chunk, me],
                    send_sem=signal_send,
                    recv_sem=signal_recv.at[chunk],
                    device_id=device,
                    device_id_type=MESH,
                ).start()

            pltpu.make_async_copy(
                signal_turned.at[chunk, z_lo * OWNERS + owner],
                signal_in.at[chunk, me],
                signal_recv.at[chunk],
            ).start()

    turn = stacked.at[896:1024]

    def transform(parts, table, passes):
        parts = jnp.concatenate(parts, axis=1).astype(jnp.bfloat16)
        part = dot(table[...], jnp.concatenate([parts, parts], axis=0))
        cos, sin = turn[:, :SIDE], turn[:, SIDE:]
        turned = []
        for u in range(GROUP):
            real = part[:SIDE, u * SIDE : (u + 1) * SIDE]
            imag = part[SIDE:, u * SIDE : (u + 1) * SIDE]
            turned.append(
                jnp.concatenate([real * cos + imag * sin, imag * cos - real * sin], axis=1)
            )
        turned = jnp.concatenate(turned, axis=0).astype(jnp.bfloat16)
        return sum(dot(turned, into[k]) for k in range(passes))

    def widen(source, target):
        target[...] = source[...].astype(jnp.float32).reshape(target.shape)

    with jax.named_scope("await_filter"):
        pltpu.make_async_copy(filter_mid, filter_mid, filter_recv).wait()
        swap = pltpu.make_async_remote_copy(
            src_ref=filter_mid.at[pl.ds((1 - core) * CHUNKS, CHUNKS)],
            dst_ref=filter_in.at[:, :, core],
            send_sem=swap_send,
            recv_sem=swap_recv.at[0],
            device_id=(owner * CORE + 1 - core, ch),
            device_id_type=MESH,
        )
        swap.start()
        keep = pltpu.make_async_copy(
            filter_mid.at[pl.ds(core * CHUNKS, CHUNKS)], filter_in.at[:, :, core], swap_recv.at[1]
        )
        keep.start()
        keep.wait()
        swap.wait()

    with jax.named_scope("transform_filter"):
        for chunk in range(CHUNKS):
            widen(filter_in.at[chunk], filter_wide)

            for group in range(OCTET // GROUP):
                parts = [
                    filter_wide[pl.ds(group * GROUP + u, SIDE, stride=OCTET), :] for u in range(GROUP)
                ]
                spectrum[chunk, group] = transform(parts, filter_coarse, 2)

    left = lax.broadcasted_iota(jnp.int32, (PEERS, SIDE), 1) < SIDE // 2

    def convolve(chunk, group):
        parts = [
            jnp.concatenate(
                [
                    signal_wide[pl.ds(tile * OCTET + group * GROUP + u, PEERS, stride=4 * OCTET), :]
                    for tile in range(4)
                ],
                axis=0,
            )
            for u in range(GROUP)
        ]
        wave = transform(parts, signal_coarse, 1)
        held = spectrum[chunk, group]
        wave_real, wave_imag = wave[:, :SIDE], wave[:, SIDE:]
        held_real, held_imag = held[:, :SIDE], held[:, SIDE:]
        product = jnp.concatenate(
            [
                wave_real * held_real - wave_imag * held_imag,
                wave_real * held_imag + wave_imag * held_real,
            ],
            axis=1,
        ).astype(jnp.bfloat16)
        part = dot(product, outof[...])
        cos, sin = turn[:, :SIDE], turn[:, SIDE:]
        spun = []
        for u in range(GROUP):
            real = part[u * SIDE : (u + 1) * SIDE, :SIDE]
            imag = part[u * SIDE : (u + 1) * SIDE, SIDE:]
            spun.append(jnp.concatenate([real * cos - imag * sin, imag * cos + real * sin], axis=0))
        spun = jnp.concatenate(spun, axis=1).astype(jnp.bfloat16)
        result = dot(back[0], spun) + dot(back[1], spun)
        block = (core * CHUNKS + chunk) * SIDE
        if chunk == 0:
            places = [block + owner * OCTET + group * GROUP + u for u in range(GROUP)]
        elif group == 0:
            places = [block + owner * GROUP + u for u in range(GROUP)]
        else:
            places = [block + 64 + 32 * (u // 2) + 2 * owner + u % 2 for u in range(GROUP)]
        return [
            result[:, u * SIDE : (u + 1) * SIDE] + gain_ref[places[u]] * parts[u]
            for u in range(GROUP)
        ]

    def spread(sums):
        for w in range(2):
            for tile in range(4):
                first, second = (p[tile * PEERS : (tile + 1) * PEERS] for p in (sums[w], sums[2 + w]))
                mixed[2 * tile, pl.ds(w, PEERS, stride=2), :] = jnp.where(
                    left, first, pltpu.roll(second, SIDE // 2, 1)
                )
                mixed[2 * tile + 1, pl.ds(w, PEERS, stride=2), :] = jnp.where(
                    left, pltpu.roll(first, SIDE // 2, 1), second
                )

    def await_signal(chunk):
        pltpu.make_async_copy(signal_in.at[chunk], signal_in.at[chunk], signal_recv.at[chunk]).wait()
        widen(signal_in.at[chunk], signal_wide)

    def send_back(source, target, which):
        @pl.loop(1, PEERS)
        def _(step):
            other, _, _, device = across(step)
            pltpu.make_async_remote_copy(
                src_ref=source.at[other],
                dst_ref=target.at[z_lo * OWNERS + owner],
                send_sem=back_send,
                recv_sem=back_recv.at[which],
                device_id=device,
                device_id_type=MESH,
            ).start()

        pltpu.make_async_copy(
            source.at[me], target.at[z_lo * OWNERS + owner], back_recv.at[which]
        ).start()

    def send_aside(source, target, send_sem, recv_sem):
        @pl.loop(1, Y * CORE)
        def _(step):
            other_y, other_core, device = aside(step)
            pltpu.make_async_remote_copy(
                src_ref=source.at[other_core * Y + other_y],
                dst_ref=target.at[y * CORE + core],
                send_sem=send_sem,
                recv_sem=recv_sem,
                device_id=device,
                device_id_type=MESH,
            ).start()

        pltpu.make_async_copy(source.at[core * Y + y], target.at[y * CORE + core], recv_sem).start()

    def arrived(ref, semaphore):
        pltpu.make_async_copy(ref, ref, semaphore).wait()

    def gather(sums, target, each, first):
        for u in range(GROUP):
            for tile in range(4):
                target[pl.ds(tile * each + first + u, PEERS, stride=4 * each), :] = sums[u][
                    tile * PEERS : (tile + 1) * PEERS
                ]

    with jax.named_scope("convolve0"):
        await_signal(0)
        for group in range(OCTET // GROUP):
            gather(convolve(0, group), wide, OCTET, group * GROUP)
        sent[...] = wide[...].astype(jnp.bfloat16).reshape(sent.shape)
        send_back(sent, returned, 0)

    with jax.named_scope("convolve1"):
        await_signal(1)
        spread(convolve(1, 1))
        aside_send[...] = mixed[...].astype(jnp.bfloat16)
        send_aside(aside_send, aside_in, mixed_send, mixed_recv)
        gather(convolve(1, 0), small, GROUP, 0)
        first_sent[...] = small[...].astype(jnp.bfloat16).reshape(first_sent.shape)
        send_back(first_sent, first_returned, 1)

    with jax.named_scope("relay1"):
        arrived(aside_in, mixed_recv)
        widen(aside_in, small)
        for peer in range(PEERS):
            lines = [small[pl.ds(peer * 2 + w, OCTET, stride=64), :] for w in range(2)]
            last_sent[peer] = jnp.concatenate(lines, axis=0).astype(jnp.bfloat16)
        send_back(last_sent, last_returned, 2)

    with jax.named_scope("send_out0"):
        arrived(returned, back_recv.at[0])
        for low in range(Z_LO):
            block = returned[low * OWNERS : (low + 1) * OWNERS].astype(jnp.float32)
            for tile in range(4):
                part = block[:, tile * OCTET : (tile + 1) * OCTET, :].reshape(SIDE, SIDE)
                rows[2 * tile : 2 * tile + 2, :, low * SIDE : (low + 1) * SIDE] = part.T.astype(
                    jnp.bfloat16
                ).reshape(2, count, SIDE)
        send_aside(rows, landed, out_send, out_recv.at[0])

    with jax.named_scope("send_out1"):
        arrived(first_returned, back_recv.at[1])
        widen(first_returned, small)
        blocks = small[...].reshape(PEERS, 4, GROUP, SIDE)
        for tile in range(4):
            part = blocks[:, tile].reshape(SIDE, SIDE)
            first_rows[2 * tile : 2 * tile + 2] = part.T.astype(jnp.bfloat16).reshape(2, count, SIDE)
        send_aside(first_rows, first_landed, out_send, out_recv.at[1])

    def put(low, other, chunk, block):
        start = ((low * Y * CORE + other) * CHUNKS + chunk) * SIDE
        out_ref[:, start : start + SIDE] = block

    with jax.named_scope("finish0"):
        arrived(landed, out_recv.at[0])
        for low in range(Z_LO):
            for other in range(Y * CORE):
                put(low, other, 0, landed[other, :, low * SIDE : (low + 1) * SIDE])

    quarter = lax.broadcasted_iota(jnp.int32, (count, SIDE), 1) // 32
    with jax.named_scope("finish1"):
        arrived(last_returned, back_recv.at[2])
        widen(last_returned, small)
        lasts = {}
        for low in range(Z_LO):
            for four in range(2):
                lines = [
                    small[pl.ds(low * 256 + four * 4 + k, PEERS, stride=OCTET), :] for k in range(4)
                ]
                block = jnp.concatenate(lines, axis=0).T
                upper, lower = block[:count], block[count:]
                for k in range(4):
                    lasts[low, four * 4 + k] = jnp.where(
                        quarter == 2,
                        upper if k == 2 else pltpu.roll(upper, (64 - 32 * k) % SIDE, 1),
                        lower if k == 3 else pltpu.roll(lower, (96 - 32 * k) % SIDE, 1),
                    )
        arrived(first_landed, out_recv.at[1])
        for other in range(Y * CORE):
            first = first_landed[other].astype(jnp.float32)
            for low in range(Z_LO):
                whole = jnp.where(
                    quarter < 2,
                    pltpu.roll(first, SIDE // 2, 1) if low else first,
                    lasts[low, other],
                )
                put(low, other, 1, whole.astype(jnp.bfloat16))

    def settle(part, semaphore):
        pltpu.make_async_copy(part, part, semaphore).wait()

    with jax.named_scope("settle"):
        others = (Y * CORE - 1) * count
        settle(slab.at[pl.ds(0, others)], row_send)
        settle(filter_turned.at[pl.ds(0, OWNERS - 1)], filter_send)
        for chunk in range(CHUNKS):
            settle(signal_turned.at[chunk, pl.ds(0, PEERS - 1)], signal_send)
        for source in (sent, first_sent, last_sent):
            settle(source.at[pl.ds(0, PEERS - 1)], back_send)
        settle(aside_send.at[pl.ds(0, Y * CORE - 1)], mixed_send)
        for source in (rows, first_rows):
            settle(source.at[pl.ds(0, Y * CORE - 1)], out_send)


def shards(query_input, key_input, value_input, filters, direct_gain):
    count, channels = key_input.shape
    table = jnp.asarray(tables())
    stays = pl.BlockSpec(memory_space=pltpu.HBM)
    half, single = jnp.bfloat16, jnp.float32
    span = Y * CORE * count
    octets = (SIDE * OCTET, SIDE)
    dma = pltpu.SemaphoreType.DMA
    mixed = pl.pallas_call(
        kernel,
        out_shape=jax.ShapeDtypeStruct((count, channels), half),
        in_specs=[stays] * 3 + [pl.BlockSpec(memory_space=pltpu.SMEM), stays],
        out_specs=pl.BlockSpec(memory_space=pltpu.VMEM),
        scratch_shapes=[
            pltpu.VMEM((count, channels), half),
            pltpu.VMEM((count, channels), half),
            pltpu.VMEM(filters.shape, half),
            pltpu.VMEM(table.shape, single),
            pltpu.VMEM((2 * SIDE, 2 * SIDE), half),
            pltpu.VMEM((2 * SIDE, 2 * SIDE), half),
            pltpu.VMEM((2, 2 * SIDE, 2 * SIDE), half),
            pltpu.VMEM((2 * SIDE, 2 * SIDE), half),
            pltpu.VMEM((2, SIDE, 2 * SIDE), half),
            pltpu.VMEM((count, channels), half),
            pltpu.VMEM((span, span), half),
            pltpu.VMEM((CHUNKS, PEERS, 4 * OCTET, SIDE), half),
            pltpu.VMEM((CHUNKS, PEERS, 4 * OCTET, SIDE), half),
            pltpu.VMEM((OWNERS, CORE * CHUNKS, 4 * OCTET, SIDE), half),
            pltpu.VMEM((CORE * CHUNKS, OWNERS, 4 * OCTET, SIDE), half),
            pltpu.VMEM((CHUNKS, OWNERS, CORE, 4 * OCTET, SIDE), half),
            pltpu.VMEM(octets, single),
            pltpu.VMEM(octets, single),
            pltpu.VMEM((CHUNKS, OCTET // GROUP, GROUP * SIDE, 2 * SIDE), single),
            pltpu.VMEM(octets, single),
            pltpu.VMEM((Y * CORE, 2 * PEERS, SIDE), single),
            pltpu.VMEM((Y * CORE, 2 * PEERS, SIDE), half),
            pltpu.VMEM((Y * CORE, 2 * PEERS, SIDE), half),
            pltpu.VMEM((SIDE * GROUP, SIDE), single),
            pltpu.VMEM((PEERS, 4 * OCTET, SIDE), half),
            pltpu.VMEM((PEERS, 4 * GROUP, SIDE), half),
            pltpu.VMEM((PEERS, 4 * GROUP, SIDE), half),
            pltpu.VMEM((PEERS, 4 * OCTET, SIDE), half),
            pltpu.VMEM((PEERS, 4 * GROUP, SIDE), half),
            pltpu.VMEM((PEERS, 4 * GROUP, SIDE), half),
            pltpu.VMEM((Y * CORE, count, Z_LO * SIDE), half),
            pltpu.VMEM((Y * CORE, count, SIDE), half),
            pltpu.VMEM((Y * CORE, count, Z_LO * SIDE), half),
            pltpu.VMEM((Y * CORE, count, SIDE), half),
            dma((4,)),
            dma(()),
            dma(()),
            dma(()),
            dma(()),
            dma(()),
            dma((2,)),
            dma(()),
            dma((CHUNKS,)),
            dma(()),
            dma((3,)),
            dma(()),
            dma(()),
            dma(()),
            dma((2,)),
        ],
        compiler_params=pltpu.CompilerParams(
            collective_id=0, has_side_effects=True, vmem_limit_bytes=56000000
        ),
    )(key_input, value_input, filters, pltpu.with_memory_space_constraint(direct_gain, pltpu.HBM), table)
    return (query_input.astype(jnp.float32) * mixed.astype(jnp.float32)).astype(jnp.bfloat16)


def solution(mesh):
    return jax.shard_map(
        shards,
        mesh=mesh,
        in_specs=(
            P(("ctx", "ch"), None),
            P(("ctx", "ch"), None),
            P(("ctx", "ch"), None),
            P("ctx", "ch"),
            P("ch"),
        ),
        out_specs=P(("ctx", "ch"), None),
        check_vma=False,
    )
```

```python
import functools

import jax
import jax.numpy as jnp
import numpy as np
from jax import lax
from jax.experimental import pallas as pl
from jax.experimental.pallas import tpu as pltpu
from jax.sharding import PartitionSpec as P

MESH = pl.DeviceIdType.MESH
SIDE = 128
OCTET = 8
GROUP = 4
X, Z_HI, CORE = 4, 4, 2
Z_LO, Y = 2, 4
OWNERS = X * Z_HI
PEERS = OWNERS * Z_LO
CHUNKS = 2


def tables():
    length = SIDE * SIDE
    side = np.arange(SIDE)
    offset = side + 0.25
    coarse = 2 * np.pi * np.outer(offset, side) / SIDE
    turn = 2 * np.pi * np.outer(offset, side) / length
    fine = 2 * np.pi * np.outer(side, side) / SIDE
    arrival = side.reshape(OWNERS, CORE, Z_LO, 2).transpose(1, 3, 0, 2).reshape(-1)

    def forward(angle):
        return np.concatenate([np.cos(angle), -np.sin(angle)], axis=0)

    angle = coarse[:, arrival].T
    back = np.concatenate([np.cos(angle), -np.sin(angle)], axis=1) / length
    cos, sin = np.cos(fine), np.sin(fine)
    into = np.block([[cos, -sin], [sin, cos]])
    outof = np.block([[cos, sin], [-sin, cos]])
    stacked = [
        np.concatenate([forward(coarse[:, arrival]), forward(coarse)], axis=1),
        into,
        outof,
        back,
        np.concatenate([np.cos(turn), np.sin(turn)], axis=1),
    ]
    return np.concatenate(stacked, axis=0).astype(np.float32)


def halves(table):
    high = table.astype(jnp.bfloat16)
    return high, (table - high.astype(jnp.float32)).astype(jnp.bfloat16)


def dot(left, right):
    return jnp.dot(left, right, preferred_element_type=jnp.float32)


def kernel(
    key_hbm,
    value_hbm,
    filter_hbm,
    gain_ref,
    tables_hbm,
    out_ref,
    key_ref,
    value_ref,
    filter_ref,
    stacked,
    signal_coarse,
    filter_coarse,
    into,
    outof,
    back,
    gated,
    slab,
    signal_turned,
    signal_in,
    part_turned,
    part_in,
    filter_turned,
    filter_mid,
    filter_in,
    signal_wide,
    filter_wide,
    spectrum,
    wide,
    mixed,
    aside_send,
    aside_in,
    small,
    sent,
    first_sent,
    last_sent,
    returned,
    first_returned,
    last_returned,
    rows,
    first_rows,
    landed,
    first_landed,
    load_sems,
    row_send,
    row_recv,
    filter_send,
    filter_recv,
    swap_send,
    swap_recv,
    signal_send,
    signal_recv,
    back_send,
    back_recv,
    mixed_send,
    mixed_recv,
    out_send,
    out_recv,
):
    count = gated.shape[0]
    ctx = lax.axis_index("ctx")
    ch = lax.axis_index("ch")
    x, z_hi, core = ctx // (Z_HI * CORE), lax.rem(ctx // CORE, Z_HI), lax.rem(ctx, CORE)
    z_lo, y = ch // Y, lax.rem(ch, Y)
    owner = x * Z_HI + z_hi
    me = owner * Z_LO + z_lo
    half = lambda low, other_y, other_core: (low * Y + other_y) * CORE + other_core

    loads = [
        pltpu.make_async_copy(source, target, load_sems.at[n])
        for n, (source, target) in enumerate(
            [
                (filter_hbm, filter_ref),
                (key_hbm, key_ref),
                (value_hbm, value_ref),
                (tables_hbm, stacked),
            ]
        )
    ]
    for load_copy in loads:
        load_copy.start()

    def across(step):
        other = lax.rem(me + step + core * (PEERS - 2 * step), PEERS)
        owner_there, low = other // Z_LO, lax.rem(other, Z_LO)
        return other, owner_there, low, (owner_there * CORE + core, low * Y + y)

    def owners(step):
        other = lax.rem(owner + step + core * (OWNERS - 2 * step), OWNERS)
        return other, (other * CORE + core, ch)

    def aside(step):
        other = lax.rem(y * CORE + core + step, Y * CORE)
        other_y, other_core = other // CORE, lax.rem(other, CORE)
        return other_y, other_core, (owner * CORE + other_core, z_lo * Y + other_y)

    barrier = pltpu.get_barrier_semaphore()

    with jax.named_scope("greet"):

        @pl.loop(1, PEERS)
        def _(step):
            pl.semaphore_signal(barrier, inc=1, device_id=across(step)[-1], device_id_type=MESH)

        @pl.loop(1, Y * CORE)
        def _(step):
            pl.semaphore_signal(barrier, inc=1, device_id=aside(step)[-1], device_id_type=MESH)

    line = lax.broadcasted_iota(jnp.int32, (SIDE, SIDE), 0)
    lane = lax.broadcasted_iota(jnp.int32, (SIDE, SIDE), 1)
    group_of = (line >> 2) & 1
    place = jnp.where(
        group_of == 1,
        64 + 32 * ((line >> 1) & 1) + 2 * (line >> 3) + (line & 1),
        4 * (line >> 3) + (line & 3),
    )
    picks = [jnp.where(lane == p, 1.0, 0.0).astype(jnp.bfloat16) for p in (line, place)]

    pairs = []
    for group in range(2):
        channel = line & 3
        if group:
            place = 64 + 32 * (channel >> 1) + 2 * (line >> 3) + (channel & 1)
        else:
            place = 4 * (line >> 3) + channel
        pairs.append(
            jnp.concatenate(
                [
                    jnp.where((lane == place) & (group_of == tile), 1.0, 0.0).astype(jnp.bfloat16)
                    for tile in range(2)
                ],
                axis=1,
            )
        )

    def turned_group(source, column, group):
        parts = []
        for pair in range(2):
            tiles = [
                source[
                    (2 * pair + t) * SIDE : (2 * pair + t + 1) * SIDE,
                    column * SIDE : (column + 1) * SIDE,
                ]
                for t in range(2)
            ]
            block = lax.dot_general(
                pairs[group],
                jnp.concatenate(tiles, axis=1),
                (((1,), (1,)), ((), ())),
                preferred_element_type=jnp.float32,
            )
            parts.append(block.reshape(OWNERS, OCTET, SIDE))
        return jnp.concatenate(parts, axis=1).astype(jnp.bfloat16)

    def turned(source, column):
        block = lax.dot_general(
            picks[column % CHUNKS],
            source[:, column * SIDE : (column + 1) * SIDE],
            (((1,), (1,)), ((), ())),
            preferred_element_type=jnp.float32,
        )
        tiles = [block[:, t * SIDE : (t + 1) * SIDE].reshape(OWNERS, OCTET, SIDE) for t in range(4)]
        return jnp.concatenate(tiles, axis=1).astype(jnp.bfloat16)

    with jax.named_scope("turn_filter"):
        loads[0].wait()
        for column in range(CORE * CHUNKS):
            filter_turned[:, column] = turned(filter_ref, column)

    with jax.named_scope("gate"):
        loads[1].wait()
        loads[2].wait()
        gated[...] = (
            key_ref[...].astype(jnp.float32) * value_ref[...].astype(jnp.float32)
        ).astype(jnp.bfloat16)

    with jax.named_scope("await_greet"):
        pl.semaphore_wait(barrier, PEERS + Y * CORE - 2)

    with jax.named_scope("send_filter"):

        @pl.loop(1, OWNERS)
        def _(step):
            other, device = owners(step)
            pltpu.make_async_remote_copy(
                src_ref=filter_turned.at[other],
                dst_ref=filter_mid.at[:, owner],
                send_sem=filter_send,
                recv_sem=filter_recv,
                device_id=device,
                device_id_type=MESH,
            ).start()

        pltpu.make_async_copy(filter_turned.at[owner], filter_mid.at[:, owner], filter_recv).start()

    def columns(low, other_y, other_core, first, size):
        start = half(low, other_y, other_core) * CHUNKS * SIDE + first
        return pl.ds(pl.multiple_of(start, SIDE), size)

    def line_of(other_y, other_core):
        return pl.ds(pl.multiple_of((other_core * Y + other_y) * count, count), count)

    with jax.named_scope("send_rows"):
        span = CHUNKS * SIDE

        @pl.loop(1, Y * CORE)
        def _(step):
            other_y, other_core, device = aside(step)
            for low in range(Z_LO):
                pltpu.make_async_remote_copy(
                    src_ref=gated.at[:, columns(low, other_y, other_core, 0, span)],
                    dst_ref=slab.at[line_of(y, core), pl.ds(low * span, span)],
                    send_sem=row_send,
                    recv_sem=row_recv,
                    device_id=device,
                    device_id_type=MESH,
                ).start()

        for low in range(Z_LO):
            pltpu.make_async_copy(
                gated.at[:, columns(low, y, core, 0, span)],
                slab.at[line_of(y, core), pl.ds(low * span, span)],
                row_recv,
            ).start()

    with jax.named_scope("split_tables"):
        loads[3].wait()
        for target, start in ((signal_coarse, 0), (filter_coarse, SIDE)):
            high, low = halves(stacked[:256, start : start + SIDE])
            target[:, :SIDE], target[:, SIDE:] = high, low
        for target, start in ((into, 256), (back, 768)):
            target[0], target[1] = halves(stacked[start : start + target.shape[1]])
        outof[...] = stacked[512:768].astype(jnp.bfloat16)

    with jax.named_scope("await_rows"):
        pltpu.make_async_copy(slab, slab, row_recv).wait()

    def send_signal(source, target, which):
        @pl.loop(1, PEERS)
        def _(step):
            _, owner_there, low, device = across(step)
            pltpu.make_async_remote_copy(
                src_ref=source.at[low * OWNERS + owner_there],
                dst_ref=target.at[me],
                send_sem=signal_send,
                recv_sem=signal_recv.at[which],
                device_id=device,
                device_id_type=MESH,
            ).start()

        pltpu.make_async_copy(
            source.at[z_lo * OWNERS + owner], target.at[me], signal_recv.at[which]
        ).start()

    with jax.named_scope("send_signal"):
        for group in (None, 1, 0):
            for low in range(Z_LO):
                here = slice(low * OWNERS, (low + 1) * OWNERS)
                if group is None:
                    signal_turned[here] = turned(slab, low * CHUNKS)
                else:
                    part_turned[group, here] = turned_group(slab, low * CHUNKS + 1, group)
            if group is None:
                send_signal(signal_turned, signal_in, 2)
            else:
                send_signal(part_turned.at[group], part_in.at[group], group)

    turn = stacked.at[896:1024]

    def transform(parts, table, passes):
        parts = jnp.concatenate(parts, axis=1).astype(jnp.bfloat16)
        part = dot(table[...], jnp.concatenate([parts, parts], axis=0))
        cos, sin = turn[:, :SIDE], turn[:, SIDE:]
        turned = []
        for u in range(GROUP):
            real = part[:SIDE, u * SIDE : (u + 1) * SIDE]
            imag = part[SIDE:, u * SIDE : (u + 1) * SIDE]
            turned.append(
                jnp.concatenate([real * cos + imag * sin, imag * cos - real * sin], axis=1)
            )
        turned = jnp.concatenate(turned, axis=0).astype(jnp.bfloat16)
        return sum(dot(turned, into[k]) for k in range(passes))

    def widen(source, target):
        target[...] = source[...].astype(jnp.float32).reshape(target.shape)

    with jax.named_scope("await_filter"):
        pltpu.make_async_copy(filter_mid, filter_mid, filter_recv).wait()
        swap = pltpu.make_async_remote_copy(
            src_ref=filter_mid.at[pl.ds((1 - core) * CHUNKS, CHUNKS)],
            dst_ref=filter_in.at[:, :, core],
            send_sem=swap_send,
            recv_sem=swap_recv.at[0],
            device_id=(owner * CORE + 1 - core, ch),
            device_id_type=MESH,
        )
        swap.start()
        keep = pltpu.make_async_copy(
            filter_mid.at[pl.ds(core * CHUNKS, CHUNKS)], filter_in.at[:, :, core], swap_recv.at[1]
        )
        keep.start()
        keep.wait()
        swap.wait()

    with jax.named_scope("transform_filter"):
        for chunk in range(CHUNKS):
            widen(filter_in.at[chunk], filter_wide)

            for group in range(OCTET // GROUP):
                parts = [
                    filter_wide[pl.ds(group * GROUP + u, SIDE, stride=OCTET), :] for u in range(GROUP)
                ]
                spectrum[chunk, group] = transform(parts, filter_coarse, 2)

    left = lax.broadcasted_iota(jnp.int32, (PEERS, SIDE), 1) < SIDE // 2

    def convolve(chunk, group):
        if chunk == 0:
            source, each, first = signal_wide, OCTET, group * GROUP
        else:
            source, each, first = small, GROUP, 0
        parts = [
            jnp.concatenate(
                [
                    source[pl.ds(tile * each + first + u, PEERS, stride=4 * each), :]
                    for tile in range(4)
                ],
                axis=0,
            )
            for u in range(GROUP)
        ]
        wave = transform(parts, signal_coarse, 1)
        held = spectrum[chunk, group]
        wave_real, wave_imag = wave[:, :SIDE], wave[:, SIDE:]
        held_real, held_imag = held[:, :SIDE], held[:, SIDE:]
        product = jnp.concatenate(
            [
                wave_real * held_real - wave_imag * held_imag,
                wave_real * held_imag + wave_imag * held_real,
            ],
            axis=1,
        ).astype(jnp.bfloat16)
        part = dot(product, outof[...])
        cos, sin = turn[:, :SIDE], turn[:, SIDE:]
        spun = []
        for u in range(GROUP):
            real = part[u * SIDE : (u + 1) * SIDE, :SIDE]
            imag = part[u * SIDE : (u + 1) * SIDE, SIDE:]
            spun.append(jnp.concatenate([real * cos - imag * sin, imag * cos + real * sin], axis=0))
        spun = jnp.concatenate(spun, axis=1).astype(jnp.bfloat16)
        result = dot(back[0], spun) + dot(back[1], spun)
        block = (core * CHUNKS + chunk) * SIDE
        if chunk == 0:
            places = [block + owner * OCTET + group * GROUP + u for u in range(GROUP)]
        elif group == 0:
            places = [block + owner * GROUP + u for u in range(GROUP)]
        else:
            places = [block + 64 + 32 * (u // 2) + 2 * owner + u % 2 for u in range(GROUP)]
        return [
            result[:, u * SIDE : (u + 1) * SIDE] + gain_ref[places[u]] * parts[u]
            for u in range(GROUP)
        ]

    def spread(sums):
        for w in range(2):
            for tile in range(4):
                first, second = (p[tile * PEERS : (tile + 1) * PEERS] for p in (sums[w], sums[2 + w]))
                mixed[2 * tile, pl.ds(w, PEERS, stride=2), :] = jnp.where(
                    left, first, pltpu.roll(second, SIDE // 2, 1)
                )
                mixed[2 * tile + 1, pl.ds(w, PEERS, stride=2), :] = jnp.where(
                    left, pltpu.roll(first, SIDE // 2, 1), second
                )

    def send_back(source, target, which):
        @pl.loop(1, PEERS)
        def _(step):
            other, _, _, device = across(step)
            pltpu.make_async_remote_copy(
                src_ref=source.at[other],
                dst_ref=target.at[z_lo * OWNERS + owner],
                send_sem=back_send,
                recv_sem=back_recv.at[which],
                device_id=device,
                device_id_type=MESH,
            ).start()

        pltpu.make_async_copy(
            source.at[me], target.at[z_lo * OWNERS + owner], back_recv.at[which]
        ).start()

    def send_aside(source, target, send_sem, recv_sem):
        @pl.loop(1, Y * CORE)
        def _(step):
            other_y, other_core, device = aside(step)
            pltpu.make_async_remote_copy(
                src_ref=source.at[other_core * Y + other_y],
                dst_ref=target.at[y * CORE + core],
                send_sem=send_sem,
                recv_sem=recv_sem,
                device_id=device,
                device_id_type=MESH,
            ).start()

        pltpu.make_async_copy(source.at[core * Y + y], target.at[y * CORE + core], recv_sem).start()

    def arrived(ref, semaphore):
        pltpu.make_async_copy(ref, ref, semaphore).wait()

    def gather(sums, target, each, first):
        for u in range(GROUP):
            for tile in range(4):
                target[pl.ds(tile * each + first + u, PEERS, stride=4 * each), :] = sums[u][
                    tile * PEERS : (tile + 1) * PEERS
                ]

    with jax.named_scope("convolve0"):
        arrived(signal_in, signal_recv.at[2])
        widen(signal_in, signal_wide)
        for group in range(OCTET // GROUP):
            gather(convolve(0, group), wide, OCTET, group * GROUP)
        sent[...] = wide[...].astype(jnp.bfloat16).reshape(sent.shape)
        send_back(sent, returned, 0)

    with jax.named_scope("convolve_last"):
        arrived(part_in.at[1], signal_recv.at[1])
        widen(part_in.at[1], small)
        spread(convolve(1, 1))
        aside_send[...] = mixed[...].astype(jnp.bfloat16)
        send_aside(aside_send, aside_in, mixed_send, mixed_recv)

    with jax.named_scope("convolve1"):
        arrived(part_in.at[0], signal_recv.at[0])
        widen(part_in.at[0], small)
        gather(convolve(1, 0), small, GROUP, 0)
        first_sent[...] = small[...].astype(jnp.bfloat16).reshape(first_sent.shape)
        send_back(first_sent, first_returned, 1)

    with jax.named_scope("relay1"):
        arrived(aside_in, mixed_recv)
        widen(aside_in, small)
        for peer in range(PEERS):
            lines = [small[pl.ds(peer * 2 + w, OCTET, stride=64), :] for w in range(2)]
            last_sent[peer] = jnp.concatenate(lines, axis=0).astype(jnp.bfloat16)
        send_back(last_sent, last_returned, 2)

    with jax.named_scope("send_out0"):
        arrived(returned, back_recv.at[0])
        for low in range(Z_LO):
            block = returned[low * OWNERS : (low + 1) * OWNERS].astype(jnp.float32)
            for tile in range(4):
                part = block[:, tile * OCTET : (tile + 1) * OCTET, :].reshape(SIDE, SIDE)
                rows[2 * tile : 2 * tile + 2, :, low * SIDE : (low + 1) * SIDE] = part.T.astype(
                    jnp.bfloat16
                ).reshape(2, count, SIDE)
        send_aside(rows, landed, out_send, out_recv.at[0])

    with jax.named_scope("send_out1"):
        arrived(first_returned, back_recv.at[1])
        widen(first_returned, small)
        blocks = small[...].reshape(PEERS, 4, GROUP, SIDE)
        for tile in range(4):
            part = blocks[:, tile].reshape(SIDE, SIDE)
            first_rows[2 * tile : 2 * tile + 2] = part.T.astype(jnp.bfloat16).reshape(2, count, SIDE)
        send_aside(first_rows, first_landed, out_send, out_recv.at[1])

    def put(low, other, chunk, block):
        start = ((low * Y * CORE + other) * CHUNKS + chunk) * SIDE
        out_ref[:, start : start + SIDE] = block

    with jax.named_scope("finish0"):
        arrived(landed, out_recv.at[0])
        for low in range(Z_LO):
            for other in range(Y * CORE):
                put(low, other, 0, landed[other, :, low * SIDE : (low + 1) * SIDE])

    quarter = lax.broadcasted_iota(jnp.int32, (count, SIDE), 1) // 32
    with jax.named_scope("finish1"):
        arrived(last_returned, back_recv.at[2])
        widen(last_returned, small)
        lasts = {}
        for low in range(Z_LO):
            for four in range(2):
                lines = [
                    small[pl.ds(low * 256 + four * 4 + k, PEERS, stride=OCTET), :] for k in range(4)
                ]
                block = jnp.concatenate(lines, axis=0).T
                upper, lower = block[:count], block[count:]
                for k in range(4):
                    lasts[low, four * 4 + k] = jnp.where(
                        quarter == 2,
                        upper if k == 2 else pltpu.roll(upper, (64 - 32 * k) % SIDE, 1),
                        lower if k == 3 else pltpu.roll(lower, (96 - 32 * k) % SIDE, 1),
                    )
        arrived(first_landed, out_recv.at[1])
        for other in range(Y * CORE):
            first = first_landed[other].astype(jnp.float32)
            for low in range(Z_LO):
                whole = jnp.where(
                    quarter < 2,
                    pltpu.roll(first, SIDE // 2, 1) if low else first,
                    lasts[low, other],
                )
                put(low, other, 1, whole.astype(jnp.bfloat16))

    def settle(part, semaphore):
        pltpu.make_async_copy(part, part, semaphore).wait()

    with jax.named_scope("settle"):
        others = (Y * CORE - 1) * count
        settle(slab.at[pl.ds(0, others)], row_send)
        settle(filter_turned.at[pl.ds(0, OWNERS - 1)], filter_send)
        for source in (signal_turned, part_turned.at[0], part_turned.at[1]):
            settle(source.at[pl.ds(0, PEERS - 1)], signal_send)
        for source in (sent, first_sent, last_sent):
            settle(source.at[pl.ds(0, PEERS - 1)], back_send)
        settle(aside_send.at[pl.ds(0, Y * CORE - 1)], mixed_send)
        for source in (rows, first_rows):
            settle(source.at[pl.ds(0, Y * CORE - 1)], out_send)


def shards(query_input, key_input, value_input, filters, direct_gain):
    count, channels = key_input.shape
    table = jnp.asarray(tables())
    stays = pl.BlockSpec(memory_space=pltpu.HBM)
    half, single = jnp.bfloat16, jnp.float32
    span = Y * CORE * count
    octets = (SIDE * OCTET, SIDE)
    dma = pltpu.SemaphoreType.DMA
    mixed = pl.pallas_call(
        kernel,
        out_shape=jax.ShapeDtypeStruct((count, channels), half),
        in_specs=[stays] * 3 + [pl.BlockSpec(memory_space=pltpu.SMEM), stays],
        out_specs=pl.BlockSpec(memory_space=pltpu.VMEM),
        scratch_shapes=[
            pltpu.VMEM((count, channels), half),
            pltpu.VMEM((count, channels), half),
            pltpu.VMEM(filters.shape, half),
            pltpu.VMEM(table.shape, single),
            pltpu.VMEM((2 * SIDE, 2 * SIDE), half),
            pltpu.VMEM((2 * SIDE, 2 * SIDE), half),
            pltpu.VMEM((2, 2 * SIDE, 2 * SIDE), half),
            pltpu.VMEM((2 * SIDE, 2 * SIDE), half),
            pltpu.VMEM((2, SIDE, 2 * SIDE), half),
            pltpu.VMEM((count, channels), half),
            pltpu.VMEM((span, span), half),
            pltpu.VMEM((PEERS, 4 * OCTET, SIDE), half),
            pltpu.VMEM((PEERS, 4 * OCTET, SIDE), half),
            pltpu.VMEM((2, PEERS, 4 * GROUP, SIDE), half),
            pltpu.VMEM((2, PEERS, 4 * GROUP, SIDE), half),
            pltpu.VMEM((OWNERS, CORE * CHUNKS, 4 * OCTET, SIDE), half),
            pltpu.VMEM((CORE * CHUNKS, OWNERS, 4 * OCTET, SIDE), half),
            pltpu.VMEM((CHUNKS, OWNERS, CORE, 4 * OCTET, SIDE), half),
            pltpu.VMEM(octets, single),
            pltpu.VMEM(octets, single),
            pltpu.VMEM((CHUNKS, OCTET // GROUP, GROUP * SIDE, 2 * SIDE), single),
            pltpu.VMEM(octets, single),
            pltpu.VMEM((Y * CORE, 2 * PEERS, SIDE), single),
            pltpu.VMEM((Y * CORE, 2 * PEERS, SIDE), half),
            pltpu.VMEM((Y * CORE, 2 * PEERS, SIDE), half),
            pltpu.VMEM((SIDE * GROUP, SIDE), single),
            pltpu.VMEM((PEERS, 4 * OCTET, SIDE), half),
            pltpu.VMEM((PEERS, 4 * GROUP, SIDE), half),
            pltpu.VMEM((PEERS, 4 * GROUP, SIDE), half),
            pltpu.VMEM((PEERS, 4 * OCTET, SIDE), half),
            pltpu.VMEM((PEERS, 4 * GROUP, SIDE), half),
            pltpu.VMEM((PEERS, 4 * GROUP, SIDE), half),
            pltpu.VMEM((Y * CORE, count, Z_LO * SIDE), half),
            pltpu.VMEM((Y * CORE, count, SIDE), half),
            pltpu.VMEM((Y * CORE, count, Z_LO * SIDE), half),
            pltpu.VMEM((Y * CORE, count, SIDE), half),
            dma((4,)),
            dma(()),
            dma(()),
            dma(()),
            dma(()),
            dma(()),
            dma((2,)),
            dma(()),
            dma((3,)),
            dma(()),
            dma((3,)),
            dma(()),
            dma(()),
            dma(()),
            dma((2,)),
        ],
        compiler_params=pltpu.CompilerParams(
            collective_id=0, has_side_effects=True, vmem_limit_bytes=56000000
        ),
    )(key_input, value_input, filters, pltpu.with_memory_space_constraint(direct_gain, pltpu.HBM), table)
    return (query_input.astype(jnp.float32) * mixed.astype(jnp.float32)).astype(jnp.bfloat16)


def solution(mesh):
    return jax.shard_map(
        shards,
        mesh=mesh,
        in_specs=(
            P(("ctx", "ch"), None),
            P(("ctx", "ch"), None),
            P(("ctx", "ch"), None),
            P("ctx", "ch"),
            P("ch"),
        ),
        out_specs=P(("ctx", "ch"), None),
        check_vma=False,
    )
```

```python
import functools

import jax
import jax.numpy as jnp
import numpy as np
from jax import lax
from jax.experimental import pallas as pl
from jax.experimental.pallas import tpu as pltpu
from jax.sharding import PartitionSpec as P

MESH = pl.DeviceIdType.MESH
SIDE = 128
OCTET = 8
GROUP = 4
X, Z_HI, CORE = 4, 4, 2
Z_LO, Y = 2, 4
OWNERS = X * Z_HI
PEERS = OWNERS * Z_LO
CHUNKS = 2
ORDER = 0, 1, 3, 2


def tables():
    length = SIDE * SIDE
    side = np.arange(SIDE)
    offset = side + 0.25
    coarse = 2 * np.pi * np.outer(offset, side) / SIDE
    turn = 2 * np.pi * np.outer(offset, side) / length
    fine = 2 * np.pi * np.outer(side, side) / SIDE
    arrival = side.reshape(OWNERS, CORE, Z_LO, 2).transpose(1, 3, 0, 2).reshape(-1)

    def forward(angle):
        return np.concatenate([np.cos(angle), -np.sin(angle)], axis=0)

    angle = coarse[:, arrival].T
    back = np.concatenate([np.cos(angle), -np.sin(angle)], axis=1) / length
    cos, sin = np.cos(fine), np.sin(fine)
    into = np.block([[cos, -sin], [sin, cos]])
    outof = np.block([[cos, sin], [-sin, cos]])
    stacked = [
        np.concatenate([forward(coarse[:, arrival]), forward(coarse)], axis=1),
        into,
        outof,
        back,
        np.concatenate([np.cos(turn), np.sin(turn)], axis=1),
    ]
    return np.concatenate(stacked, axis=0).astype(np.float32)


def halves(table):
    high = table.astype(jnp.bfloat16)
    return high, (table - high.astype(jnp.float32)).astype(jnp.bfloat16)


def dot(left, right):
    return jnp.dot(left, right, preferred_element_type=jnp.float32)


def kernel(
    key_hbm,
    value_hbm,
    filter_hbm,
    gain_ref,
    tables_hbm,
    out_ref,
    key_ref,
    value_ref,
    filter_ref,
    stacked,
    signal_coarse,
    filter_coarse,
    into,
    outof,
    back,
    gated,
    slab,
    part_turned,
    part_in,
    filter_turned,
    filter_mid,
    filter_in,
    filter_wide,
    spectrum,
    mixed,
    aside_send,
    aside_in,
    small,
    sent,
    returned,
    rows,
    landed,
    load_sems,
    row_send,
    row_recv,
    filter_send,
    filter_recv,
    swap_send,
    swap_recv,
    signal_send,
    signal_recv,
    back_send,
    back_recv,
    mixed_send,
    mixed_recv,
    out_send,
    out_recv,
):
    count = gated.shape[0]
    ctx = lax.axis_index("ctx")
    ch = lax.axis_index("ch")
    x, z_hi, core = ctx // (Z_HI * CORE), lax.rem(ctx // CORE, Z_HI), lax.rem(ctx, CORE)
    z_lo, y = ch // Y, lax.rem(ch, Y)
    owner = x * Z_HI + z_hi
    me = owner * Z_LO + z_lo
    half = lambda low, other_y, other_core: (low * Y + other_y) * CORE + other_core

    loads = [
        pltpu.make_async_copy(source, target, load_sems.at[n])
        for n, (source, target) in enumerate(
            [
                (filter_hbm, filter_ref),
                (key_hbm, key_ref),
                (value_hbm, value_ref),
                (tables_hbm, stacked),
            ]
        )
    ]
    for load_copy in loads:
        load_copy.start()

    def across(step):
        other = lax.rem(me + step + core * (PEERS - 2 * step), PEERS)
        owner_there, low = other // Z_LO, lax.rem(other, Z_LO)
        return other, owner_there, low, (owner_there * CORE + core, low * Y + y)

    def owners(step):
        other = lax.rem(owner + step + core * (OWNERS - 2 * step), OWNERS)
        return other, (other * CORE + core, ch)

    def aside(step):
        other = lax.rem(y * CORE + core + step, Y * CORE)
        other_y, other_core = other // CORE, lax.rem(other, CORE)
        return other_y, other_core, (owner * CORE + other_core, z_lo * Y + other_y)

    barrier = pltpu.get_barrier_semaphore()

    with jax.named_scope("greet"):

        @pl.loop(1, PEERS)
        def _(step):
            pl.semaphore_signal(barrier, inc=1, device_id=across(step)[-1], device_id_type=MESH)

        @pl.loop(1, Y * CORE)
        def _(step):
            pl.semaphore_signal(barrier, inc=1, device_id=aside(step)[-1], device_id_type=MESH)

    line = lax.broadcasted_iota(jnp.int32, (SIDE, SIDE), 0)
    lane = lax.broadcasted_iota(jnp.int32, (SIDE, SIDE), 1)
    group_of = (line >> 2) & 1
    direct = 64 * group_of + 4 * (line >> 3) + (line & 3)
    place = jnp.where(
        group_of == 1, 64 + 32 * ((line >> 1) & 1) + 2 * (line >> 3) + (line & 1), direct
    )
    picks = [jnp.where(lane == p, 1.0, 0.0).astype(jnp.bfloat16) for p in (direct, place)]

    pairs = []
    for group in range(4):
        channel = line & 3
        if group == 3:
            place = 64 + 32 * (channel >> 1) + 2 * (line >> 3) + (channel & 1)
        else:
            place = 64 * (group % 2) + 4 * (line >> 3) + channel
        pairs.append(
            jnp.concatenate(
                [
                    jnp.where((lane == place) & (group_of == tile), 1.0, 0.0).astype(jnp.bfloat16)
                    for tile in range(2)
                ],
                axis=1,
            )
        )

    def turned_group(source, group):
        parts = []
        for pair in range(2):
            tiles = [source[(2 * pair + t) * SIDE : (2 * pair + t + 1) * SIDE] for t in range(2)]
            block = lax.dot_general(
                pairs[group],
                jnp.concatenate(tiles, axis=1),
                (((1,), (1,)), ((), ())),
                preferred_element_type=jnp.float32,
            )
            parts.append(block.reshape(OWNERS, OCTET, SIDE))
        return jnp.concatenate(parts, axis=1).astype(jnp.bfloat16)

    def turned(source, column):
        block = lax.dot_general(
            picks[column % CHUNKS],
            source[:, column * SIDE : (column + 1) * SIDE],
            (((1,), (1,)), ((), ())),
            preferred_element_type=jnp.float32,
        )
        tiles = [block[:, t * SIDE : (t + 1) * SIDE].reshape(OWNERS, OCTET, SIDE) for t in range(4)]
        return jnp.concatenate(tiles, axis=1).astype(jnp.bfloat16)

    with jax.named_scope("turn_filter"):
        loads[0].wait()
        for there in range(CORE):
            for chunk in range(CHUNKS):
                filter_turned[:, chunk, there] = turned(filter_ref, there * CHUNKS + chunk)

    with jax.named_scope("gate"):
        loads[1].wait()
        loads[2].wait()
        gated[...] = (
            key_ref[...].astype(jnp.float32) * value_ref[...].astype(jnp.float32)
        ).astype(jnp.bfloat16)

    with jax.named_scope("await_greet"):
        pl.semaphore_wait(barrier, PEERS + Y * CORE - 2)

    def send_filter(chunk):
        @pl.loop(1, OWNERS)
        def _(step):
            other, device = owners(step)
            pltpu.make_async_remote_copy(
                src_ref=filter_turned.at[other, chunk],
                dst_ref=filter_mid.at[chunk, :, owner],
                send_sem=filter_send,
                recv_sem=filter_recv.at[chunk],
                device_id=device,
                device_id_type=MESH,
            ).start()

        pltpu.make_async_copy(
            filter_turned.at[owner, chunk], filter_mid.at[chunk, :, owner], filter_recv.at[chunk]
        ).start()

    with jax.named_scope("send_filter"):
        send_filter(0)

    def columns(low, other_y, other_core, first, size):
        start = half(low, other_y, other_core) * CHUNKS * SIDE + first
        return pl.ds(pl.multiple_of(start, SIDE), size)

    def line_of(other_y, other_core):
        return pl.ds(pl.multiple_of((other_core * Y + other_y) * count, count), count)

    with jax.named_scope("send_rows"):
        for chunk in range(CHUNKS):

            @pl.loop(1, Y * CORE)
            def _(step):
                other_y, other_core, device = aside(step)
                for low in range(Z_LO):
                    pltpu.make_async_remote_copy(
                        src_ref=gated.at[:, columns(low, other_y, other_core, chunk * SIDE, SIDE)],
                        dst_ref=slab.at[chunk, low, line_of(y, core), :],
                        send_sem=row_send,
                        recv_sem=row_recv.at[chunk],
                        device_id=device,
                        device_id_type=MESH,
                    ).start()

            for low in range(Z_LO):
                pltpu.make_async_copy(
                    gated.at[:, columns(low, y, core, chunk * SIDE, SIDE)],
                    slab.at[chunk, low, line_of(y, core), :],
                    row_recv.at[chunk],
                ).start()

    with jax.named_scope("send_filter1"):
        send_filter(1)

    with jax.named_scope("split_tables"):
        loads[3].wait()
        for target, start in ((signal_coarse, 0), (filter_coarse, SIDE)):
            high, low = halves(stacked[:256, start : start + SIDE])
            target[:, :SIDE], target[:, SIDE:] = high, low
        for target, start in ((into, 256), (back, 768)):
            target[0], target[1] = halves(stacked[start : start + target.shape[1]])
        outof[...] = stacked[512:768].astype(jnp.bfloat16)

    def send_signal(source, target, which):
        @pl.loop(1, PEERS)
        def _(step):
            _, owner_there, low, device = across(step)
            pltpu.make_async_remote_copy(
                src_ref=source.at[low * OWNERS + owner_there],
                dst_ref=target.at[me],
                send_sem=signal_send,
                recv_sem=signal_recv.at[which],
                device_id=device,
                device_id_type=MESH,
            ).start()

        pltpu.make_async_copy(
            source.at[z_lo * OWNERS + owner], target.at[me], signal_recv.at[which]
        ).start()

    def send_signals(chunk, groups):
        pltpu.make_async_copy(slab.at[chunk], slab.at[chunk], row_recv.at[chunk]).wait()
        for group in groups:
            for low in range(Z_LO):
                here = slice(low * OWNERS, (low + 1) * OWNERS)
                part_turned[group, here] = turned_group(slab[chunk, low], group)
            send_signal(part_turned.at[group], part_in.at[group], group)

    with jax.named_scope("send_signal"):
        send_signals(0, ORDER[:2])
        send_signals(1, ORDER[2:])

    turn = stacked.at[896:1024]

    def transform(parts, table, passes):
        parts = jnp.concatenate(parts, axis=1).astype(jnp.bfloat16)
        part = dot(table[...], jnp.concatenate([parts, parts], axis=0))
        cos, sin = turn[:, :SIDE], turn[:, SIDE:]
        turned = []
        for u in range(GROUP):
            real = part[:SIDE, u * SIDE : (u + 1) * SIDE]
            imag = part[SIDE:, u * SIDE : (u + 1) * SIDE]
            turned.append(
                jnp.concatenate([real * cos + imag * sin, imag * cos - real * sin], axis=1)
            )
        turned = jnp.concatenate(turned, axis=0).astype(jnp.bfloat16)
        return sum(dot(turned, into[k]) for k in range(passes))

    def widen(source, target):
        target[...] = source[...].astype(jnp.float32).reshape(target.shape)

    def take_filter(chunk):
        pltpu.make_async_copy(
            filter_mid.at[chunk], filter_mid.at[chunk], filter_recv.at[chunk]
        ).wait()
        swap = pltpu.make_async_remote_copy(
            src_ref=filter_mid.at[chunk, 1 - core],
            dst_ref=filter_in.at[chunk, :, core],
            send_sem=swap_send,
            recv_sem=swap_recv.at[0, chunk],
            device_id=(owner * CORE + 1 - core, ch),
            device_id_type=MESH,
        )
        swap.start()
        keep = pltpu.make_async_copy(
            filter_mid.at[chunk, core], filter_in.at[chunk, :, core], swap_recv.at[1, chunk]
        )
        keep.start()
        keep.wait()
        swap.wait()

    def transform_filter(chunk):
        widen(filter_in.at[chunk], filter_wide)
        for group in range(OCTET // GROUP):
            parts = [
                filter_wide[pl.ds(group * GROUP + u, SIDE, stride=OCTET), :] for u in range(GROUP)
            ]
            spectrum[chunk, group] = transform(parts, filter_coarse, 2)

    with jax.named_scope("take_filter0"):
        take_filter(0)
        transform_filter(0)

    left = lax.broadcasted_iota(jnp.int32, (PEERS, SIDE), 1) < SIDE // 2

    def convolve(chunk, group):
        parts = [
            jnp.concatenate(
                [
                    small[pl.ds(tile * GROUP + u, PEERS, stride=4 * GROUP), :]
                    for tile in range(4)
                ],
                axis=0,
            )
            for u in range(GROUP)
        ]
        wave = transform(parts, signal_coarse, 1)
        held = spectrum[chunk, group]
        wave_real, wave_imag = wave[:, :SIDE], wave[:, SIDE:]
        held_real, held_imag = held[:, :SIDE], held[:, SIDE:]
        product = jnp.concatenate(
            [
                wave_real * held_real - wave_imag * held_imag,
                wave_real * held_imag + wave_imag * held_real,
            ],
            axis=1,
        ).astype(jnp.bfloat16)
        part = dot(product, outof[...])
        cos, sin = turn[:, :SIDE], turn[:, SIDE:]
        spun = []
        for u in range(GROUP):
            real = part[u * SIDE : (u + 1) * SIDE, :SIDE]
            imag = part[u * SIDE : (u + 1) * SIDE, SIDE:]
            spun.append(jnp.concatenate([real * cos - imag * sin, imag * cos + real * sin], axis=0))
        spun = jnp.concatenate(spun, axis=1).astype(jnp.bfloat16)
        result = dot(back[0], spun) + dot(back[1], spun)
        block = (core * CHUNKS + chunk) * SIDE
        if chunk == 0 or group == 0:
            places = [block + 64 * group + owner * GROUP + u for u in range(GROUP)]
        else:
            places = [block + 64 + 32 * (u // 2) + 2 * owner + u % 2 for u in range(GROUP)]
        return [
            result[:, u * SIDE : (u + 1) * SIDE] + gain_ref[places[u]] * parts[u]
            for u in range(GROUP)
        ]

    def spread(sums):
        for w in range(2):
            for tile in range(4):
                first, second = (p[tile * PEERS : (tile + 1) * PEERS] for p in (sums[w], sums[2 + w]))
                mixed[2 * tile, pl.ds(w, PEERS, stride=2), :] = jnp.where(
                    left, first, pltpu.roll(second, SIDE // 2, 1)
                )
                mixed[2 * tile + 1, pl.ds(w, PEERS, stride=2), :] = jnp.where(
                    left, pltpu.roll(first, SIDE // 2, 1), second
                )

    def send_back(source, target, which):
        @pl.loop(1, PEERS)
        def _(step):
            other, _, _, device = across(step)
            pltpu.make_async_remote_copy(
                src_ref=source.at[other],
                dst_ref=target.at[z_lo * OWNERS + owner],
                send_sem=back_send,
                recv_sem=back_recv.at[which],
                device_id=device,
                device_id_type=MESH,
            ).start()

        pltpu.make_async_copy(
            source.at[me], target.at[z_lo * OWNERS + owner], back_recv.at[which]
        ).start()

    def send_aside(source, target, send_sem, recv_sem):
        @pl.loop(1, Y * CORE)
        def _(step):
            other_y, other_core, device = aside(step)
            pltpu.make_async_remote_copy(
                src_ref=source.at[other_core * Y + other_y],
                dst_ref=target.at[y * CORE + core],
                send_sem=send_sem,
                recv_sem=recv_sem,
                device_id=device,
                device_id_type=MESH,
            ).start()

        pltpu.make_async_copy(source.at[core * Y + y], target.at[y * CORE + core], recv_sem).start()

    def arrived(ref, semaphore):
        pltpu.make_async_copy(ref, ref, semaphore).wait()

    def await_signal(group):
        arrived(part_in.at[group], signal_recv.at[group])
        widen(part_in.at[group], small)

    def send_direct(which):
        await_signal(which)
        sums = convolve(which // 2, which % 2)
        for u in range(GROUP):
            for tile in range(4):
                small[pl.ds(tile * GROUP + u, PEERS, stride=4 * GROUP), :] = sums[u][
                    tile * PEERS : (tile + 1) * PEERS
                ]
        sent[which] = small[...].astype(jnp.bfloat16).reshape(sent.shape[1:])
        send_back(sent.at[which], returned.at[which], which)

    def send_first():
        await_signal(3)
        spread(convolve(1, 1))
        aside_send[...] = mixed[...].astype(jnp.bfloat16)
        send_aside(aside_send, aside_in, mixed_send, mixed_recv)

    for group in ORDER:
        if group == ORDER[2]:
            with jax.named_scope("take_filter1"):
                take_filter(1)
                transform_filter(1)

        with jax.named_scope(f"convolve{group}"):
            if group < 3:
                send_direct(group)
            else:
                send_first()

    with jax.named_scope("relay"):
        arrived(aside_in, mixed_recv)
        widen(aside_in, small)
        for peer in range(PEERS):
            lines = [small[pl.ds(peer * 2 + w, OCTET, stride=64), :] for w in range(2)]
            sent[3, peer] = jnp.concatenate(lines, axis=0).astype(jnp.bfloat16)
        send_back(sent.at[3], returned.at[3], 3)

    for which in range(3):
        with jax.named_scope(f"send_out{which}"):
            arrived(returned.at[which], back_recv.at[which])
            widen(returned.at[which], small)
            blocks = small[...].reshape(PEERS, 4, GROUP, SIDE)
            for tile in range(4):
                part = blocks[:, tile].reshape(SIDE, SIDE)
                rows[which, 2 * tile : 2 * tile + 2] = part.T.astype(jnp.bfloat16).reshape(
                    2, count, SIDE
                )
            send_aside(rows.at[which], landed.at[which], out_send, out_recv.at[which])

    def put(low, other, chunk, block):
        start = ((low * Y * CORE + other) * CHUNKS + chunk) * SIDE
        out_ref[:, start : start + SIDE] = block

    quarter = lax.broadcasted_iota(jnp.int32, (count, SIDE), 1) // 32
    with jax.named_scope("finish0"):
        arrived(landed.at[0], out_recv.at[0])
        arrived(landed.at[1], out_recv.at[1])
        for other in range(Y * CORE):
            first, second = (landed[group, other].astype(jnp.float32) for group in range(2))
            for low in range(Z_LO):
                whole = jnp.where(
                    quarter < 2,
                    pltpu.roll(first, SIDE // 2, 1) if low else first,
                    second if low else pltpu.roll(second, SIDE // 2, 1),
                )
                put(low, other, 0, whole.astype(jnp.bfloat16))

    with jax.named_scope("finish1"):
        arrived(returned.at[3], back_recv.at[3])
        widen(returned.at[3], small)
        lasts = {}
        for low in range(Z_LO):
            for four in range(2):
                lines = [
                    small[pl.ds(low * 256 + four * 4 + k, PEERS, stride=OCTET), :] for k in range(4)
                ]
                block = jnp.concatenate(lines, axis=0).T
                upper, lower = block[:count], block[count:]
                for k in range(4):
                    lasts[low, four * 4 + k] = jnp.where(
                        quarter == 2,
                        upper if k == 2 else pltpu.roll(upper, (64 - 32 * k) % SIDE, 1),
                        lower if k == 3 else pltpu.roll(lower, (96 - 32 * k) % SIDE, 1),
                    )
        arrived(landed.at[2], out_recv.at[2])
        for other in range(Y * CORE):
            first = landed[2, other].astype(jnp.float32)
            for low in range(Z_LO):
                whole = jnp.where(
                    quarter < 2,
                    pltpu.roll(first, SIDE // 2, 1) if low else first,
                    lasts[low, other],
                )
                put(low, other, 1, whole.astype(jnp.bfloat16))

    def settle(part, semaphore):
        pltpu.make_async_copy(part, part, semaphore).wait()

    with jax.named_scope("settle"):
        for chunk in range(CHUNKS):
            settle(slab.at[chunk, :, pl.ds(0, (Y * CORE - 1) * count)], row_send)
        settle(filter_turned.at[pl.ds(0, OWNERS - 1)], filter_send)
        for which in range(4):
            settle(part_turned.at[which, pl.ds(0, PEERS - 1)], signal_send)
            settle(sent.at[which, pl.ds(0, PEERS - 1)], back_send)
        settle(aside_send.at[pl.ds(0, Y * CORE - 1)], mixed_send)
        for which in range(3):
            settle(rows.at[which, pl.ds(0, Y * CORE - 1)], out_send)


def shards(query_input, key_input, value_input, filters, direct_gain):
    count, channels = key_input.shape
    table = jnp.asarray(tables())
    stays = pl.BlockSpec(memory_space=pltpu.HBM)
    half, single = jnp.bfloat16, jnp.float32
    span = Y * CORE * count
    octets = (SIDE * OCTET, SIDE)
    dma = pltpu.SemaphoreType.DMA
    mixed = pl.pallas_call(
        kernel,
        out_shape=jax.ShapeDtypeStruct((count, channels), half),
        in_specs=[stays] * 3 + [pl.BlockSpec(memory_space=pltpu.SMEM), stays],
        out_specs=pl.BlockSpec(memory_space=pltpu.VMEM),
        scratch_shapes=[
            pltpu.VMEM((count, channels), half),
            pltpu.VMEM((count, channels), half),
            pltpu.VMEM(filters.shape, half),
            pltpu.VMEM(table.shape, single),
            pltpu.VMEM((2 * SIDE, 2 * SIDE), half),
            pltpu.VMEM((2 * SIDE, 2 * SIDE), half),
            pltpu.VMEM((2, 2 * SIDE, 2 * SIDE), half),
            pltpu.VMEM((2 * SIDE, 2 * SIDE), half),
            pltpu.VMEM((2, SIDE, 2 * SIDE), half),
            pltpu.VMEM((count, channels), half),
            pltpu.VMEM((CHUNKS, Z_LO, span, SIDE), half),
            pltpu.VMEM((4, PEERS, 4 * GROUP, SIDE), half),
            pltpu.VMEM((4, PEERS, 4 * GROUP, SIDE), half),
            pltpu.VMEM((OWNERS, CHUNKS, CORE, 4 * OCTET, SIDE), half),
            pltpu.VMEM((CHUNKS, CORE, OWNERS, 4 * OCTET, SIDE), half),
            pltpu.VMEM((CHUNKS, OWNERS, CORE, 4 * OCTET, SIDE), half),
            pltpu.VMEM(octets, single),
            pltpu.VMEM((CHUNKS, OCTET // GROUP, GROUP * SIDE, 2 * SIDE), single),
            pltpu.VMEM((Y * CORE, 2 * PEERS, SIDE), single),
            pltpu.VMEM((Y * CORE, 2 * PEERS, SIDE), half),
            pltpu.VMEM((Y * CORE, 2 * PEERS, SIDE), half),
            pltpu.VMEM((SIDE * GROUP, SIDE), single),
            pltpu.VMEM((4, PEERS, 4 * GROUP, SIDE), half),
            pltpu.VMEM((4, PEERS, 4 * GROUP, SIDE), half),
            pltpu.VMEM((3, Y * CORE, count, SIDE), half),
            pltpu.VMEM((3, Y * CORE, count, SIDE), half),
            dma((4,)),
            dma(()),
            dma((CHUNKS,)),
            dma(()),
            dma((CHUNKS,)),
            dma(()),
            dma((2, CHUNKS)),
            dma(()),
            dma((4,)),
            dma(()),
            dma((4,)),
            dma(()),
            dma(()),
            dma(()),
            dma((3,)),
        ],
        compiler_params=pltpu.CompilerParams(
            collective_id=0, has_side_effects=True, vmem_limit_bytes=56000000
        ),
    )(key_input, value_input, filters, pltpu.with_memory_space_constraint(direct_gain, pltpu.HBM), table)
    return (query_input.astype(jnp.float32) * mixed.astype(jnp.float32)).astype(jnp.bfloat16)


def solution(mesh):
    return jax.shard_map(
        shards,
        mesh=mesh,
        in_specs=(
            P(("ctx", "ch"), None),
            P(("ctx", "ch"), None),
            P(("ctx", "ch"), None),
            P("ctx", "ch"),
            P("ch"),
        ),
        out_specs=P(("ctx", "ch"), None),
        check_vma=False,
    )
```

```python
import functools

import jax
import jax.numpy as jnp
import numpy as np
from jax import lax
from jax.experimental import pallas as pl
from jax.experimental.pallas import tpu as pltpu
from jax.sharding import PartitionSpec as P

MESH = pl.DeviceIdType.MESH
SIDE = 128
OCTET = 8
GROUP = 4
X, Z_HI, CORE = 4, 4, 2
Z_LO, Y = 2, 4
OWNERS = X * Z_HI
PEERS = OWNERS * Z_LO
CHUNKS = 2
ORDER = 0, 1, 3, 2


def tables():
    length = SIDE * SIDE
    side = np.arange(SIDE)
    offset = side + 0.25
    coarse = 2 * np.pi * np.outer(offset, side) / SIDE
    turn = 2 * np.pi * np.outer(offset, side) / length
    fine = 2 * np.pi * np.outer(side, side) / SIDE
    arrival = side.reshape(OWNERS, CORE, Z_LO, 2).transpose(1, 3, 0, 2).reshape(-1)

    def forward(angle):
        return np.concatenate([np.cos(angle), -np.sin(angle)], axis=0)

    angle = coarse[:, arrival].T
    back = np.concatenate([np.cos(angle), -np.sin(angle)], axis=1) / length
    cos, sin = np.cos(fine), np.sin(fine)
    into = np.block([[cos, -sin], [sin, cos]])
    outof = np.block([[cos, sin], [-sin, cos]])
    stacked = [
        np.concatenate([forward(coarse[:, arrival]), forward(coarse)], axis=1),
        into,
        outof,
        back,
        np.concatenate([np.cos(turn), np.sin(turn)], axis=1),
    ]
    return np.concatenate(stacked, axis=0).astype(np.float32)


def halves(table):
    high = table.astype(jnp.bfloat16)
    return high, (table - high.astype(jnp.float32)).astype(jnp.bfloat16)


def dot(left, right):
    return jnp.dot(left, right, preferred_element_type=jnp.float32)


def kernel(
    key_hbm,
    value_hbm,
    filter_hbm,
    gain_ref,
    tables_hbm,
    out_ref,
    key_ref,
    value_ref,
    filter_ref,
    stacked,
    signal_coarse,
    filter_coarse,
    into,
    outof,
    back,
    gated,
    slab,
    part_turned,
    part_in,
    filter_turned,
    filter_mid,
    filter_in,
    filter_wide,
    spectrum,
    mixed,
    aside_send,
    aside_in,
    small,
    sent,
    returned,
    rows,
    landed,
    load_sems,
    row_send,
    row_recv,
    filter_send,
    filter_recv,
    swap_send,
    swap_recv,
    signal_send,
    signal_recv,
    back_send,
    back_recv,
    mixed_send,
    mixed_recv,
    out_send,
    out_recv,
):
    count = gated.shape[0]
    ctx = lax.axis_index("ctx")
    ch = lax.axis_index("ch")
    x, z_hi, core = ctx // (Z_HI * CORE), lax.rem(ctx // CORE, Z_HI), lax.rem(ctx, CORE)
    z_lo, y = ch // Y, lax.rem(ch, Y)
    owner = x * Z_HI + z_hi
    me = owner * Z_LO + z_lo
    half = lambda low, other_y, other_core: (low * Y + other_y) * CORE + other_core

    loads = [
        pltpu.make_async_copy(source, target, load_sems.at[n])
        for n, (source, target) in enumerate(
            [
                (filter_hbm, filter_ref),
                (key_hbm, key_ref),
                (value_hbm, value_ref),
                (tables_hbm, stacked),
            ]
        )
    ]
    for load_copy in loads:
        load_copy.start()

    def across(step):
        other = lax.rem(me + step + core * (PEERS - 2 * step), PEERS)
        owner_there, low = other // Z_LO, lax.rem(other, Z_LO)
        return other, owner_there, low, (owner_there * CORE + core, low * Y + y)

    def owners(step):
        other = lax.rem(owner + step + core * (OWNERS - 2 * step), OWNERS)
        return other, (other * CORE + core, ch)

    def aside(step):
        other = lax.rem(y * CORE + core + step, Y * CORE)
        other_y, other_core = other // CORE, lax.rem(other, CORE)
        return other_y, other_core, (owner * CORE + other_core, z_lo * Y + other_y)

    barrier = pltpu.get_barrier_semaphore()

    with jax.named_scope("greet"):

        @pl.loop(1, PEERS)
        def _(step):
            pl.semaphore_signal(barrier, inc=1, device_id=across(step)[-1], device_id_type=MESH)

        @pl.loop(1, Y * CORE)
        def _(step):
            pl.semaphore_signal(barrier, inc=1, device_id=aside(step)[-1], device_id_type=MESH)

    line = lax.broadcasted_iota(jnp.int32, (SIDE, SIDE), 0)
    lane = lax.broadcasted_iota(jnp.int32, (SIDE, SIDE), 1)
    group_of = (line >> 2) & 1
    direct = 64 * group_of + 4 * (line >> 3) + (line & 3)
    place = jnp.where(
        group_of == 1, 64 + 32 * ((line >> 1) & 1) + 2 * (line >> 3) + (line & 1), direct
    )
    picks = [jnp.where(lane == p, 1.0, 0.0).astype(jnp.bfloat16) for p in (direct, place)]

    pairs = []
    for group in range(4):
        channel = line & 3
        if group == 3:
            place = 64 + 32 * (channel >> 1) + 2 * (line >> 3) + (channel & 1)
        else:
            place = 64 * (group % 2) + 4 * (line >> 3) + channel
        pairs.append(
            jnp.concatenate(
                [
                    jnp.where((lane == place) & (group_of == tile), 1.0, 0.0).astype(jnp.bfloat16)
                    for tile in range(2)
                ],
                axis=1,
            )
        )

    def turned_group(source, group):
        parts = []
        for pair in range(2):
            tiles = [source[(2 * pair + t) * SIDE : (2 * pair + t + 1) * SIDE] for t in range(2)]
            block = lax.dot_general(
                pairs[group],
                jnp.concatenate(tiles, axis=1),
                (((1,), (1,)), ((), ())),
                preferred_element_type=jnp.float32,
            )
            parts.append(block.reshape(OWNERS, OCTET, SIDE))
        return jnp.concatenate(parts, axis=1).astype(jnp.bfloat16)

    def turned(source, column):
        block = lax.dot_general(
            picks[column % CHUNKS],
            source[:, column * SIDE : (column + 1) * SIDE],
            (((1,), (1,)), ((), ())),
            preferred_element_type=jnp.float32,
        )
        tiles = [block[:, t * SIDE : (t + 1) * SIDE].reshape(OWNERS, OCTET, SIDE) for t in range(4)]
        return jnp.concatenate(tiles, axis=1).astype(jnp.bfloat16)

    with jax.named_scope("turn_filter"):
        loads[0].wait()
        for there in range(CORE):
            for chunk in range(CHUNKS):
                filter_turned[:, chunk, there] = turned(filter_ref, there * CHUNKS + chunk)

    with jax.named_scope("gate"):
        loads[1].wait()
        loads[2].wait()
        gated[...] = (
            key_ref[...].astype(jnp.float32) * value_ref[...].astype(jnp.float32)
        ).astype(jnp.bfloat16)

    with jax.named_scope("await_greet"):
        pl.semaphore_wait(barrier, PEERS + Y * CORE - 2)

    def send_filter(chunk):
        @pl.loop(1, OWNERS)
        def _(step):
            other, device = owners(step)
            pltpu.make_async_remote_copy(
                src_ref=filter_turned.at[other, chunk],
                dst_ref=filter_mid.at[chunk, :, owner],
                send_sem=filter_send,
                recv_sem=filter_recv.at[chunk],
                device_id=device,
                device_id_type=MESH,
            ).start()

        pltpu.make_async_copy(
            filter_turned.at[owner, chunk], filter_mid.at[chunk, :, owner], filter_recv.at[chunk]
        ).start()

    with jax.named_scope("send_filter"):
        send_filter(0)

    def columns(low, other_y, other_core, first, size):
        start = half(low, other_y, other_core) * CHUNKS * SIDE + first
        return pl.ds(pl.multiple_of(start, SIDE), size)

    def line_of(other_y, other_core):
        return pl.ds(pl.multiple_of((other_core * Y + other_y) * count, count), count)

    with jax.named_scope("send_rows"):
        for chunk in range(CHUNKS):

            @pl.loop(1, Y * CORE)
            def _(step):
                other_y, other_core, device = aside(step)
                for low in range(Z_LO):
                    pltpu.make_async_remote_copy(
                        src_ref=gated.at[:, columns(low, other_y, other_core, chunk * SIDE, SIDE)],
                        dst_ref=slab.at[chunk, low, line_of(y, core), :],
                        send_sem=row_send,
                        recv_sem=row_recv.at[chunk],
                        device_id=device,
                        device_id_type=MESH,
                    ).start()

            for low in range(Z_LO):
                pltpu.make_async_copy(
                    gated.at[:, columns(low, y, core, chunk * SIDE, SIDE)],
                    slab.at[chunk, low, line_of(y, core), :],
                    row_recv.at[chunk],
                ).start()

    with jax.named_scope("send_filter1"):
        send_filter(1)

    with jax.named_scope("split_tables"):
        loads[3].wait()
        for target, start in ((signal_coarse, 0), (filter_coarse, SIDE)):
            high, low = halves(stacked[:256, start : start + SIDE])
            target[:, :SIDE], target[:, SIDE:] = high, low
        for target, start in ((into, 256), (back, 768)):
            target[0], target[1] = halves(stacked[start : start + target.shape[1]])
        outof[...] = stacked[512:768].astype(jnp.bfloat16)

    def send_signal(source, target, which):
        @pl.loop(1, PEERS)
        def _(step):
            _, owner_there, low, device = across(step)
            pltpu.make_async_remote_copy(
                src_ref=source.at[low * OWNERS + owner_there],
                dst_ref=target.at[me],
                send_sem=signal_send,
                recv_sem=signal_recv.at[which],
                device_id=device,
                device_id_type=MESH,
            ).start()

        pltpu.make_async_copy(
            source.at[z_lo * OWNERS + owner], target.at[me], signal_recv.at[which]
        ).start()

    def send_signals(chunk, groups):
        pltpu.make_async_copy(slab.at[chunk], slab.at[chunk], row_recv.at[chunk]).wait()
        for group in groups:
            for low in range(Z_LO):
                here = slice(low * OWNERS, (low + 1) * OWNERS)
                part_turned[group, here] = turned_group(slab[chunk, low], group)
            send_signal(part_turned.at[group], part_in.at[group], group)

    with jax.named_scope("send_signal"):
        send_signals(0, ORDER[:2])
        send_signals(1, ORDER[2:])

    turn = stacked.at[896:1024]

    def transform(parts, table, passes):
        parts = jnp.concatenate(parts, axis=1).astype(jnp.bfloat16)
        part = dot(table[...], jnp.concatenate([parts, parts], axis=0))
        cos, sin = turn[:, :SIDE], turn[:, SIDE:]
        turned = []
        for u in range(GROUP):
            real = part[:SIDE, u * SIDE : (u + 1) * SIDE]
            imag = part[SIDE:, u * SIDE : (u + 1) * SIDE]
            turned.append(
                jnp.concatenate([real * cos + imag * sin, imag * cos - real * sin], axis=1)
            )
        turned = jnp.concatenate(turned, axis=0).astype(jnp.bfloat16)
        return sum(dot(turned, into[k]) for k in range(passes))

    def widen(source, target):
        target[...] = source[...].astype(jnp.float32).reshape(target.shape)

    def take_filter(chunk):
        pltpu.make_async_copy(
            filter_mid.at[chunk], filter_mid.at[chunk], filter_recv.at[chunk]
        ).wait()
        swap = pltpu.make_async_remote_copy(
            src_ref=filter_mid.at[chunk, 1 - core],
            dst_ref=filter_in.at[chunk, :, core],
            send_sem=swap_send,
            recv_sem=swap_recv.at[0, chunk],
            device_id=(owner * CORE + 1 - core, ch),
            device_id_type=MESH,
        )
        swap.start()
        keep = pltpu.make_async_copy(
            filter_mid.at[chunk, core], filter_in.at[chunk, :, core], swap_recv.at[1, chunk]
        )
        keep.start()
        keep.wait()
        swap.wait()

    def transform_filter(chunk):
        widen(filter_in.at[chunk], filter_wide)
        for group in range(OCTET // GROUP):
            parts = [
                filter_wide[pl.ds(group * GROUP + u, SIDE, stride=OCTET), :] for u in range(GROUP)
            ]
            spectrum[chunk, group] = transform(parts, filter_coarse, 2)

    with jax.named_scope("take_filter0"):
        take_filter(0)
        transform_filter(0)

    left = lax.broadcasted_iota(jnp.int32, (PEERS, SIDE), 1) < SIDE // 2

    def convolve(chunk, group):
        parts = [
            jnp.concatenate(
                [
                    small[pl.ds(tile * GROUP + u, PEERS, stride=4 * GROUP), :]
                    for tile in range(4)
                ],
                axis=0,
            )
            for u in range(GROUP)
        ]
        wave = transform(parts, signal_coarse, 1)
        held = spectrum[chunk, group]
        wave_real, wave_imag = wave[:, :SIDE], wave[:, SIDE:]
        held_real, held_imag = held[:, :SIDE], held[:, SIDE:]
        product = jnp.concatenate(
            [
                wave_real * held_real - wave_imag * held_imag,
                wave_real * held_imag + wave_imag * held_real,
            ],
            axis=1,
        ).astype(jnp.bfloat16)
        part = dot(product, outof[...])
        cos, sin = turn[:, :SIDE], turn[:, SIDE:]
        spun = []
        for u in range(GROUP):
            real = part[u * SIDE : (u + 1) * SIDE, :SIDE]
            imag = part[u * SIDE : (u + 1) * SIDE, SIDE:]
            spun.append(jnp.concatenate([real * cos - imag * sin, imag * cos + real * sin], axis=0))
        spun = jnp.concatenate(spun, axis=1).astype(jnp.bfloat16)
        result = dot(back[0], spun)
        block = (core * CHUNKS + chunk) * SIDE
        if chunk == 0 or group == 0:
            places = [block + 64 * group + owner * GROUP + u for u in range(GROUP)]
        else:
            places = [block + 64 + 32 * (u // 2) + 2 * owner + u % 2 for u in range(GROUP)]
        return [
            result[:, u * SIDE : (u + 1) * SIDE] + gain_ref[places[u]] * parts[u]
            for u in range(GROUP)
        ]

    def spread(sums):
        for w in range(2):
            for tile in range(4):
                first, second = (p[tile * PEERS : (tile + 1) * PEERS] for p in (sums[w], sums[2 + w]))
                mixed[2 * tile, pl.ds(w, PEERS, stride=2), :] = jnp.where(
                    left, first, pltpu.roll(second, SIDE // 2, 1)
                )
                mixed[2 * tile + 1, pl.ds(w, PEERS, stride=2), :] = jnp.where(
                    left, pltpu.roll(first, SIDE // 2, 1), second
                )

    def send_back(source, target, which):
        @pl.loop(1, PEERS)
        def _(step):
            other, _, _, device = across(step)
            pltpu.make_async_remote_copy(
                src_ref=source.at[other],
                dst_ref=target.at[z_lo * OWNERS + owner],
                send_sem=back_send,
                recv_sem=back_recv.at[which],
                device_id=device,
                device_id_type=MESH,
            ).start()

        pltpu.make_async_copy(
            source.at[me], target.at[z_lo * OWNERS + owner], back_recv.at[which]
        ).start()

    def send_aside(source, target, send_sem, recv_sem):
        @pl.loop(1, Y * CORE)
        def _(step):
            other_y, other_core, device = aside(step)
            pltpu.make_async_remote_copy(
                src_ref=source.at[other_core * Y + other_y],
                dst_ref=target.at[y * CORE + core],
                send_sem=send_sem,
                recv_sem=recv_sem,
                device_id=device,
                device_id_type=MESH,
            ).start()

        pltpu.make_async_copy(source.at[core * Y + y], target.at[y * CORE + core], recv_sem).start()

    def arrived(ref, semaphore):
        pltpu.make_async_copy(ref, ref, semaphore).wait()

    def await_signal(group):
        arrived(part_in.at[group], signal_recv.at[group])
        widen(part_in.at[group], small)

    def send_direct(which):
        await_signal(which)
        sums = convolve(which // 2, which % 2)
        for u in range(GROUP):
            for tile in range(4):
                small[pl.ds(tile * GROUP + u, PEERS, stride=4 * GROUP), :] = sums[u][
                    tile * PEERS : (tile + 1) * PEERS
                ]
        sent[which] = small[...].astype(jnp.bfloat16).reshape(sent.shape[1:])
        send_back(sent.at[which], returned.at[which], which)

    def send_first():
        await_signal(3)
        spread(convolve(1, 1))
        aside_send[...] = mixed[...].astype(jnp.bfloat16)
        send_aside(aside_send, aside_in, mixed_send, mixed_recv)

    for group in ORDER:
        if group == ORDER[2]:
            with jax.named_scope("take_filter1"):
                take_filter(1)
                transform_filter(1)

        with jax.named_scope(f"convolve{group}"):
            if group < 3:
                send_direct(group)
            else:
                send_first()

    with jax.named_scope("relay"):
        arrived(aside_in, mixed_recv)
        widen(aside_in, small)
        for peer in range(PEERS):
            lines = [small[pl.ds(peer * 2 + w, OCTET, stride=64), :] for w in range(2)]
            sent[3, peer] = jnp.concatenate(lines, axis=0).astype(jnp.bfloat16)
        send_back(sent.at[3], returned.at[3], 3)

    def send_tile(tile):
        for upper in range(2):
            other_core, other_y = tile // 2, 2 * (tile % 2) + upper
            mine = jnp.logical_and(core == other_core, y == other_y)
            source = rows.at[2, 2 * tile + upper]
            target = landed.at[2, y * CORE + core]

            @pl.when(mine)
            def _():
                pltpu.make_async_copy(source, target, out_recv.at[2]).start()

            @pl.when(jnp.logical_not(mine))
            def _():
                pltpu.make_async_remote_copy(
                    src_ref=source,
                    dst_ref=target,
                    send_sem=out_send,
                    recv_sem=out_recv.at[2],
                    device_id=(owner * CORE + other_core, z_lo * Y + other_y),
                    device_id_type=MESH,
                ).start()

    for which in range(3):
        with jax.named_scope(f"send_out{which}"):
            arrived(returned.at[which], back_recv.at[which])
            widen(returned.at[which], small)
            blocks = small[...].reshape(PEERS, 4, GROUP, SIDE)
            for tile in range(4):
                part = blocks[:, tile].reshape(SIDE, SIDE)
                rows[which, 2 * tile : 2 * tile + 2] = part.T.astype(jnp.bfloat16).reshape(
                    2, count, SIDE
                )
                if which == 2:
                    send_tile(tile)
            if which < 2:
                send_aside(rows.at[which], landed.at[which], out_send, out_recv.at[which])

    def put(low, other, chunk, block):
        start = ((low * Y * CORE + other) * CHUNKS + chunk) * SIDE
        out_ref[:, start : start + SIDE] = block

    quarter = lax.broadcasted_iota(jnp.int32, (count, SIDE), 1) // 32
    with jax.named_scope("finish0"):
        arrived(landed.at[0], out_recv.at[0])
        arrived(landed.at[1], out_recv.at[1])
        for other in range(Y * CORE):
            first, second = (landed[group, other].astype(jnp.float32) for group in range(2))
            for low in range(Z_LO):
                whole = jnp.where(
                    quarter < 2,
                    pltpu.roll(first, SIDE // 2, 1) if low else first,
                    second if low else pltpu.roll(second, SIDE // 2, 1),
                )
                put(low, other, 0, whole.astype(jnp.bfloat16))

    with jax.named_scope("finish1"):
        arrived(returned.at[3], back_recv.at[3])
        widen(returned.at[3], small)
        lasts = {}
        for low in range(Z_LO):
            for four in range(2):
                lines = [
                    small[pl.ds(low * 256 + four * 4 + k, PEERS, stride=OCTET), :] for k in range(4)
                ]
                block = jnp.concatenate(lines, axis=0).T
                upper, lower = block[:count], block[count:]
                for k in range(4):
                    lasts[low, four * 4 + k] = jnp.where(
                        quarter == 2,
                        upper if k == 2 else pltpu.roll(upper, (64 - 32 * k) % SIDE, 1),
                        lower if k == 3 else pltpu.roll(lower, (96 - 32 * k) % SIDE, 1),
                    )
        arrived(landed.at[2], out_recv.at[2])
        for other in range(Y * CORE):
            first = landed[2, other].astype(jnp.float32)
            for low in range(Z_LO):
                whole = jnp.where(
                    quarter < 2,
                    pltpu.roll(first, SIDE // 2, 1) if low else first,
                    lasts[low, other],
                )
                put(low, other, 1, whole.astype(jnp.bfloat16))

    def settle(part, semaphore):
        pltpu.make_async_copy(part, part, semaphore).wait()

    with jax.named_scope("settle"):
        for chunk in range(CHUNKS):
            settle(slab.at[chunk, :, pl.ds(0, (Y * CORE - 1) * count)], row_send)
        settle(filter_turned.at[pl.ds(0, OWNERS - 1)], filter_send)
        for which in range(4):
            settle(part_turned.at[which, pl.ds(0, PEERS - 1)], signal_send)
            settle(sent.at[which, pl.ds(0, PEERS - 1)], back_send)
        settle(aside_send.at[pl.ds(0, Y * CORE - 1)], mixed_send)
        for which in range(3):
            settle(rows.at[which, pl.ds(0, Y * CORE - 1)], out_send)


def shards(query_input, key_input, value_input, filters, direct_gain):
    count, channels = key_input.shape
    table = jnp.asarray(tables())
    stays = pl.BlockSpec(memory_space=pltpu.HBM)
    half, single = jnp.bfloat16, jnp.float32
    span = Y * CORE * count
    octets = (SIDE * OCTET, SIDE)
    dma = pltpu.SemaphoreType.DMA
    mixed = pl.pallas_call(
        kernel,
        out_shape=jax.ShapeDtypeStruct((count, channels), half),
        in_specs=[stays] * 3 + [pl.BlockSpec(memory_space=pltpu.SMEM), stays],
        out_specs=pl.BlockSpec(memory_space=pltpu.VMEM),
        scratch_shapes=[
            pltpu.VMEM((count, channels), half),
            pltpu.VMEM((count, channels), half),
            pltpu.VMEM(filters.shape, half),
            pltpu.VMEM(table.shape, single),
            pltpu.VMEM((2 * SIDE, 2 * SIDE), half),
            pltpu.VMEM((2 * SIDE, 2 * SIDE), half),
            pltpu.VMEM((2, 2 * SIDE, 2 * SIDE), half),
            pltpu.VMEM((2 * SIDE, 2 * SIDE), half),
            pltpu.VMEM((2, SIDE, 2 * SIDE), half),
            pltpu.VMEM((count, channels), half),
            pltpu.VMEM((CHUNKS, Z_LO, span, SIDE), half),
            pltpu.VMEM((4, PEERS, 4 * GROUP, SIDE), half),
            pltpu.VMEM((4, PEERS, 4 * GROUP, SIDE), half),
            pltpu.VMEM((OWNERS, CHUNKS, CORE, 4 * OCTET, SIDE), half),
            pltpu.VMEM((CHUNKS, CORE, OWNERS, 4 * OCTET, SIDE), half),
            pltpu.VMEM((CHUNKS, OWNERS, CORE, 4 * OCTET, SIDE), half),
            pltpu.VMEM(octets, single),
            pltpu.VMEM((CHUNKS, OCTET // GROUP, GROUP * SIDE, 2 * SIDE), single),
            pltpu.VMEM((Y * CORE, 2 * PEERS, SIDE), single),
            pltpu.VMEM((Y * CORE, 2 * PEERS, SIDE), half),
            pltpu.VMEM((Y * CORE, 2 * PEERS, SIDE), half),
            pltpu.VMEM((SIDE * GROUP, SIDE), single),
            pltpu.VMEM((4, PEERS, 4 * GROUP, SIDE), half),
            pltpu.VMEM((4, PEERS, 4 * GROUP, SIDE), half),
            pltpu.VMEM((3, Y * CORE, count, SIDE), half),
            pltpu.VMEM((3, Y * CORE, count, SIDE), half),
            dma((4,)),
            dma(()),
            dma((CHUNKS,)),
            dma(()),
            dma((CHUNKS,)),
            dma(()),
            dma((2, CHUNKS)),
            dma(()),
            dma((4,)),
            dma(()),
            dma((4,)),
            dma(()),
            dma(()),
            dma(()),
            dma((3,)),
        ],
        compiler_params=pltpu.CompilerParams(
            collective_id=0, has_side_effects=True, vmem_limit_bytes=56000000
        ),
    )(key_input, value_input, filters, pltpu.with_memory_space_constraint(direct_gain, pltpu.HBM), table)
    return (query_input.astype(jnp.float32) * mixed.astype(jnp.float32)).astype(jnp.bfloat16)


def solution(mesh):
    return jax.shard_map(
        shards,
        mesh=mesh,
        in_specs=(
            P(("ctx", "ch"), None),
            P(("ctx", "ch"), None),
            P(("ctx", "ch"), None),
            P("ctx", "ch"),
            P("ch"),
        ),
        out_specs=P(("ctx", "ch"), None),
        check_vma=False,
    )
```

```python
import functools

import jax
import jax.numpy as jnp
import numpy as np
from jax import lax
from jax.experimental import pallas as pl
from jax.experimental.pallas import tpu as pltpu
from jax.sharding import PartitionSpec as P

MESH = pl.DeviceIdType.MESH
SIDE = 128
OCTET = 8
GROUP = 4
X, Z_HI, CORE = 4, 4, 2
Z_LO, Y = 2, 4
OWNERS = X * Z_HI
PEERS = OWNERS * Z_LO
CHUNKS = 2
ORDER = 0, 1, 3, 2


def tables():
    length = SIDE * SIDE
    side = np.arange(SIDE)
    offset = side + 0.25
    coarse = 2 * np.pi * np.outer(offset, side) / SIDE
    turn = 2 * np.pi * np.outer(offset, side) / length
    fine = 2 * np.pi * np.outer(side, side) / SIDE
    arrival = side.reshape(OWNERS, CORE, Z_LO, 2).transpose(1, 3, 0, 2).reshape(-1)

    def forward(angle):
        return np.concatenate([np.cos(angle), -np.sin(angle)], axis=0)

    angle = coarse[:, arrival].T
    back = np.concatenate([np.cos(angle), -np.sin(angle)], axis=1) / length
    cos, sin = np.cos(fine), np.sin(fine)
    into = np.block([[cos, -sin], [sin, cos]])
    outof = np.block([[cos, sin], [-sin, cos]])
    stacked = [
        np.concatenate([forward(coarse[:, arrival]), forward(coarse)], axis=1),
        into,
        outof,
        back,
        np.concatenate([np.cos(turn), np.sin(turn)], axis=1),
    ]
    return np.concatenate(stacked, axis=0).astype(np.float32)


def halves(table):
    high = table.astype(jnp.bfloat16)
    return high, (table - high.astype(jnp.float32)).astype(jnp.bfloat16)


def dot(left, right):
    return jnp.dot(left, right, preferred_element_type=jnp.float32)


def kernel(
    key_hbm,
    value_hbm,
    filter_hbm,
    gain_ref,
    tables_hbm,
    out_ref,
    key_ref,
    value_ref,
    filter_ref,
    stacked,
    signal_coarse,
    filter_coarse,
    into,
    outof,
    back,
    gated,
    slab,
    part_turned,
    part_in,
    filter_turned,
    filter_mid,
    filter_in,
    filter_wide,
    spectrum,
    mixed,
    aside_send,
    aside_in,
    small,
    sent,
    returned,
    rows,
    landed,
    load_sems,
    row_send,
    row_recv,
    filter_send,
    filter_recv,
    swap_send,
    swap_recv,
    signal_send,
    signal_recv,
    back_send,
    back_recv,
    mixed_send,
    mixed_recv,
    out_send,
    out_recv,
):
    count = gated.shape[0]
    ctx = lax.axis_index("ctx")
    ch = lax.axis_index("ch")
    x, z_hi, core = ctx // (Z_HI * CORE), lax.rem(ctx // CORE, Z_HI), lax.rem(ctx, CORE)
    z_lo, y = ch // Y, lax.rem(ch, Y)
    owner = x * Z_HI + z_hi
    me = owner * Z_LO + z_lo
    half = lambda low, other_y, other_core: (low * Y + other_y) * CORE + other_core

    loads = [
        pltpu.make_async_copy(source, target, load_sems.at[n])
        for n, (source, target) in enumerate(
            [
                (filter_hbm, filter_ref),
                (key_hbm, key_ref),
                (value_hbm, value_ref),
                (tables_hbm, stacked),
            ]
        )
    ]
    for load_copy in loads:
        load_copy.start()

    def across(step):
        other = lax.rem(me + step + core * (PEERS - 2 * step), PEERS)
        owner_there, low = other // Z_LO, lax.rem(other, Z_LO)
        return other, owner_there, low, (owner_there * CORE + core, low * Y + y)

    def owners(step):
        other = lax.rem(owner + step + core * (OWNERS - 2 * step), OWNERS)
        return other, (other * CORE + core, ch)

    def aside(step):
        other = lax.rem(y * CORE + core + step, Y * CORE)
        other_y, other_core = other // CORE, lax.rem(other, CORE)
        return other_y, other_core, (owner * CORE + other_core, z_lo * Y + other_y)

    barrier = pltpu.get_barrier_semaphore()

    with jax.named_scope("greet"):

        @pl.loop(1, PEERS)
        def _(step):
            pl.semaphore_signal(barrier, inc=1, device_id=across(step)[-1], device_id_type=MESH)

        @pl.loop(1, Y * CORE)
        def _(step):
            pl.semaphore_signal(barrier, inc=1, device_id=aside(step)[-1], device_id_type=MESH)

    line = lax.broadcasted_iota(jnp.int32, (SIDE, SIDE), 0)
    lane = lax.broadcasted_iota(jnp.int32, (SIDE, SIDE), 1)
    group_of = (line >> 2) & 1
    direct = 64 * group_of + 4 * (line >> 3) + (line & 3)
    place = jnp.where(
        group_of == 1, 64 + 32 * ((line >> 1) & 1) + 2 * (line >> 3) + (line & 1), direct
    )
    picks = [jnp.where(lane == p, 1.0, 0.0).astype(jnp.bfloat16) for p in (direct, place)]

    pairs = []
    for group in range(4):
        channel = line & 3
        if group == 3:
            place = 64 + 32 * (channel >> 1) + 2 * (line >> 3) + (channel & 1)
        else:
            place = 64 * (group % 2) + 4 * (line >> 3) + channel
        pairs.append(
            jnp.concatenate(
                [
                    jnp.where((lane == place) & (group_of == tile), 1.0, 0.0).astype(jnp.bfloat16)
                    for tile in range(2)
                ],
                axis=1,
            )
        )

    def turned_group(source, group):
        parts = []
        for pair in range(2):
            tiles = [source[(2 * pair + t) * SIDE : (2 * pair + t + 1) * SIDE] for t in range(2)]
            block = lax.dot_general(
                pairs[group],
                jnp.concatenate(tiles, axis=1),
                (((1,), (1,)), ((), ())),
                preferred_element_type=jnp.float32,
            )
            parts.append(block.reshape(OWNERS, OCTET, SIDE))
        return jnp.concatenate(parts, axis=1).astype(jnp.bfloat16)

    def turned(source, column):
        block = lax.dot_general(
            picks[column % CHUNKS],
            source[:, column * SIDE : (column + 1) * SIDE],
            (((1,), (1,)), ((), ())),
            preferred_element_type=jnp.float32,
        )
        tiles = [block[:, t * SIDE : (t + 1) * SIDE].reshape(OWNERS, OCTET, SIDE) for t in range(4)]
        return jnp.concatenate(tiles, axis=1).astype(jnp.bfloat16)

    with jax.named_scope("turn_filter"):
        loads[0].wait()
        for there in range(CORE):
            for chunk in range(CHUNKS):
                filter_turned[:, chunk, there] = turned(filter_ref, there * CHUNKS + chunk)

    with jax.named_scope("gate"):
        loads[1].wait()
        loads[2].wait()
        gated[...] = (
            key_ref[...].astype(jnp.float32) * value_ref[...].astype(jnp.float32)
        ).astype(jnp.bfloat16)

    with jax.named_scope("await_greet"):
        pl.semaphore_wait(barrier, PEERS + Y * CORE - 2)

    def send_filter(chunk):
        @pl.loop(1, OWNERS)
        def _(step):
            other, device = owners(step)
            pltpu.make_async_remote_copy(
                src_ref=filter_turned.at[other, chunk],
                dst_ref=filter_mid.at[chunk, :, owner],
                send_sem=filter_send,
                recv_sem=filter_recv.at[chunk],
                device_id=device,
                device_id_type=MESH,
            ).start()

        pltpu.make_async_copy(
            filter_turned.at[owner, chunk], filter_mid.at[chunk, :, owner], filter_recv.at[chunk]
        ).start()

    with jax.named_scope("send_filter"):
        send_filter(0)

    def columns(low, other_y, other_core, first, size):
        start = half(low, other_y, other_core) * CHUNKS * SIDE + first
        return pl.ds(pl.multiple_of(start, SIDE), size)

    def line_of(other_y, other_core):
        return pl.ds(pl.multiple_of((other_core * Y + other_y) * count, count), count)

    with jax.named_scope("send_rows"):
        for chunk in range(CHUNKS):

            @pl.loop(1, Y * CORE)
            def _(step):
                other_y, other_core, device = aside(step)
                for low in range(Z_LO):
                    pltpu.make_async_remote_copy(
                        src_ref=gated.at[:, columns(low, other_y, other_core, chunk * SIDE, SIDE)],
                        dst_ref=slab.at[chunk, low, line_of(y, core), :],
                        send_sem=row_send,
                        recv_sem=row_recv.at[chunk],
                        device_id=device,
                        device_id_type=MESH,
                    ).start()

            for low in range(Z_LO):
                pltpu.make_async_copy(
                    gated.at[:, columns(low, y, core, chunk * SIDE, SIDE)],
                    slab.at[chunk, low, line_of(y, core), :],
                    row_recv.at[chunk],
                ).start()

    with jax.named_scope("send_filter1"):
        send_filter(1)

    with jax.named_scope("split_tables"):
        loads[3].wait()
        for target, start in ((signal_coarse, 0), (filter_coarse, SIDE)):
            high, low = halves(stacked[:256, start : start + SIDE])
            target[:, :SIDE], target[:, SIDE:] = high, low
        for target, start in ((into, 256), (back, 768)):
            target[0], target[1] = halves(stacked[start : start + target.shape[1]])
        outof[...] = stacked[512:768].astype(jnp.bfloat16)

    def send_signal(source, target, which):
        @pl.loop(1, PEERS)
        def _(step):
            _, owner_there, low, device = across(step)
            pltpu.make_async_remote_copy(
                src_ref=source.at[low * OWNERS + owner_there],
                dst_ref=target.at[me],
                send_sem=signal_send,
                recv_sem=signal_recv.at[which],
                device_id=device,
                device_id_type=MESH,
            ).start()

        pltpu.make_async_copy(
            source.at[z_lo * OWNERS + owner], target.at[me], signal_recv.at[which]
        ).start()

    def send_signals(chunk, groups):
        pltpu.make_async_copy(slab.at[chunk], slab.at[chunk], row_recv.at[chunk]).wait()
        for group in groups:
            for low in range(Z_LO):
                here = slice(low * OWNERS, (low + 1) * OWNERS)
                part_turned[group, here] = turned_group(slab[chunk, low], group)
            send_signal(part_turned.at[group], part_in.at[group], group)

    with jax.named_scope("send_signal"):
        send_signals(0, ORDER[:2])
        send_signals(1, ORDER[2:])

    turn = stacked.at[896:1024]

    def transform(parts, table, passes):
        parts = jnp.concatenate(parts, axis=1).astype(jnp.bfloat16)
        part = dot(table[...], jnp.concatenate([parts, parts], axis=0))
        cos, sin = turn[:, :SIDE], turn[:, SIDE:]
        turned = []
        for u in range(GROUP):
            real = part[:SIDE, u * SIDE : (u + 1) * SIDE]
            imag = part[SIDE:, u * SIDE : (u + 1) * SIDE]
            turned.append(
                jnp.concatenate([real * cos + imag * sin, imag * cos - real * sin], axis=1)
            )
        turned = jnp.concatenate(turned, axis=0).astype(jnp.bfloat16)
        return sum(dot(turned, into[k]) for k in range(passes))

    def widen(source, target):
        target[...] = source[...].astype(jnp.float32).reshape(target.shape)

    def take_filter(chunk):
        pltpu.make_async_copy(
            filter_mid.at[chunk], filter_mid.at[chunk], filter_recv.at[chunk]
        ).wait()
        swap = pltpu.make_async_remote_copy(
            src_ref=filter_mid.at[chunk, 1 - core],
            dst_ref=filter_in.at[chunk, :, core],
            send_sem=swap_send,
            recv_sem=swap_recv.at[0, chunk],
            device_id=(owner * CORE + 1 - core, ch),
            device_id_type=MESH,
        )
        swap.start()
        keep = pltpu.make_async_copy(
            filter_mid.at[chunk, core], filter_in.at[chunk, :, core], swap_recv.at[1, chunk]
        )
        keep.start()
        keep.wait()
        swap.wait()

    def transform_filter(chunk):
        widen(filter_in.at[chunk], filter_wide)
        for group in range(OCTET // GROUP):
            parts = [
                filter_wide[pl.ds(group * GROUP + u, SIDE, stride=OCTET), :] for u in range(GROUP)
            ]
            spectrum[chunk, group] = transform(parts, filter_coarse, 2)

    with jax.named_scope("take_filter0"):
        take_filter(0)
        transform_filter(0)

    left = lax.broadcasted_iota(jnp.int32, (PEERS, SIDE), 1) < SIDE // 2

    def convolve(chunk, group):
        parts = [
            jnp.concatenate(
                [
                    small[pl.ds(tile * GROUP + u, PEERS, stride=4 * GROUP), :]
                    for tile in range(4)
                ],
                axis=0,
            )
            for u in range(GROUP)
        ]
        wave = transform(parts, signal_coarse, 1)
        held = spectrum[chunk, group]
        wave_real, wave_imag = wave[:, :SIDE], wave[:, SIDE:]
        held_real, held_imag = held[:, :SIDE], held[:, SIDE:]
        product = jnp.concatenate(
            [
                wave_real * held_real - wave_imag * held_imag,
                wave_real * held_imag + wave_imag * held_real,
            ],
            axis=1,
        ).astype(jnp.bfloat16)
        part = dot(product, outof[...])
        cos, sin = turn[:, :SIDE], turn[:, SIDE:]
        spun = []
        for u in range(GROUP):
            real = part[u * SIDE : (u + 1) * SIDE, :SIDE]
            imag = part[u * SIDE : (u + 1) * SIDE, SIDE:]
            spun.append(jnp.concatenate([real * cos - imag * sin, imag * cos + real * sin], axis=0))
        spun = jnp.concatenate(spun, axis=1).astype(jnp.bfloat16)
        result = dot(back[0], spun)
        block = (core * CHUNKS + chunk) * SIDE
        if chunk == 0 or group == 0:
            places = [block + 64 * group + owner * GROUP + u for u in range(GROUP)]
        else:
            places = [block + 64 + 32 * (u // 2) + 2 * owner + u % 2 for u in range(GROUP)]
        return [
            result[:, u * SIDE : (u + 1) * SIDE] + gain_ref[places[u]] * parts[u]
            for u in range(GROUP)
        ]

    def spread(sums):
        for w in range(2):
            for tile in range(4):
                first, second = (p[tile * PEERS : (tile + 1) * PEERS] for p in (sums[w], sums[2 + w]))
                mixed[2 * tile, pl.ds(w, PEERS, stride=2), :] = jnp.where(
                    left, first, pltpu.roll(second, SIDE // 2, 1)
                )
                mixed[2 * tile + 1, pl.ds(w, PEERS, stride=2), :] = jnp.where(
                    left, pltpu.roll(first, SIDE // 2, 1), second
                )

    def send_back(source, target, which):
        @pl.loop(1, PEERS)
        def _(step):
            other, _, _, device = across(step)
            pltpu.make_async_remote_copy(
                src_ref=source.at[other],
                dst_ref=target.at[z_lo * OWNERS + owner],
                send_sem=back_send,
                recv_sem=back_recv.at[which],
                device_id=device,
                device_id_type=MESH,
            ).start()

        pltpu.make_async_copy(
            source.at[me], target.at[z_lo * OWNERS + owner], back_recv.at[which]
        ).start()

    def send_aside(source, target, send_sem, recv_sem):
        @pl.loop(1, Y * CORE)
        def _(step):
            other_y, other_core, device = aside(step)
            pltpu.make_async_remote_copy(
                src_ref=source.at[other_core * Y + other_y],
                dst_ref=target.at[y * CORE + core],
                send_sem=send_sem,
                recv_sem=recv_sem,
                device_id=device,
                device_id_type=MESH,
            ).start()

        pltpu.make_async_copy(source.at[core * Y + y], target.at[y * CORE + core], recv_sem).start()

    def arrived(ref, semaphore):
        pltpu.make_async_copy(ref, ref, semaphore).wait()

    def await_signal(group):
        arrived(part_in.at[group], signal_recv.at[group])
        widen(part_in.at[group], small)

    def send_direct(which):
        await_signal(which)
        sums = convolve(which // 2, which % 2)
        for u in range(GROUP):
            for tile in range(4):
                small[pl.ds(tile * GROUP + u, PEERS, stride=4 * GROUP), :] = sums[u][
                    tile * PEERS : (tile + 1) * PEERS
                ]
        sent[which] = small[...].astype(jnp.bfloat16).reshape(sent.shape[1:])
        send_back(sent.at[which], returned.at[which], which)

    def send_first():
        await_signal(3)
        spread(convolve(1, 1))
        aside_send[...] = mixed[...].astype(jnp.bfloat16)
        send_aside(aside_send, aside_in, mixed_send, mixed_recv)

    for group in ORDER:
        if group == ORDER[2]:
            with jax.named_scope("take_filter1"):
                take_filter(1)
                transform_filter(1)

        with jax.named_scope(f"convolve{group}"):
            if group < 3:
                send_direct(group)
            else:
                send_first()

    with jax.named_scope("relay"):
        arrived(aside_in, mixed_recv)
        widen(aside_in, small)
        for peer in range(PEERS):
            lines = [small[pl.ds(peer * 2 + w, OCTET, stride=64), :] for w in range(2)]
            sent[3, peer] = jnp.concatenate(lines, axis=0).astype(jnp.bfloat16)
        send_back(sent.at[3], returned.at[3], 3)

    def send_tile(tile):
        for turn_of in range(2):
            upper = lax.rem(core + turn_of, 2)
            other_core, other_y = tile // 2, 2 * (tile % 2) + upper
            mine = jnp.logical_and(core == other_core, y == other_y)
            source = rows.at[2, 2 * tile + upper]
            target = landed.at[2, y * CORE + core]

            @pl.when(mine)
            def _():
                pltpu.make_async_copy(source, target, out_recv.at[2]).start()

            @pl.when(jnp.logical_not(mine))
            def _():
                pltpu.make_async_remote_copy(
                    src_ref=source,
                    dst_ref=target,
                    send_sem=out_send,
                    recv_sem=out_recv.at[2],
                    device_id=(owner * CORE + other_core, z_lo * Y + other_y),
                    device_id_type=MESH,
                ).start()

    for which in range(3):
        with jax.named_scope(f"send_out{which}"):
            arrived(returned.at[which], back_recv.at[which])
            widen(returned.at[which], small)
            blocks = small[...].reshape(PEERS, 4, GROUP, SIDE)
            for tile in range(4):
                part = blocks[:, tile].reshape(SIDE, SIDE)
                rows[which, 2 * tile : 2 * tile + 2] = part.T.astype(jnp.bfloat16).reshape(
                    2, count, SIDE
                )
                if which == 2:
                    send_tile(tile)
            if which < 2:
                send_aside(rows.at[which], landed.at[which], out_send, out_recv.at[which])

    def put(low, other, chunk, block):
        start = ((low * Y * CORE + other) * CHUNKS + chunk) * SIDE
        out_ref[:, start : start + SIDE] = block

    quarter = lax.broadcasted_iota(jnp.int32, (count, SIDE), 1) // 32
    with jax.named_scope("finish0"):
        arrived(landed.at[0], out_recv.at[0])
        arrived(landed.at[1], out_recv.at[1])
        for other in range(Y * CORE):
            first, second = (landed[group, other].astype(jnp.float32) for group in range(2))
            for low in range(Z_LO):
                whole = jnp.where(
                    quarter < 2,
                    pltpu.roll(first, SIDE // 2, 1) if low else first,
                    second if low else pltpu.roll(second, SIDE // 2, 1),
                )
                put(low, other, 0, whole.astype(jnp.bfloat16))

    with jax.named_scope("finish1"):
        arrived(returned.at[3], back_recv.at[3])
        widen(returned.at[3], small)
        lasts = {}
        for low in range(Z_LO):
            for four in range(2):
                lines = [
                    small[pl.ds(low * 256 + four * 4 + k, PEERS, stride=OCTET), :] for k in range(4)
                ]
                block = jnp.concatenate(lines, axis=0).T
                upper, lower = block[:count], block[count:]
                for k in range(4):
                    lasts[low, four * 4 + k] = jnp.where(
                        quarter == 2,
                        upper if k == 2 else pltpu.roll(upper, (64 - 32 * k) % SIDE, 1),
                        lower if k == 3 else pltpu.roll(lower, (96 - 32 * k) % SIDE, 1),
                    )
        arrived(landed.at[2], out_recv.at[2])
        for other in range(Y * CORE):
            first = landed[2, other].astype(jnp.float32)
            for low in range(Z_LO):
                whole = jnp.where(
                    quarter < 2,
                    pltpu.roll(first, SIDE // 2, 1) if low else first,
                    lasts[low, other],
                )
                put(low, other, 1, whole.astype(jnp.bfloat16))

    def settle(part, semaphore):
        pltpu.make_async_copy(part, part, semaphore).wait()

    with jax.named_scope("settle"):
        for chunk in range(CHUNKS):
            settle(slab.at[chunk, :, pl.ds(0, (Y * CORE - 1) * count)], row_send)
        settle(filter_turned.at[pl.ds(0, OWNERS - 1)], filter_send)
        for which in range(4):
            settle(part_turned.at[which, pl.ds(0, PEERS - 1)], signal_send)
            settle(sent.at[which, pl.ds(0, PEERS - 1)], back_send)
        settle(aside_send.at[pl.ds(0, Y * CORE - 1)], mixed_send)
        for which in range(3):
            settle(rows.at[which, pl.ds(0, Y * CORE - 1)], out_send)


def shards(query_input, key_input, value_input, filters, direct_gain):
    count, channels = key_input.shape
    table = jnp.asarray(tables())
    stays = pl.BlockSpec(memory_space=pltpu.HBM)
    half, single = jnp.bfloat16, jnp.float32
    span = Y * CORE * count
    octets = (SIDE * OCTET, SIDE)
    dma = pltpu.SemaphoreType.DMA
    mixed = pl.pallas_call(
        kernel,
        out_shape=jax.ShapeDtypeStruct((count, channels), half),
        in_specs=[stays] * 3 + [pl.BlockSpec(memory_space=pltpu.SMEM), stays],
        out_specs=pl.BlockSpec(memory_space=pltpu.VMEM),
        scratch_shapes=[
            pltpu.VMEM((count, channels), half),
            pltpu.VMEM((count, channels), half),
            pltpu.VMEM(filters.shape, half),
            pltpu.VMEM(table.shape, single),
            pltpu.VMEM((2 * SIDE, 2 * SIDE), half),
            pltpu.VMEM((2 * SIDE, 2 * SIDE), half),
            pltpu.VMEM((2, 2 * SIDE, 2 * SIDE), half),
            pltpu.VMEM((2 * SIDE, 2 * SIDE), half),
            pltpu.VMEM((2, SIDE, 2 * SIDE), half),
            pltpu.VMEM((count, channels), half),
            pltpu.VMEM((CHUNKS, Z_LO, span, SIDE), half),
            pltpu.VMEM((4, PEERS, 4 * GROUP, SIDE), half),
            pltpu.VMEM((4, PEERS, 4 * GROUP, SIDE), half),
            pltpu.VMEM((OWNERS, CHUNKS, CORE, 4 * OCTET, SIDE), half),
            pltpu.VMEM((CHUNKS, CORE, OWNERS, 4 * OCTET, SIDE), half),
            pltpu.VMEM((CHUNKS, OWNERS, CORE, 4 * OCTET, SIDE), half),
            pltpu.VMEM(octets, single),
            pltpu.VMEM((CHUNKS, OCTET // GROUP, GROUP * SIDE, 2 * SIDE), single),
            pltpu.VMEM((Y * CORE, 2 * PEERS, SIDE), single),
            pltpu.VMEM((Y * CORE, 2 * PEERS, SIDE), half),
            pltpu.VMEM((Y * CORE, 2 * PEERS, SIDE), half),
            pltpu.VMEM((SIDE * GROUP, SIDE), single),
            pltpu.VMEM((4, PEERS, 4 * GROUP, SIDE), half),
            pltpu.VMEM((4, PEERS, 4 * GROUP, SIDE), half),
            pltpu.VMEM((3, Y * CORE, count, SIDE), half),
            pltpu.VMEM((3, Y * CORE, count, SIDE), half),
            dma((4,)),
            dma(()),
            dma((CHUNKS,)),
            dma(()),
            dma((CHUNKS,)),
            dma(()),
            dma((2, CHUNKS)),
            dma(()),
            dma((4,)),
            dma(()),
            dma((4,)),
            dma(()),
            dma(()),
            dma(()),
            dma((3,)),
        ],
        compiler_params=pltpu.CompilerParams(
            collective_id=0, has_side_effects=True, vmem_limit_bytes=56000000
        ),
    )(key_input, value_input, filters, pltpu.with_memory_space_constraint(direct_gain, pltpu.HBM), table)
    return (query_input.astype(jnp.float32) * mixed.astype(jnp.float32)).astype(jnp.bfloat16)


def solution(mesh):
    return jax.shard_map(
        shards,
        mesh=mesh,
        in_specs=(
            P(("ctx", "ch"), None),
            P(("ctx", "ch"), None),
            P(("ctx", "ch"), None),
            P("ctx", "ch"),
            P("ch"),
        ),
        out_specs=P(("ctx", "ch"), None),
        check_vma=False,
    )
```
